128 devices in a mesh: gx: 32 (over z, y, core), gy: 4 (over x).
Axes of the slice: x: 4, y: 4, z: 4, core: 2. Of those that a mesh axis runs over, the one named last changes fastest.
Arguments:
- features: bfloat16 [32, 4, 2048, 256], P('gx', 'gy'), may hold values from -6 to 6
- pre_norm: bfloat16 [32, 4, 2048, 256], P('gx', 'gy')
- out_grad: bfloat16 [32, 4, 2048, 256], P('gx', 'gy'), may hold values from -6 to 6
- weight: bfloat16 [27, 256, 256], replicated, may hold values from -0.375 to 0.375
- gamma: float32 [256], replicated, may hold values from 0.1 to 1.9
- beta: float32 [256], replicated, may hold values from -3 to 3
- neighbors: int32 [32, 4, 27, 2048], P('gx', 'gy'), may hold values from 0 to 8384, as said below
- boundary: int32 [32, 4, 704], P('gx', 'gy'), may hold values from 0 to 2048, as said below
- counts: int32 [32, 4], P('gx', 'gy'), may hold values from 1 to 2048, as said below
Outputs:
- in_grad: bfloat16 [32, 4, 2048, 256], P('gx', 'gy')
- weight_grad: float32 [6912, 256], P(('gx', 'gy'))
- gamma_grad: float32 [256], replicated
- beta_grad: float32 [256], replicated
The draws below stay inside these ranges and needn't reach their ends.
Inputs may be any that keep to these rules, and one draw needn't show every extreme that they name: `neighbors`: the map is that of a submanifold convolution on a voxel grid: each device owns an 8 x 16 x 16 block of positions, its live rows are its occupied positions in order, rows at or past its count name no row at any offset, offset 13 names the row itself, and if pair (r, k) on one device names row q then row q's device names r at offset 26 - k. Rows named on other devices lie on that device's faces and are listed in its boundary list. `boundary`: A device's live rows on its x and y faces in increasing order, then 2048 in the unused slots. `counts`: some device holds 2048 live rows.
All inputs are finite; a program needn't handle non-finite values.
Results may differ from the reference program's by a relative error of at most 0.0049.
Values may be sent and summed in bfloat16 or wider, within the bound.
A program may use at most 64 MiB of HBM per device.

```python
import jax
import jax.numpy as jnp
from jax import lax

C = 256
LX = 8
LY = 16
LZ = 16
R = 2048
HB = 704
SLABS = 32
STRIPS = 4


def geometry(key):
    base = jax.random.fold_in(key, 7)
    k_jit, k_full, k_roll = jax.random.split(base, 3)
    ndev = SLABS * STRIPS
    positions = LX * LY * LZ
    slab_ix = jnp.arange(SLABS, dtype=jnp.int32)[:, None]
    level = 250 + 750 * slab_ix * slab_ix // ((SLABS - 1) * (SLABS - 1))
    level = level + jax.random.randint(k_jit, (SLABS, STRIPS), -100, 101)
    level = jnp.clip(level, 150, 1000)
    full = jax.random.randint(k_full, (), 0, ndev)
    dev_ids = jnp.arange(ndev, dtype=jnp.int32).reshape(SLABS, STRIPS)
    level = jnp.where(dev_ids == full, 1000, level)
    rolled = jax.random.randint(k_roll, (SLABS, STRIPS, LX, LY, LZ), 0, 1000)
    active = (rolled < level[:, :, None, None, None]).astype(jnp.int32)
    flat = active.reshape(SLABS, STRIPS, positions)
    rowid = jnp.cumsum(flat, axis=2) - 1
    counts = jnp.sum(flat, axis=2).astype(jnp.int32)
    pos_x = jnp.arange(LX, dtype=jnp.int32)[:, None, None]
    pos_y = jnp.arange(LY, dtype=jnp.int32)[None, :, None]
    edge = (pos_x == 0) | (pos_x == LX - 1) | (pos_y == 0) | (pos_y == LY - 1)
    edge = jnp.broadcast_to(edge, (LX, LY, LZ)).reshape(positions).astype(jnp.int32)
    bflat = flat * edge[None, None, :]
    brank = jnp.cumsum(bflat, axis=2) - 1
    target = jnp.where(bflat == 1, brank, HB)

    def fill_one(where_to, rows_of):
        return jnp.full((HB + 1,), positions, jnp.int32).at[where_to].set(rows_of)[:HB]
    border = jax.vmap(jax.vmap(fill_one))(target, rowid)
    offs = jnp.arange(27, dtype=jnp.int32)
    off_x = (offs // 9 - 1)[None, None, :, None, None, None]
    off_y = (offs // 3 % 3 - 1)[None, None, :, None, None, None]
    off_z = (offs % 3 - 1)[None, None, :, None, None, None]
    big_i = jnp.arange(SLABS, dtype=jnp.int32)[:, None, None, None, None, None]
    big_j = jnp.arange(STRIPS, dtype=jnp.int32)[None, :, None, None, None, None]
    cell_x = jnp.arange(LX, dtype=jnp.int32)[None, None, None, :, None, None]
    cell_y = jnp.arange(LY, dtype=jnp.int32)[None, None, None, None, :, None]
    cell_z = jnp.arange(LZ, dtype=jnp.int32)[None, None, None, None, None, :]
    reach_x = big_i * LX + cell_x + off_x
    reach_y = big_j * LY + cell_y + off_y
    reach_z = cell_z + off_z
    inside = (reach_x >= 0) & (reach_x < SLABS * LX) & (reach_y >= 0) & (reach_y < STRIPS * LY) & (reach_z >= 0) & (reach_z < LZ)
    clip_x = jnp.clip(reach_x, 0, SLABS * LX - 1)
    clip_y = jnp.clip(reach_y, 0, STRIPS * LY - 1)
    clip_z = jnp.clip(reach_z, 0, LZ - 1)
    owner_i = clip_x // LX
    owner_j = clip_y // LY
    linear = (clip_x % LX * LY + clip_y % LY) * LZ + clip_z
    target_on = flat[owner_i, owner_j, linear]
    target_row = rowid[owner_i, owner_j, linear]
    target_rank = brank[owner_i, owner_j, linear]
    step_i = owner_i - big_i
    step_j = owner_j - big_j
    same = (step_i == 0) & (step_j == 0)
    index = jnp.where(same, target_row, positions + ((step_i + 1) * 3 + (step_j + 1)) * HB + target_rank)
    source_on = active[:, :, None, :, :, :]
    valid = inside & (target_on == 1) & (source_on == 1)
    index = jnp.where(valid, index, positions + 9 * HB).reshape(SLABS, STRIPS, 27, positions)
    dest = jnp.where(flat == 1, rowid, positions)

    def place(index_rows, dest_rows):
        return jnp.full((27, positions + 1), positions + 9 * HB, jnp.int32).at[:, dest_rows].set(index_rows)[:, :positions]
    mapped = jax.vmap(jax.vmap(place))(index, dest)
    return (mapped.astype(jnp.int32), border.astype(jnp.int32), counts)


def draw_neighbors(key, part):
    return geometry(key)[0]


def draw_boundary(key, part):
    return geometry(key)[1]


def draw_counts(key, part):
    return geometry(key)[2]


def draw_pre_norm(key, part):
    k_base, k_scale, k_mean = jax.random.split(jax.random.fold_in(key, 3), 3)
    ramp = (jnp.arange(SLABS, dtype=jnp.float32) / (SLABS - 1))[:, None, None, None]
    dev_scale = 1.0 + 2.0 * ramp
    chan_scale = jnp.exp(jax.random.uniform(k_scale, (C,), jnp.float32, 0.0, 2.3026))
    chan_mean = jax.random.normal(k_mean, (C,), jnp.float32) * 0.5
    noise = jax.random.normal(k_base, (SLABS, STRIPS, R, C), jnp.float32)
    return (noise * dev_scale * chan_scale + chan_mean * chan_scale + 0.5 * ramp).astype(jnp.bfloat16)


def strengthened(entries, own_key, source, target, shards_of, factor):
    owner, partner = [(jnp.arange(entries.shape[axis_at]) // (entries.shape[axis_at] // shards_of)).reshape([-1 if axis == axis_at else 1 for axis in range(entries.ndim)]) for axis_at in (source, target)]
    chosen = jax.random.permutation(own_key, shards_of)[partner]
    strong = (owner == chosen) | (owner == (partner + shards_of // 2) % shards_of)
    return jnp.where(strong, factor * entries, entries)


def level_of(own_key, extent, pieces, low, top_value):
    loudness, own = 1.0, jax.random.fold_in(own_key, 6)
    for position, parts in pieces:
        draws = jnp.exp(jax.random.uniform(jax.random.fold_in(own, position), (parts,), jnp.float32, low / len(pieces), top_value / len(pieces)))
        loudness = loudness * jnp.repeat(draws, extent[position] // parts).reshape([-1 if axis == position else 1 for axis in range(len(extent))])
    return loudness


def scatter_about(key, dims, width, limit, cuts=(), kind=jnp.bfloat16):
    result = width * jax.random.normal(key, dims, jnp.float32)
    if cuts:
        result = result * level_of(key, dims, cuts, -0.22, 0.18)
    return jnp.clip(result, -limit, limit).astype(kind)


def gaussian_with(rng, extent, deviation, most, pieces, heavy, kind=jnp.bfloat16):
    drawn = deviation * jax.random.normal(rng, extent, jnp.float32)
    if pieces:
        drawn = drawn * level_of(rng, extent, pieces, -0.22, 0.18)
    return jnp.clip(strengthened(drawn, jax.random.fold_in(rng, 3), *heavy), -most, most).astype(kind)


def setup_inputs(seed: int = 0) -> dict:
    splits = jax.random.split(jax.random.key(seed), 10)
    features = gaussian_with(splits[0], (SLABS, STRIPS, R, C), 1.0, 6.0, ((0, 32), (1, 4)), (0, 3, 32, 2.75))
    pre_norm = draw_pre_norm(jax.random.fold_in(splits[9], 71), 0)
    out_grad = scatter_about(splits[2], (SLABS, STRIPS, R, C), 1.0, 6.0, ((0, 32), (1, 4)))
    weight = scatter_about(splits[3], (27, C, C), C ** -0.5, 0.375)
    gamma = jnp.clip(1.0 + 0.18 * jax.random.normal(splits[4], (C,), jnp.float32), 0.1, 1.9)
    beta = scatter_about(splits[5], (C,), 0.5, 3.0, (), jnp.float32)
    neighbors = draw_neighbors(jax.random.fold_in(splits[9], 71), 0)
    boundary = draw_boundary(jax.random.fold_in(splits[9], 71), 0)
    counts = draw_counts(jax.random.fold_in(splits[9], 71), 0)
    return {"features": features, "pre_norm": pre_norm, "out_grad": out_grad, "weight": weight, "gamma": gamma, "beta": beta, "neighbors": neighbors, "boundary": boundary, "counts": counts}


def global_rows(neighbors, boundary):
    total = SLABS * STRIPS * R
    slab_ix = jnp.arange(SLABS, dtype=jnp.int32)[:, None, None, None]
    strip_ix = jnp.arange(STRIPS, dtype=jnp.int32)[None, :, None, None]
    local = neighbors < R
    absent = neighbors >= R + 9 * HB
    rel = jnp.clip(neighbors - R, 0, 9 * HB - 1)
    block = rel // HB
    slot = rel % HB
    near_x = jnp.clip(slab_ix + block // 3 - 1, 0, SLABS - 1)
    near_y = jnp.clip(strip_ix + block % 3 - 1, 0, STRIPS - 1)
    brow = boundary[near_x, near_y, slot]
    remote = jnp.where(brow >= R, total, (near_x * STRIPS + near_y) * R + brow)
    own = (slab_ix * STRIPS + strip_ix) * R + neighbors
    return jnp.where(local, own, jnp.where(absent, total, remote)).astype(jnp.int32)

def reference(features, pre_norm, out_grad, weight, gamma, beta, neighbors, boundary, counts):
    total = SLABS * STRIPS * R
    live = (jnp.arange(R, dtype=jnp.int32)[None, None, :] < counts[:, :, None])[..., None]
    zval = pre_norm.astype(jnp.float32)
    zlive = jnp.where(live, zval, jnp.float32(0.0))
    count = jnp.sum(counts).astype(jnp.float32)
    mean = lax.optimization_barrier(jnp.sum(zlive, axis=(0, 1, 2))) / count
    var = lax.optimization_barrier(jnp.sum(zlive * zval, axis=(0, 1, 2))) / count - mean * mean
    rstd = lax.rsqrt(var + 1e-05)
    zhat = (zval - mean) * rstd
    act = gamma * zhat + beta
    sig = jax.nn.sigmoid(act)
    grad_act = jnp.where(live, out_grad.astype(jnp.float32) * sig * (1.0 + act * (1.0 - sig)), jnp.float32(0.0))
    beta_grad = lax.optimization_barrier(jnp.sum(grad_act, axis=(0, 1, 2)))
    gamma_grad = lax.optimization_barrier(jnp.sum(grad_act * zhat, axis=(0, 1, 2)))
    dz = jnp.where(live, gamma * rstd * (grad_act - beta_grad / count - zhat * gamma_grad / count), jnp.float32(0.0)).astype(jnp.bfloat16)
    source = global_rows(neighbors, boundary)
    source_k = jnp.moveaxis(source, 2, 0).reshape(27, total)
    dz_flat = dz.reshape(total, C)
    x_padded = jnp.concatenate([features.reshape(total, C), jnp.zeros((1, C), jnp.bfloat16)], axis=0)

    def wgrad_one(index_row):
        picked = x_padded[index_row]
        return jnp.dot(picked.T, dz_flat, preferred_element_type=jnp.float32)
    weight_grad = lax.map(wgrad_one, source_k)

    def add_one(k, accum):
        contrib = jnp.dot(dz_flat, weight[k].T, preferred_element_type=jnp.float32)
        return accum.at[source_k[k]].add(contrib)
    accum = lax.fori_loop(0, 27, add_one, jnp.zeros((total + 1, C), jnp.float32))
    in_grad = accum[:total].reshape(SLABS, STRIPS, R, C).astype(jnp.bfloat16)
    return (in_grad, weight_grad.reshape(27 * C, C), gamma_grad, beta_grad)
```

```python
import functools

import jax
import jax.numpy as jnp
from jax import lax
from jax.experimental import pallas as pl
from jax.experimental.pallas import tpu as pltpu
from jax.sharding import Mesh
from jax.sharding import PartitionSpec as P

GX_GY = ("gx_0", "gx_1", "gx_2", "gy")
GX = ("gx_0", "gx_1", "gx_2")


def one_axis_at_a_time(shard, axes):
    return functools.reduce(lax.psum, axes, shard)


def extended(block, sides, width):
    for axis, dim in sides:
        count = lax.axis_size(axis)
        forward = [(i, i + 1) for i in range(count - 1)]
        backward = [(target, source) for source, target in forward]
        low = lax.ppermute(
            lax.slice_in_dim(block, block.shape[dim] - width, None, axis=dim), axis, forward
        )
        high = lax.ppermute(lax.slice_in_dim(block, 0, width, axis=dim), axis, backward)
        block = jnp.concatenate([low, block, high], axis=dim)
    return block


def sum_in_order(blocks, axes, order):
    lengths = [lax.axis_size(a) for a in axes]
    blocks = blocks.reshape(*lengths, *blocks.shape[1:])
    blocks = blocks.transpose(*order, *range(len(axes), blocks.ndim))
    blocks = blocks.reshape(-1, *blocks.shape[len(axes) :])
    for k in order:
        blocks = lax.psum_scatter(blocks, axes[k], scatter_dimension=0, tiled=True)
    return blocks[0]


def cut_along(shard, dim, length):
    before, after = (shard.shape[:dim], shard.shape[dim + 1 :])
    return jnp.moveaxis(shard.reshape(*before, length, -1, *after), dim, 0)


def sum_by_axis_2(shard, axes, order, dim):
    length = lax.axis_size(axes)
    return sum_in_order(cut_along(shard, dim, length), axes, order)


def sum_at_owner(shard, axis, dim):
    blocks = cut_along(shard, dim, lax.axis_size(axis))
    arrived = lax.all_to_all(blocks, axis, split_axis=0, concat_axis=0, tiled=True)
    return arrived.sum(axis=0)


def gather_rows(local, border):
    padded = jnp.concatenate([local, jnp.zeros((1, local.shape[1]), local.dtype)], axis=0)
    return jnp.take(padded, border, axis=0, mode="clip")


def make_table(local, around):
    flat = around.reshape(-1, local.shape[1])
    tail = jnp.zeros((WIN, C), local.dtype)
    return jnp.concatenate([local, flat, tail], axis=0)


C = 256
R = 2048
SUB = 128
TILE = 256
WIN = 256
NROW = 8384
FAR = 1.0e6


def plan_windows(links):
    idx = links[::-1]
    idx = jnp.where(idx < NROW, idx, jnp.int32(FAR))
    cut = idx.reshape(9, 3, R // SUB, SUB)
    starts = []
    for _ in range(3):
        low = jnp.min(cut, axis=(1, 3))
        start = jnp.where(low < NROW, low // 16 * 16, jnp.int32(FAR))
        starts.append(start)
        cut = jnp.where(cut >= start[:, None, :, None] + WIN, cut, jnp.int32(FAR))
    first, second, third = starts
    starts = jnp.stack([jnp.minimum(first, NROW), jnp.minimum(second, NROW), third], axis=-1)
    columns = jnp.pad(idx.astype(jnp.float32).T, ((0, 0), (0, 5)), constant_values=FAR)
    return columns, starts.reshape(-1)


def one_hot(columns, start):
    lanes = lax.broadcasted_iota(jnp.int32, (SUB, WIN), 1).astype(jnp.float32)
    place = columns - start.astype(jnp.float32)
    return jnp.where(place == lanes, 1.0, 0.0).astype(jnp.bfloat16)


def dot(a, b, dims):
    return lax.dot_general(a, b, (dims, ((), ())), preferred_element_type=jnp.float32)


def conv_kernel(starts, idx, table, feat, weight, in_grad, wgrad, acc, feat_t, picked, colbuf):
    step = pl.program_id(0)
    tiles = R // TILE

    @pl.when(step == 0)
    def _():
        acc[...] = jnp.zeros_like(acc)

        @pl.loop(0, tiles)
        def _(t):
            rows = pl.ds(pl.multiple_of(t * TILE, TILE), TILE)
            feat_t[t] = feat[rows, :].T

    def gather(t, slot):
        for half in range(TILE // SUB):
            row = pl.multiple_of(t * TILE + half * SUB, SUB)
            at = (step * (R // SUB) + t * (TILE // SUB) + half) * 3
            columns = pltpu.roll(idx[pl.ds(row, SUB), :], (128 - 3 * step) % 128, 1)
            colbuf[pl.ds(half * SUB, SUB), :] = columns
            total = None
            cols = [jnp.broadcast_to(columns[:, i : i + 1], (SUB, WIN)) for i in range(3)]
            for w in range(2):
                start = pl.multiple_of(starts[at + w], 16)
                hot = jnp.concatenate([one_hot(c, start) for c in cols], axis=0)
                part = dot(hot, table[pl.ds(start, WIN), :], ((1,), (0,)))
                total = part if total is None else total + part
            total = total.astype(jnp.bfloat16)
            for i in range(3):
                picked[slot, pl.ds(row, SUB), i * C : (i + 1) * C] = total[i * SUB : (i + 1) * SUB]

    def gather_rest(t, slot):
        for half in range(TILE // SUB):
            row = pl.multiple_of(t * TILE + half * SUB, SUB)
            at = (step * (R // SUB) + t * (TILE // SUB) + half) * 3

            def more(start):
                columns = colbuf[pl.ds(half * SUB, SUB), :]
                start = pl.multiple_of(start, 16)
                cols = [jnp.broadcast_to(columns[:, i : i + 1], (SUB, WIN)) for i in range(3)]
                hot = jnp.concatenate([one_hot(c, start) for c in cols], axis=0)
                part = dot(hot, table[pl.ds(start, WIN), :], ((1,), (0,))).astype(jnp.bfloat16)
                for i in range(3):
                    picked[slot, pl.ds(row, SUB), i * C : (i + 1) * C] += part[
                        i * SUB : (i + 1) * SUB
                    ]
                lane = lax.broadcasted_iota(jnp.int32, (SUB, 128), 1)
                ahead = (lane < 3) & (columns >= (start + WIN).astype(jnp.float32))
                low = jnp.min(jnp.where(ahead, columns, FAR)).astype(jnp.int32)
                return jnp.where(low < NROW, low // 16 * 16, jnp.int32(FAR))

            lax.while_loop(lambda start: start < NROW, more, starts[at + 2])

    def dense(t, slot):
        rows = pl.ds(pl.multiple_of(t * TILE, TILE), TILE)
        total = acc[rows, :]
        for i in range(3):
            block = picked[slot, rows, i * C : (i + 1) * C]
            total = total + dot(block, weight[i], ((1,), (1,)))
            wgrad[i] += dot(feat_t[t], block, ((1,), (0,)))
        acc[rows, :] = total

    now = step % 2

    @pl.when(step > 0)
    def _():
        wgrad[...] = jnp.zeros_like(wgrad)

    @pl.when(step == 0)
    def _():
        @pl.loop(0, tiles)
        def _(t):
            gather(t, now)
            gather_rest(t, now)

    @pl.when((step > 0) & (step < 9))
    def _():
        @pl.loop(0, tiles)
        def _(t):
            gather(t, now)
            dense(t, 1 - now)
            gather_rest(t, now)

    @pl.when(step == 9)
    def _():
        @pl.loop(0, tiles)
        def _(t):
            dense(t, 1 - now)
        in_grad[...] = acc[...].astype(jnp.bfloat16)


def convolve(starts, idx, table, feat, weight):
    idx = jnp.pad(idx, ((0, 0), (0, 96)), constant_values=FAR)
    whole = pl.BlockSpec(memory_space=pltpu.VMEM)
    in_grad, wgrad = pl.pallas_call(
        conv_kernel,
        grid=(10,),
        out_shape=(
            jax.ShapeDtypeStruct((R, C), jnp.bfloat16),
            jax.ShapeDtypeStruct((27, C, C), jnp.float32),
        ),
        in_specs=[
            pl.BlockSpec(memory_space=pltpu.SMEM),
            whole,
            whole,
            whole,
            pl.BlockSpec((3, C, C), lambda g: (jnp.maximum(g - 1, 0), 0, 0)),
        ],
        out_specs=(
            whole,
            pl.BlockSpec((3, C, C), lambda g: (jnp.maximum(g - 1, 0), 0, 0)),
        ),
        scratch_shapes=[
            pltpu.VMEM((R, C), jnp.float32),
            pltpu.VMEM((R // TILE, C, TILE), jnp.bfloat16),
            pltpu.VMEM((2, R, 3 * C), jnp.bfloat16),
            pltpu.VMEM((TILE, 128), jnp.float32),
        ],
        compiler_params=pltpu.CompilerParams(vmem_limit_bytes=56 * 1024 * 1024),
        cost_estimate=pl.CostEstimate(
            flops=30_000_000_000, bytes_accessed=20_000_000, transcendentals=0
        ),
        name="conv_backward",
    )(starts, idx, table, feat, weight)
    return in_grad, wgrad.reshape(27 * C, C)


def body(features, pre_norm, out_grad, weight, gamma, beta, neighbors, boundary, counts):
    feat = features[0, 0]
    rows = feat.shape[0]
    chans = feat.shape[1]
    border = boundary[0, 0]
    links = neighbors[0, 0]
    live = (lax.iota(jnp.int32, rows) < counts[0, 0])[:, None]
    zval = pre_norm[0, 0].astype(jnp.float32)
    zlive = jnp.where(live, zval, jnp.float32(0.0))
    sum_z, sum_sq, sum_count = (
        one_axis_at_a_time(jnp.sum(zlive, axis=0), GX_GY),
        one_axis_at_a_time(jnp.sum(zlive * zval, axis=0), GX_GY),
        one_axis_at_a_time(counts[0].astype(jnp.float32), GX_GY),
    )
    count = sum_count[0]
    mean = sum_z / count
    var = sum_sq / count - mean * mean
    rstd = lax.rsqrt(var + 1e-05)
    zhat = (zval - mean) * rstd
    act = gamma * zhat + beta
    sig = jax.nn.sigmoid(act)
    grad_act = jnp.where(
        live, out_grad[0, 0].astype(jnp.float32) * sig * (1.0 + act * (1.0 - sig)), jnp.float32(0.0)
    )
    beta_grad, gamma_grad = (
        one_axis_at_a_time(jnp.sum(grad_act, axis=0), GX_GY),
        one_axis_at_a_time(jnp.sum(grad_act * zhat, axis=0), GX_GY),
    )
    dz = jnp.where(
        live,
        gamma * rstd * (grad_act - beta_grad / count - zhat * gamma_grad / count),
        jnp.float32(0.0),
    ).astype(jnp.bfloat16)
    grad_edge = gather_rows(dz, border)
    grad_around = extended(grad_edge[None, None], ((GX, 0), ("gy", 1)), 1)
    grad_table = make_table(dz, grad_around)

    idx, starts = plan_windows(links)
    in_grad, local_wgrad = convolve(starts, idx, grad_table, feat, weight)
    slab_part = sum_by_axis_2(local_wgrad, GX, (2, 0, 1), 0)
    weight_grad = sum_at_owner(slab_part, "gy", 0)
    in_grad = in_grad[None, None]
    return (in_grad, weight_grad, gamma_grad, beta_grad)


def solution(mesh):
    torus = Mesh(mesh.devices.reshape(4, 4, 2, mesh.shape["gy"]), ("gx_0", "gx_1", "gx_2", "gy"))
    return jax.shard_map(
        body,
        mesh=torus,
        in_specs=(
            P(GX, "gy", None, None),
            P(GX, "gy", None, None),
            P(GX, "gy", None, None),
            P(),
            P(),
            P(),
            P(GX, "gy", None, None),
            P(GX, "gy", None),
            P(GX, "gy"),
        ),
        out_specs=(P(GX, "gy", None, None), P(GX_GY, None), P(), P()),
        check_vma=False,
    )
```

```python
import functools

import jax
import jax.numpy as jnp
from jax import lax
from jax.experimental import pallas as pl
from jax.experimental.pallas import tpu as pltpu
from jax.sharding import Mesh
from jax.sharding import PartitionSpec as P

GX_GY = ("gx_0", "gx_1", "gx_2", "gy")
GX = ("gx_0", "gx_1", "gx_2")
MESH = pl.DeviceIdType.MESH


def one_axis_at_a_time(shard, axes):
    return functools.reduce(lax.psum, axes, shard)


def extended(block, sides, width):
    for axis, dim in sides:
        count = lax.axis_size(axis)
        forward = [(i, i + 1) for i in range(count - 1)]
        backward = [(target, source) for source, target in forward]
        low = lax.ppermute(
            lax.slice_in_dim(block, block.shape[dim] - width, None, axis=dim), axis, forward
        )
        high = lax.ppermute(lax.slice_in_dim(block, 0, width, axis=dim), axis, backward)
        block = jnp.concatenate([low, block, high], axis=dim)
    return block


def gather_rows(local, border):
    padded = jnp.concatenate([local, jnp.zeros((1, local.shape[1]), local.dtype)], axis=0)
    return jnp.take(padded, border, axis=0, mode="clip")


def make_table(local, around):
    flat = around.reshape(-1, local.shape[1])
    tail = jnp.zeros((WIN, C), local.dtype)
    return jnp.concatenate([local, flat, tail], axis=0)


C = 256
R = 2048
SUB = 128
TILE = 256
WIN = 256
NROW = 8384
FAR = 1.0e6


def plan_windows(links):
    idx = links[::-1]
    idx = jnp.where(idx < NROW, idx, jnp.int32(FAR))
    cut = idx.reshape(9, 3, R // SUB, SUB)
    starts = []
    for _ in range(3):
        low = jnp.min(cut, axis=(1, 3))
        start = jnp.where(low < NROW, low // 16 * 16, jnp.int32(FAR))
        starts.append(start)
        cut = jnp.where(cut >= start[:, None, :, None] + WIN, cut, jnp.int32(FAR))
    first, second, third = starts
    starts = jnp.stack([jnp.minimum(first, NROW), jnp.minimum(second, NROW), third], axis=-1)
    columns = jnp.pad(idx.astype(jnp.float32).T, ((0, 0), (0, 5)), constant_values=FAR)
    return columns, starts.reshape(-1)


def one_hot(columns, start):
    lanes = lax.broadcasted_iota(jnp.int32, (SUB, WIN), 1).astype(jnp.float32)
    place = columns - start.astype(jnp.float32)
    return jnp.where(place == lanes, 1.0, 0.0).astype(jnp.bfloat16)


def dot(a, b, dims):
    return lax.dot_general(a, b, (dims, ((), ())), preferred_element_type=jnp.float32)


def conv_kernel(starts, idx, table, feat, weight, in_grad, wgrad, acc, feat_t, picked, colbuf):
    step = pl.program_id(0)
    tiles = R // TILE

    @pl.when(step == 0)
    def _():
        acc[...] = jnp.zeros_like(acc)

        @pl.loop(0, tiles)
        def _(t):
            rows = pl.ds(pl.multiple_of(t * TILE, TILE), TILE)
            feat_t[t] = feat[rows, :].T

    def gather(t, slot):
        for half in range(TILE // SUB):
            row = pl.multiple_of(t * TILE + half * SUB, SUB)
            at = (step * (R // SUB) + t * (TILE // SUB) + half) * 3
            columns = pltpu.roll(idx[pl.ds(row, SUB), :], (128 - 3 * step) % 128, 1)
            colbuf[pl.ds(half * SUB, SUB), :] = columns
            total = None
            cols = [jnp.broadcast_to(columns[:, i : i + 1], (SUB, WIN)) for i in range(3)]
            for w in range(2):
                start = pl.multiple_of(starts[at + w], 16)
                hot = jnp.concatenate([one_hot(c, start) for c in cols], axis=0)
                part = dot(hot, table[pl.ds(start, WIN), :], ((1,), (0,)))
                total = part if total is None else total + part
            total = total.astype(jnp.bfloat16)
            for i in range(3):
                picked[slot, pl.ds(row, SUB), i * C : (i + 1) * C] = total[i * SUB : (i + 1) * SUB]

    def gather_rest(t, slot):
        for half in range(TILE // SUB):
            row = pl.multiple_of(t * TILE + half * SUB, SUB)
            at = (step * (R // SUB) + t * (TILE // SUB) + half) * 3

            def more(start):
                columns = colbuf[pl.ds(half * SUB, SUB), :]
                start = pl.multiple_of(start, 16)
                cols = [jnp.broadcast_to(columns[:, i : i + 1], (SUB, WIN)) for i in range(3)]
                hot = jnp.concatenate([one_hot(c, start) for c in cols], axis=0)
                part = dot(hot, table[pl.ds(start, WIN), :], ((1,), (0,))).astype(jnp.bfloat16)
                for i in range(3):
                    picked[slot, pl.ds(row, SUB), i * C : (i + 1) * C] += part[
                        i * SUB : (i + 1) * SUB
                    ]
                lane = lax.broadcasted_iota(jnp.int32, (SUB, 128), 1)
                ahead = (lane < 3) & (columns >= (start + WIN).astype(jnp.float32))
                low = jnp.min(jnp.where(ahead, columns, FAR)).astype(jnp.int32)
                return jnp.where(low < NROW, low // 16 * 16, jnp.int32(FAR))

            lax.while_loop(lambda start: start < NROW, more, starts[at + 2])

    def dense(t, slot):
        rows = pl.ds(pl.multiple_of(t * TILE, TILE), TILE)
        total = acc[rows, :]
        for i in range(3):
            block = picked[slot, rows, i * C : (i + 1) * C]
            total = total + dot(block, weight[i], ((1,), (1,)))
            wgrad[i] += dot(feat_t[t], block, ((1,), (0,)))
        acc[rows, :] = total

    now = step % 2

    @pl.when(step > 0)
    def _():
        wgrad[...] = jnp.zeros_like(wgrad)

    @pl.when(step == 0)
    def _():
        @pl.loop(0, tiles)
        def _(t):
            gather(t, now)
            gather_rest(t, now)

    @pl.when((step > 0) & (step < 9))
    def _():
        @pl.loop(0, tiles)
        def _(t):
            gather(t, now)
            dense(t, 1 - now)
            gather_rest(t, now)

    @pl.when(step == 9)
    def _():
        @pl.loop(0, tiles)
        def _(t):
            dense(t, 1 - now)
        in_grad[...] = acc[...].astype(jnp.bfloat16)


def convolve(starts, idx, table, feat, weight):
    idx = jnp.pad(idx, ((0, 0), (0, 96)), constant_values=FAR)
    whole = pl.BlockSpec(memory_space=pltpu.VMEM)
    in_grad, wgrad = pl.pallas_call(
        conv_kernel,
        grid=(10,),
        out_shape=(
            jax.ShapeDtypeStruct((R, C), jnp.bfloat16),
            jax.ShapeDtypeStruct((27, C, C), jnp.float32),
        ),
        in_specs=[
            pl.BlockSpec(memory_space=pltpu.SMEM),
            whole,
            whole,
            whole,
            pl.BlockSpec((3, C, C), lambda g: (jnp.maximum(g - 1, 0), 0, 0)),
        ],
        out_specs=(
            whole,
            pl.BlockSpec((3, C, C), lambda g: (jnp.maximum(g - 1, 0), 0, 0)),
        ),
        scratch_shapes=[
            pltpu.VMEM((R, C), jnp.float32),
            pltpu.VMEM((R // TILE, C, TILE), jnp.bfloat16),
            pltpu.VMEM((2, R, 3 * C), jnp.bfloat16),
            pltpu.VMEM((TILE, 128), jnp.float32),
        ],
        compiler_params=pltpu.CompilerParams(vmem_limit_bytes=56 * 1024 * 1024),
        cost_estimate=pl.CostEstimate(
            flops=30_000_000_000, bytes_accessed=20_000_000, transcendentals=0
        ),
        name="conv_backward",
    )(starts, idx, table, feat, weight)
    return in_grad, wgrad.reshape(27 * C, C)


AXES = ("gy", "gx_1", "gx_0")
TILE_AT = (0, 16, 32, 38)
HOLDS = ((0,), (1,), (2, 3))


def scatter_kernel(part, out, local, s_a, r_a, *rest):
    s_b, r_b, s_c, r_c, s_d, r_d = (rest[3 * i : 3 * i + 3] for i in range(6))
    load_sem, a_sem, b_sem, c_sem, d_sem = rest[18:]
    pos = [lax.axis_index(a) for a in AXES]
    core = lax.axis_index("gx_2")
    z = pos[2]

    def around(i):
        return lax.rem(z + 1 + i, 4)

    loads = []
    for i in range(4):
        rows = pl.ds(pl.multiple_of(around(i) * 1728, 64), 1728)
        loads.append(pltpu.make_async_copy(part.at[rows, :], local.at[i], load_sem.at[i]))
        loads[-1].start()

    barrier = pltpu.get_barrier_semaphore()
    pl.semaphore_signal(barrier, 1, device_id={"gx_2": 1 - core}, device_id_type=MESH)
    for axis, at in zip(AXES, pos):
        for d in range(1, 4):
            peer = {axis: lax.rem(at + d, 4)}
            pl.semaphore_signal(barrier, 1, device_id=peer, device_id_type=MESH)

    def block(i, y, x, side, t):
        skip = (x * 54 + TILE_AT[t]) % 8
        base = (y * 2 + side) * 216 + x * 54 + TILE_AT[t] - skip
        rows = local[i, pl.ds(pl.multiple_of(base, 8), 24 if skip else 16), :]
        return rows[skip : skip + 16]

    sends = []

    def send(src, dst, sems, at, device):
        copy = pltpu.make_async_remote_copy(
            src_ref=src,
            dst_ref=dst,
            send_sem=sems.at[(0,) + at],
            recv_sem=sems.at[(1,) + at],
            device_id=device,
            device_id_type=MESH,
        )
        copy.start()
        sends.append(copy)
        return copy

    first = []
    for i in range(4):
        loads[i].wait()

        @pl.loop(0, 4)
        def _(y):
            for x in range(4):
                for t in range(4):
                    mine = block(i, y, x, 1 - core, t)
                    s_a[i, y * 4 + x, t] = mine.astype(jnp.bfloat16)

        if i == 0:
            pl.semaphore_wait(barrier, 10)
        first.append(send(s_a.at[i], r_a.at[i], a_sem, (i,), {"gx_2": 1 - core}))

    def spread(p, stage, sems, src, dst):
        axis = (p + stage) % 3
        return [
            send(
                src.at[lax.rem(pos[axis] + d, 4)],
                dst.at[d - 1],
                sems,
                (p, d - 1),
                {AXES[axis]: lax.rem(pos[axis] + d, 4)},
            )
            for d in range(1, 4)
        ]

    second = [None, None, []]
    for i in range(4):
        first[i].wait_recv()
        z_of = around(i)

        @pl.loop(0, 4)
        def _(y):
            for x in range(4):
                for t in range(4):
                    both = block(i, y, x, core, t) + r_a[i, y * 4 + x, t].astype(jnp.float32)
                    both = both.astype(jnp.bfloat16)
                    if t == 0:
                        s_b[0][x, y * 4 + z_of, 0] = both
                    elif t == 1:
                        s_b[1][y, z_of * 4 + x, 0] = both
                    else:
                        s_b[2][z_of, x * 4 + y, t - 2] = both

        if i < 3:
            second[2].append(
                send(s_b[2].at[z_of], r_b[2].at[i], b_sem, (2, i), {"gx_0": z_of})
            )
    for p in range(2):
        second[p] = spread(p, 0, b_sem, s_b[p], r_b[p])

    def total(own, came, at):
        kind = jnp.float32
        return (own[at].astype(kind) + came[(0,) + at[1:]].astype(kind)) + (
            came[(1,) + at[1:]].astype(kind) + came[(2,) + at[1:]].astype(kind)
        )

    third = []
    for p in range(3):
        for copy in second[p]:
            copy.wait_recv()
        me = pos[p]

        @pl.loop(0, 16)
        def _(j):
            for t in range(len(HOLDS[p])):
                s_c[p][j // 4, j % 4, t] = total(s_b[p], r_b[p], (me, j, t)).astype(jnp.bfloat16)

        third.append(spread(p, 1, c_sem, s_c[p], r_c[p]))

    fourth = []
    for p in range(3):
        for copy in third[p]:
            copy.wait_recv()
        me = pos[(p + 1) % 3]

        @pl.loop(0, 4)
        def _(j):
            for t in range(len(HOLDS[p])):
                s_d[p][j, t] = total(s_c[p], r_c[p], (me, j, t))

        fourth.append(spread(p, 2, d_sem, s_d[p], r_d[p]))

    for p in range(3):
        for copy in fourth[p]:
            copy.wait_recv()
        me = pos[(p + 2) % 3]
        for t, which in enumerate(HOLDS[p]):
            out[TILE_AT[which] : TILE_AT[which] + 16, :] = total(s_d[p], r_d[p], (me, t))

    for copy in sends:
        copy.wait_send()


def scatter_sum(part):
    def stage(lead, kind):
        return [pltpu.VMEM(lead + (len(h), 16, C), kind) for h in HOLDS]

    half, full = jnp.bfloat16, jnp.float32
    return pl.pallas_call(
        scatter_kernel,
        out_shape=jax.ShapeDtypeStruct((54, C), jnp.float32),
        in_specs=[pl.BlockSpec(memory_space=pl.ANY)],
        out_specs=pl.BlockSpec(memory_space=pltpu.VMEM),
        scratch_shapes=[
            pltpu.VMEM((4, 1728, C), jnp.float32),
            pltpu.VMEM((4, 16, 4, 16, C), jnp.bfloat16),
            pltpu.VMEM((4, 16, 4, 16, C), jnp.bfloat16),
            *stage((4, 16), half),
            *stage((3, 16), half),
            *stage((4, 4), half),
            *stage((3, 4), half),
            *stage((4,), full),
            *stage((3,), full),
            pltpu.SemaphoreType.DMA((4,)),
            pltpu.SemaphoreType.DMA((2, 4)),
            pltpu.SemaphoreType.DMA((2, 3, 3)),
            pltpu.SemaphoreType.DMA((2, 3, 3)),
            pltpu.SemaphoreType.DMA((2, 3, 3)),
        ],
        compiler_params=pltpu.CompilerParams(
            collective_id=1, has_side_effects=True, vmem_limit_bytes=40 * 1024 * 1024
        ),
        cost_estimate=pl.CostEstimate(flops=10_000_000, bytes_accessed=7_000_000, transcendentals=0),
        name="scatter_sum",
    )(part)


def body(features, pre_norm, out_grad, weight, gamma, beta, neighbors, boundary, counts):
    feat = features[0, 0]
    rows = feat.shape[0]
    chans = feat.shape[1]
    border = boundary[0, 0]
    links = neighbors[0, 0]
    live = (lax.iota(jnp.int32, rows) < counts[0, 0])[:, None]
    zval = pre_norm[0, 0].astype(jnp.float32)
    zlive = jnp.where(live, zval, jnp.float32(0.0))
    sum_z, sum_sq, sum_count = (
        one_axis_at_a_time(jnp.sum(zlive, axis=0), GX_GY),
        one_axis_at_a_time(jnp.sum(zlive * zval, axis=0), GX_GY),
        one_axis_at_a_time(counts[0].astype(jnp.float32), GX_GY),
    )
    count = sum_count[0]
    mean = sum_z / count
    var = sum_sq / count - mean * mean
    rstd = lax.rsqrt(var + 1e-05)
    zhat = (zval - mean) * rstd
    act = gamma * zhat + beta
    sig = jax.nn.sigmoid(act)
    grad_act = jnp.where(
        live, out_grad[0, 0].astype(jnp.float32) * sig * (1.0 + act * (1.0 - sig)), jnp.float32(0.0)
    )
    beta_grad, gamma_grad = (
        one_axis_at_a_time(jnp.sum(grad_act, axis=0), GX_GY),
        one_axis_at_a_time(jnp.sum(grad_act * zhat, axis=0), GX_GY),
    )
    dz = jnp.where(
        live,
        gamma * rstd * (grad_act - beta_grad / count - zhat * gamma_grad / count),
        jnp.float32(0.0),
    ).astype(jnp.bfloat16)
    grad_edge = gather_rows(dz, border)
    grad_around = extended(grad_edge[None, None], ((GX, 0), ("gy", 1)), 1)
    grad_table = make_table(dz, grad_around)

    idx, starts = plan_windows(links)
    in_grad, local_wgrad = convolve(starts, idx, grad_table, feat, weight)
    weight_grad = scatter_sum(local_wgrad)
    in_grad = in_grad[None, None]
    return (in_grad, weight_grad, gamma_grad, beta_grad)


def solution(mesh):
    torus = Mesh(mesh.devices.reshape(4, 4, 2, mesh.shape["gy"]), ("gx_0", "gx_1", "gx_2", "gy"))
    return jax.shard_map(
        body,
        mesh=torus,
        in_specs=(
            P(GX, "gy", None, None),
            P(GX, "gy", None, None),
            P(GX, "gy", None, None),
            P(),
            P(),
            P(),
            P(GX, "gy", None, None),
            P(GX, "gy", None),
            P(GX, "gy"),
        ),
        out_specs=(P(GX, "gy", None, None), P(GX_GY, None), P(), P()),
        check_vma=False,
    )
```

```python
import jax
import jax.numpy as jnp
from jax import lax
from jax.experimental import pallas as pl
from jax.experimental.pallas import tpu as pltpu
from jax.sharding import Mesh
from jax.sharding import PartitionSpec as P

GX_GY = ("gx_0", "gx_1", "gx_2", "gy")
GX = ("gx_0", "gx_1", "gx_2")
MESH = pl.DeviceIdType.MESH


C = 256
R = 2048
SUB = 128
TILE = 256
WIN = 256
NROW = 8384
FAR = 1.0e6


def one_hot(columns, start):
    lanes = lax.broadcasted_iota(jnp.int32, (SUB, WIN), 1).astype(jnp.float32)
    place = columns - start.astype(jnp.float32)
    return jnp.where(place == lanes, 1.0, 0.0).astype(jnp.bfloat16)


def dot(a, b, dims):
    return lax.dot_general(a, b, (dims, ((), ())), preferred_element_type=jnp.float32)


def conv_kernel(starts, idx, table, feat, weight, in_grad, wgrad, acc, feat_t, picked, colbuf):
    step = pl.program_id(0)
    tiles = R // TILE
    lane0 = jnp.maximum(24 - 3 * step, 0)

    @pl.when(step == 0)
    def _():
        acc[...] = jnp.zeros_like(acc)

        @pl.loop(0, tiles)
        def _(t):
            rows = pl.ds(pl.multiple_of(t * TILE, TILE), TILE)
            feat_t[t] = feat[rows, :].T

    def gather(t, slot):
        for half in range(TILE // SUB):
            row = pl.multiple_of(t * TILE + half * SUB, SUB)
            at = (t * (TILE // SUB) + half) * 8
            columns = pltpu.roll(idx[pl.ds(row, SUB), :], (128 - lane0) % 128, 1)
            colbuf[pl.ds(half * SUB, SUB), :] = columns
            total = None
            cols = [jnp.broadcast_to(columns[:, 2 - i : 3 - i], (SUB, WIN)) for i in range(3)]
            for w in range(2):
                start = pl.multiple_of(starts[at + w, lane0], 16)
                hot = jnp.concatenate([one_hot(c, start) for c in cols], axis=0)
                part = dot(hot, table[pl.ds(start, WIN), :], ((1,), (0,)))
                total = part if total is None else total + part
            total = total.astype(jnp.bfloat16)
            for i in range(3):
                picked[slot, pl.ds(row, SUB), i * C : (i + 1) * C] = total[i * SUB : (i + 1) * SUB]

    def gather_rest(t, slot):
        for half in range(TILE // SUB):
            row = pl.multiple_of(t * TILE + half * SUB, SUB)
            at = (t * (TILE // SUB) + half) * 8

            def more(start):
                columns = colbuf[pl.ds(half * SUB, SUB), :]
                start = pl.multiple_of(start, 16)
                cols = [jnp.broadcast_to(columns[:, 2 - i : 3 - i], (SUB, WIN)) for i in range(3)]
                hot = jnp.concatenate([one_hot(c, start) for c in cols], axis=0)
                part = dot(hot, table[pl.ds(start, WIN), :], ((1,), (0,))).astype(jnp.bfloat16)
                for i in range(3):
                    picked[slot, pl.ds(row, SUB), i * C : (i + 1) * C] += part[
                        i * SUB : (i + 1) * SUB
                    ]
                lane = lax.broadcasted_iota(jnp.int32, (SUB, 128), 1)
                ahead = (lane < 3) & (columns >= (start + WIN).astype(jnp.float32))
                low = jnp.min(jnp.where(ahead, columns, FAR)).astype(jnp.int32)
                return jnp.where(low < NROW, low // 16 * 16, jnp.int32(FAR))

            lax.while_loop(lambda start: start < NROW, more, starts[at + 2, lane0])

    def dense(t, slot):
        rows = pl.ds(pl.multiple_of(t * TILE, TILE), TILE)
        total = acc[rows, :]
        for i in range(3):
            block = picked[slot, rows, i * C : (i + 1) * C]
            total = total + dot(block, weight[i], ((1,), (1,)))
            wgrad[i] += dot(feat_t[t], block, ((1,), (0,)))
        acc[rows, :] = total

    now = step % 2

    @pl.when(step > 0)
    def _():
        wgrad[...] = jnp.zeros_like(wgrad)

    @pl.when(step == 0)
    def _():
        @pl.loop(0, tiles)
        def _(t):
            gather(t, now)
            gather_rest(t, now)

    @pl.when((step > 0) & (step < 9))
    def _():
        @pl.loop(0, tiles)
        def _(t):
            gather(t, now)
            dense(t, 1 - now)
            gather_rest(t, now)

    @pl.when(step == 9)
    def _():
        @pl.loop(0, tiles)
        def _(t):
            dense(t, 1 - now)
        in_grad[...] = acc[...].astype(jnp.bfloat16)


def convolve(starts, idx, table, feat, weight):
    whole = pl.BlockSpec(memory_space=pltpu.VMEM)
    in_grad, wgrad = pl.pallas_call(
        conv_kernel,
        grid=(10,),
        out_shape=(
            jax.ShapeDtypeStruct((R, C), jnp.bfloat16),
            jax.ShapeDtypeStruct((27, C, C), jnp.float32),
        ),
        in_specs=[
            pl.BlockSpec(memory_space=pltpu.SMEM),
            whole,
            whole,
            whole,
            pl.BlockSpec((3, C, C), lambda g: (jnp.maximum(g - 1, 0), 0, 0)),
        ],
        out_specs=(
            whole,
            pl.BlockSpec((3, C, C), lambda g: (jnp.maximum(g - 1, 0), 0, 0)),
        ),
        scratch_shapes=[
            pltpu.VMEM((R, C), jnp.float32),
            pltpu.VMEM((R // TILE, C, TILE), jnp.bfloat16),
            pltpu.VMEM((2, R, 3 * C), jnp.bfloat16),
            pltpu.VMEM((TILE, 128), jnp.float32),
        ],
        compiler_params=pltpu.CompilerParams(vmem_limit_bytes=56 * 1024 * 1024),
        cost_estimate=pl.CostEstimate(
            flops=30_000_000_000, bytes_accessed=20_000_000, transcendentals=0
        ),
        name="conv_backward",
    )(starts, idx, table, feat, weight)
    return in_grad, wgrad.reshape(27 * C, C)


AXES = ("gy", "gx_1", "gx_0")
TILE_AT = (0, 16, 32, 38)
HOLDS = ((0,), (1,), (2, 3))


def scatter_kernel(part, out, local, s_a, r_a, *rest):
    s_b, r_b, s_c, r_c, s_d, r_d = (rest[3 * i : 3 * i + 3] for i in range(6))
    load_sem, a_sem, b_sem, c_sem, d_sem = rest[18:]
    pos = [lax.axis_index(a) for a in AXES]
    core = lax.axis_index("gx_2")
    z = pos[2]

    def around(i):
        return lax.rem(z + 1 + i, 4)

    loads = []
    for i in range(4):
        rows = pl.ds(pl.multiple_of(around(i) * 1728, 64), 1728)
        loads.append(pltpu.make_async_copy(part.at[rows, :], local.at[i], load_sem.at[i]))
        loads[-1].start()

    barrier = pltpu.get_barrier_semaphore()
    pl.semaphore_signal(barrier, 1, device_id={"gx_2": 1 - core}, device_id_type=MESH)
    for axis, at in zip(AXES, pos):
        for d in range(1, 4):
            peer = {axis: lax.rem(at + d, 4)}
            pl.semaphore_signal(barrier, 1, device_id=peer, device_id_type=MESH)

    def block(i, y, x, side, t):
        skip = (x * 54 + TILE_AT[t]) % 8
        base = (y * 2 + side) * 216 + x * 54 + TILE_AT[t] - skip
        rows = local[i, pl.ds(pl.multiple_of(base, 8), 24 if skip else 16), :]
        return rows[skip : skip + 16]

    sends = []

    def send(src, dst, sems, at, device):
        copy = pltpu.make_async_remote_copy(
            src_ref=src,
            dst_ref=dst,
            send_sem=sems.at[(0,) + at],
            recv_sem=sems.at[(1,) + at],
            device_id=device,
            device_id_type=MESH,
        )
        copy.start()
        sends.append(copy)
        return copy

    first = []
    for i in range(4):
        loads[i].wait()

        @pl.loop(0, 4)
        def _(y):
            for x in range(4):
                for t in range(4):
                    mine = block(i, y, x, 1 - core, t)
                    s_a[i, y * 4 + x, t] = mine.astype(jnp.bfloat16)

        if i == 0:
            pl.semaphore_wait(barrier, 10)
        first.append(send(s_a.at[i], r_a.at[i], a_sem, (i,), {"gx_2": 1 - core}))

    def spread(p, stage, sems, src, dst):
        axis = (p + stage) % 3
        return [
            send(
                src.at[lax.rem(pos[axis] + d, 4)],
                dst.at[d - 1],
                sems,
                (p, d - 1),
                {AXES[axis]: lax.rem(pos[axis] + d, 4)},
            )
            for d in range(1, 4)
        ]

    second = [None, None, []]
    for i in range(4):
        first[i].wait_recv()
        z_of = around(i)

        @pl.loop(0, 4)
        def _(y):
            for x in range(4):
                for t in range(4):
                    both = block(i, y, x, core, t) + r_a[i, y * 4 + x, t].astype(jnp.float32)
                    both = both.astype(jnp.bfloat16)
                    if t == 0:
                        s_b[0][x, y * 4 + z_of, 0] = both
                    elif t == 1:
                        s_b[1][y, z_of * 4 + x, 0] = both
                    else:
                        s_b[2][z_of, x * 4 + y, t - 2] = both

        if i < 3:
            second[2].append(
                send(s_b[2].at[z_of], r_b[2].at[i], b_sem, (2, i), {"gx_0": z_of})
            )
    for p in range(2):
        second[p] = spread(p, 0, b_sem, s_b[p], r_b[p])

    def total(own, came, at):
        kind = jnp.float32
        return (own[at].astype(kind) + came[(0,) + at[1:]].astype(kind)) + (
            came[(1,) + at[1:]].astype(kind) + came[(2,) + at[1:]].astype(kind)
        )

    third = []
    for p in range(3):
        for copy in second[p]:
            copy.wait_recv()
        me = pos[p]

        @pl.loop(0, 16)
        def _(j):
            for t in range(len(HOLDS[p])):
                s_c[p][j // 4, j % 4, t] = total(s_b[p], r_b[p], (me, j, t)).astype(jnp.bfloat16)

        third.append(spread(p, 1, c_sem, s_c[p], r_c[p]))

    fourth = []
    for p in range(3):
        for copy in third[p]:
            copy.wait_recv()
        me = pos[(p + 1) % 3]

        @pl.loop(0, 4)
        def _(j):
            for t in range(len(HOLDS[p])):
                s_d[p][j, t] = total(s_c[p], r_c[p], (me, j, t))

        fourth.append(spread(p, 2, d_sem, s_d[p], r_d[p]))

    for p in range(3):
        for copy in fourth[p]:
            copy.wait_recv()
        me = pos[(p + 2) % 3]
        for t, which in enumerate(HOLDS[p]):
            out[TILE_AT[which] : TILE_AT[which] + 16, :] = total(s_d[p], r_d[p], (me, t))

    for copy in sends:
        copy.wait_send()


def scatter_sum(part):
    def stage(lead, kind):
        return [pltpu.VMEM(lead + (len(h), 16, C), kind) for h in HOLDS]

    half, full = jnp.bfloat16, jnp.float32
    return pl.pallas_call(
        scatter_kernel,
        out_shape=jax.ShapeDtypeStruct((54, C), jnp.float32),
        in_specs=[pl.BlockSpec(memory_space=pl.ANY)],
        out_specs=pl.BlockSpec(memory_space=pltpu.VMEM),
        scratch_shapes=[
            pltpu.VMEM((4, 1728, C), jnp.float32),
            pltpu.VMEM((4, 16, 4, 16, C), jnp.bfloat16),
            pltpu.VMEM((4, 16, 4, 16, C), jnp.bfloat16),
            *stage((4, 16), half),
            *stage((3, 16), half),
            *stage((4, 4), half),
            *stage((3, 4), half),
            *stage((4,), full),
            *stage((3,), full),
            pltpu.SemaphoreType.DMA((4,)),
            pltpu.SemaphoreType.DMA((2, 4)),
            pltpu.SemaphoreType.DMA((2, 3, 3)),
            pltpu.SemaphoreType.DMA((2, 3, 3)),
            pltpu.SemaphoreType.DMA((2, 3, 3)),
        ],
        compiler_params=pltpu.CompilerParams(
            collective_id=1, has_side_effects=True, vmem_limit_bytes=40 * 1024 * 1024
        ),
        cost_estimate=pl.CostEstimate(flops=10_000_000, bytes_accessed=7_000_000, transcendentals=0),
        name="scatter_sum",
    )(part)


HB = 704
ROWS = NROW + WIN


def seg(b):
    return R + b * HB


def front_kernel(
    count, pre, cot, gamma, beta, links, border,
    table, columns, starts, gamma_grad, beta_grad,
    grad, pick, near, far, near_sem, far_sem, halo_sem,
):
    f32 = jnp.float32
    z, y, core, x = (lax.axis_index(a) for a in GX_GY)
    slab = (z * 4 + y) * 2 + core
    me_near, me_far = x * 2 + core, z * 4 + y

    def near_id(p):
        return {"gy": p // 2, "gx_2": lax.rem(p, 2)}

    def far_id(p):
        return {"gx_0": p // 4, "gx_1": lax.rem(p, 4)}

    def slab_id(s):
        return {"gx_0": s // 8, "gx_1": lax.rem(s // 2, 4), "gx_2": lax.rem(s, 2)}

    barrier = pltpu.get_barrier_semaphore()
    for d in range(1, 8):
        pl.semaphore_signal(
            barrier, 1, device_id=near_id(lax.rem(me_near + d, 8)), device_id_type=MESH
        )
    for d in range(1, 16):
        pl.semaphore_signal(
            barrier, 1, device_id=far_id(lax.rem(me_far + d, 16)), device_id_type=MESH
        )
    up, down = (core == 1) & (slab < 31), (core == 0) & (slab > 0)

    @pl.when(up)
    def _():
        pl.semaphore_signal(barrier, 1, device_id=slab_id(slab + 1), device_id_type=MESH)

    @pl.when(down)
    def _():
        pl.semaphore_signal(barrier, 1, device_id=slab_id(slab - 1), device_id_type=MESH)

    live_rows = count[0, 0]
    block = 128

    def live_at(t):
        row = lax.broadcasted_iota(jnp.int32, (block, C), 0) + t * block
        return row < live_rows

    def rows_at(t):
        return pl.ds(pl.multiple_of(t * block, block), block)

    def fold(a):
        return jnp.sum(a.reshape(block // 8, 8, C), axis=0)

    def first_sums(t, sums):
        zval = pre[rows_at(t), :].astype(f32)
        zlive = jnp.where(live_at(t), zval, 0.0)
        return sums[0] + fold(zlive), sums[1] + fold(zlive * zval)

    zero = jnp.zeros((8, C), f32)
    line = lax.broadcasted_iota(jnp.int32, (8, C), 0)

    def stacked(a, b, c):
        a, b = jnp.sum(a, axis=0, keepdims=True), jnp.sum(b, axis=0, keepdims=True)
        return jnp.where(line == 0, a, jnp.where(line == 1, b, jnp.where(line == 2, c, 0.0)))

    def exchange(slots, me, size, sems, turn, ids):
        copies = []
        for d in range(1, size):
            copies.append(
                pltpu.make_async_remote_copy(
                    src_ref=slots.at[turn, me],
                    dst_ref=slots.at[turn, me],
                    send_sem=sems.at[turn, 0, d - 1],
                    recv_sem=sems.at[turn, 1, d - 1],
                    device_id=ids(lax.rem(me + d, size)),
                    device_id_type=MESH,
                )
            )
            copies[-1].start()
        return copies

    def add_up(slots, size, turn, copies):
        for copy in copies:
            copy.wait_recv()
        total = slots[turn, 0]
        for i in range(1, size):
            total = total + slots[turn, i]
        return total

    def all_sum(turn, value, meanwhile):
        near[turn, me_near] = value
        one = exchange(near, me_near, 8, near_sem, turn, near_id)
        meanwhile()
        far[turn, me_far] = add_up(near, 8, turn, one)
        two = exchange(far, me_far, 16, far_sem, turn, far_id)
        total = add_up(far, 16, turn, two)
        for copy in one + two:
            copy.wait_send()
        return total

    def plan():
        lane = lax.broadcasted_iota(jnp.int32, (1, 128), 1)
        third = lax.rem(lane, 3)

        @pl.loop(0, R // SUB)
        def _(j):
            at = pl.ds(pl.multiple_of(j * SUB, SUB), SUB)
            idx = links[:, at]
            idx = jnp.where(idx < NROW, idx, jnp.int32(FAR)).astype(f32)
            idx = jnp.concatenate([idx, jnp.full((101, SUB), FAR, f32)], axis=0).T
            columns[at, :] = idx
            begin = []
            for w in range(3):
                low = jnp.min(idx, axis=0, keepdims=True)
                low = jnp.minimum(low, jnp.minimum(pltpu.roll(low, 127, 1), pltpu.roll(low, 126, 1)))
                low = jnp.where(
                    third == 0,
                    low,
                    jnp.where(third == 1, pltpu.roll(low, 1, 1), pltpu.roll(low, 2, 1)),
                )
                start = jnp.where(low < NROW, jnp.floor(low * 0.0625) * 16.0, FAR)
                idx = jnp.where(idx >= start + WIN, idx, FAR)
                begin.append(jnp.minimum(start, float(NROW)) if w < 2 else start)
            begin = [jnp.broadcast_to(b, (8, 128)) for b in begin]
            row = lax.broadcasted_iota(jnp.int32, (8, 128), 0)
            begin = jnp.where(row == 0, begin[0], jnp.where(row == 1, begin[1], begin[2]))
            starts[pl.ds(pl.multiple_of(j * 8, 8), 8), :] = begin.astype(jnp.int32)

    def choose():
        @pl.loop(0, 11)
        def _(t):
            at = pl.ds(pl.multiple_of(t * 64, 64), 64)
            wanted = jnp.broadcast_to(border[at, :], (64, R))
            row = lax.broadcasted_iota(jnp.int32, (64, R), 1)
            pick[at, :] = jnp.where(wanted == row, 1.0, 0.0).astype(jnp.bfloat16)

        def clear(at, size):
            table[at : at + size, :] = jnp.zeros((size, C), jnp.bfloat16)

        clear(NROW, WIN)

        @pl.when(slab == 0)
        def _():
            for b in (0, 1, 2):
                clear(seg(b), HB)

        @pl.when(slab == 31)
        def _():
            for b in (6, 7, 8):
                clear(seg(b), WIN)

        for b in (6, 7, 8):
            clear(seg(b) + WIN, HB - WIN)

        for edge, db in ((0, 0), (3, 2)):
            @pl.when(x == edge)
            def _():
                clear(seg(3 + db), HB)

                @pl.when(slab > 0)
                def _():
                    clear(seg(db), HB)

                @pl.when(slab < 31)
                def _():
                    clear(seg(6 + db), WIN)

    sum_z, sum_sq = lax.fori_loop(0, R // block, first_sums, (zero, zero))
    extra = jnp.where(up | down, 1, 0)
    pl.semaphore_wait(barrier, 22 + extra)
    whole = all_sum(0, stacked(sum_z, sum_sq, live_rows.astype(f32)), plan)
    amount = whole[2:3]
    mean = whole[0:1] / amount
    var = whole[1:2] / amount - mean * mean
    rstd = lax.rsqrt(var + 1e-05)
    gain, shift = gamma[...], beta[...]

    def second_sums(t, sums):
        zhat = (pre[rows_at(t), :].astype(f32) - mean) * rstd
        act = gain * zhat + shift
        sig = jax.nn.sigmoid(act)
        g = cot[rows_at(t), :].astype(f32) * sig * (1.0 + act * (1.0 - sig))
        g = jnp.where(live_at(t), g, 0.0)
        grad[rows_at(t), :] = g
        return sums[0] + fold(g), sums[1] + fold(g * zhat)

    sum_g, sum_gz = lax.fori_loop(0, R // block, second_sums, (zero, zero))
    whole = all_sum(1, stacked(sum_g, sum_gz, 0.0), choose)
    beta_grad[...] = whole[0:1]
    gamma_grad[...] = whole[1:2]
    scale = gain * rstd
    part_g, part_gz = whole[0:1] / amount, whole[1:2] / amount

    @pl.loop(0, R // block)
    def _(t):
        zhat = (pre[rows_at(t), :].astype(f32) - mean) * rstd
        dz = scale * (grad[rows_at(t), :] - part_g - zhat * part_gz)
        table[rows_at(t), :] = jnp.where(live_at(t), dz, 0.0).astype(jnp.bfloat16)

    @pl.loop(0, 4)
    def _(t):
        at = pl.multiple_of(t * 176, 16)
        rows = dot(pick[pl.ds(at, 176), :], table[0:R, :], ((1,), (0,)))
        table[pl.ds(pl.multiple_of(seg(4) + at, 16), 176), :] = rows.astype(jnp.bfloat16)

    def hop(source, target, size, device):
        return pltpu.make_async_remote_copy(
            src_ref=table.at[pl.ds(seg(source), size), :],
            dst_ref=table.at[pl.ds(seg(target), size), :],
            send_sem=halo_sem.at[0, target],
            recv_sem=halo_sem.at[1, target],
            device_id=device,
            device_id_type=MESH,
        )

    def right():
        return hop(4, 3, HB, {"gy": x + 1})

    def left():
        return hop(4, 5, HB, {"gy": x - 1})

    def ahead(db):
        return hop(3 + db, db, HB, slab_id(slab + 1))

    def behind(db):
        return hop(3 + db, 6 + db, WIN, slab_id(slab - 1))

    has_right, has_left, has_next, has_last = x < 3, x > 0, slab < 31, slab > 0

    def when(cond, act):
        @pl.when(cond)
        def _():
            act()

    when(has_right, lambda: right().start())
    when(has_left, lambda: left().start())
    when(has_next, lambda: ahead(1).start())
    when(has_last, lambda: behind(1).start())
    for db, there, came in ((0, has_left, right), (2, has_right, left)):
        when(there, lambda: came().wait_recv())
        when(there & has_next, lambda: ahead(db).start())
        when(there & has_last, lambda: behind(db).start())
    for db, there in ((1, True), (0, has_left), (2, has_right)):
        when(has_last & there, lambda: ahead(db).wait_recv())
        when(has_next & there, lambda: behind(db).wait_recv())
    when(has_right, lambda: right().wait_send())
    when(has_left, lambda: left().wait_send())
    for db, there in ((1, True), (0, has_left), (2, has_right)):
        when(has_next & there, lambda: ahead(db).wait_send())
        when(has_last & there, lambda: behind(db).wait_send())


def front(counts, pre_norm, out_grad, gamma, beta, links, border):
    vmem = pl.BlockSpec(memory_space=pltpu.VMEM)
    return pl.pallas_call(
        front_kernel,
        out_shape=(
            jax.ShapeDtypeStruct((ROWS, C), jnp.bfloat16),
            jax.ShapeDtypeStruct((R, 128), jnp.float32),
            jax.ShapeDtypeStruct((R // SUB * 8, 128), jnp.int32),
            jax.ShapeDtypeStruct((1, C), jnp.float32),
            jax.ShapeDtypeStruct((1, C), jnp.float32),
        ),
        in_specs=[pl.BlockSpec(memory_space=pltpu.SMEM)] + [vmem] * 6,
        out_specs=(vmem,) * 5,
        scratch_shapes=[
            pltpu.VMEM((R, C), jnp.float32),
            pltpu.VMEM((HB, R), jnp.bfloat16),
            pltpu.VMEM((2, 8, 8, C), jnp.float32),
            pltpu.VMEM((2, 16, 8, C), jnp.float32),
            pltpu.SemaphoreType.DMA((2, 2, 7)),
            pltpu.SemaphoreType.DMA((2, 2, 15)),
            pltpu.SemaphoreType.DMA((2, 9)),
        ],
        compiler_params=pltpu.CompilerParams(
            collective_id=0, has_side_effects=True, vmem_limit_bytes=40 * 1024 * 1024
        ),
        cost_estimate=pl.CostEstimate(
            flops=1_000_000_000, bytes_accessed=10_000_000, transcendentals=1_000_000
        ),
        name="front",
    )(counts, pre_norm, out_grad, gamma, beta, links, border)


def body(features, pre_norm, out_grad, weight, gamma, beta, neighbors, boundary, counts):
    table, columns, starts, gamma_grad, beta_grad = front(
        counts,
        pre_norm[0, 0],
        out_grad[0, 0],
        gamma[None],
        beta[None],
        neighbors[0, 0],
        boundary[0, 0][:, None],
    )
    in_grad, local_wgrad = convolve(starts, columns, table, features[0, 0], weight)
    weight_grad = scatter_sum(local_wgrad)
    return (in_grad[None, None], weight_grad, gamma_grad[0], beta_grad[0])


def solution(mesh):
    torus = Mesh(mesh.devices.reshape(4, 4, 2, mesh.shape["gy"]), ("gx_0", "gx_1", "gx_2", "gy"))
    return jax.shard_map(
        body,
        mesh=torus,
        in_specs=(
            P(GX, "gy", None, None),
            P(GX, "gy", None, None),
            P(GX, "gy", None, None),
            P(),
            P(),
            P(),
            P(GX, "gy", None, None),
            P(GX, "gy", None),
            P(GX, "gy"),
        ),
        out_specs=(P(GX, "gy", None, None), P(GX_GY, None), P(), P()),
        check_vma=False,
    )
```

```python
import jax
import jax.numpy as jnp
from jax import lax
from jax.experimental import pallas as pl
from jax.experimental.pallas import tpu as pltpu
from jax.sharding import Mesh
from jax.sharding import PartitionSpec as P

GX_GY = ("gx_0", "gx_1", "gx_2", "gy")
GX = ("gx_0", "gx_1", "gx_2")
MESH = pl.DeviceIdType.MESH


C = 256
R = 2048
SUB = 128
WIN = 256
NROW = 8384
FAR = 1.0e6


def dot(a, b, dims):
    return lax.dot_general(a, b, (dims, ((), ())), preferred_element_type=jnp.float32)


def one_hot(columns, start):
    lanes = lax.broadcasted_iota(jnp.int32, (SUB, WIN), 1).astype(jnp.float32)
    place = columns - start.astype(jnp.float32)
    return jnp.where(place == lanes, 1.0, 0.0).astype(jnp.bfloat16)

def conv_kernel(starts, idx, table, feat, weight, in_grad, wgrad, acc, feat_t, picked):
    step = pl.program_id(0)
    lane0 = 24 - 3 * step

    @pl.when(step == 0)
    def _():
        acc[...] = jnp.zeros_like(acc)

        @pl.loop(0, 8)
        def _(t):
            rows = pl.ds(pl.multiple_of(t * 256, 256), 256)
            feat_t[:, rows] = feat[rows, :].T

    def columns_at(row):
        columns = pltpu.roll(idx[pl.ds(row, SUB), :], 128 - lane0, 1)
        return columns

    def window(columns, start):
        hot = [
            one_hot(jnp.broadcast_to(columns[:, 2 - i : 3 - i], (SUB, WIN)), start)
            for i in range(3)
        ]
        return jnp.concatenate(hot, axis=0)

    def gather(j):
        row = j * SUB
        columns = columns_at(row)
        s = [pl.multiple_of(starts[j * 8 + w, lane0], 16) for w in range(2)]
        hots = [window(columns, a) for a in s]
        tabs = [table[pl.ds(a, WIN), :] for a in s]
        total = dot(jnp.concatenate(hots, axis=1), jnp.concatenate(tabs, axis=0), ((1,), (0,)))
        total = total.astype(jnp.bfloat16)
        for i in range(3):
            picked[pl.ds(row, SUB), i * C : (i + 1) * C] = total[i * SUB : (i + 1) * SUB]

    def gather_rest(j):
        row = j * SUB

        def more(start):
            columns = columns_at(row)
            start = pl.multiple_of(start, 16)
            part = dot(window(columns, start), table[pl.ds(start, WIN), :], ((1,), (0,)))
            part = part.astype(jnp.bfloat16)
            for i in range(3):
                picked[pl.ds(row, SUB), i * C : (i + 1) * C] += part[i * SUB : (i + 1) * SUB]
            lane = lax.broadcasted_iota(jnp.int32, (SUB, 128), 1)
            ahead = (lane < 3) & (columns >= (start + WIN).astype(jnp.float32))
            low = jnp.min(jnp.where(ahead, columns, FAR)).astype(jnp.int32)
            return jnp.where(low < NROW, low // 16 * 16, jnp.int32(FAR))

        lax.while_loop(lambda start: start < NROW, more, starts[j * 8 + 2, lane0])

    for j in range(R // SUB):
        gather(j)
    for j in range(R // SUB):
        gather_rest(j)
    for i in range(3):
        wgrad[i] = dot(feat_t[...], picked[:, i * C : (i + 1) * C], ((1,), (0,)))
    turned = jnp.concatenate([weight[i].T for i in range(3)], axis=0)
    acc[...] += dot(picked[...], turned, ((1,), (0,)))

    @pl.when(step == 8)
    def _():
        in_grad[...] = acc[...].astype(jnp.bfloat16)


def convolve(starts, idx, table, feat, weight):
    whole = pl.BlockSpec(memory_space=pltpu.VMEM)
    in_grad, wgrad = pl.pallas_call(
        conv_kernel,
        grid=(9,),
        out_shape=(
            jax.ShapeDtypeStruct((R, C), jnp.bfloat16),
            jax.ShapeDtypeStruct((27, C, C), jnp.float32),
        ),
        in_specs=[
            pl.BlockSpec(memory_space=pltpu.SMEM),
            whole,
            whole,
            whole,
            pl.BlockSpec((3, C, C), lambda g: (g, 0, 0)),
        ],
        out_specs=(whole, pl.BlockSpec((3, C, C), lambda g: (g, 0, 0))),
        scratch_shapes=[
            pltpu.VMEM((R, C), jnp.float32),
            pltpu.VMEM((C, R), jnp.bfloat16),
            pltpu.VMEM((R, 3 * C), jnp.bfloat16),
        ],
        compiler_params=pltpu.CompilerParams(vmem_limit_bytes=28 * 1024 * 1024),
        cost_estimate=pl.CostEstimate(
            flops=30_000_000_000, bytes_accessed=20_000_000, transcendentals=0
        ),
        name="conv_backward",
    )(starts, idx, table, feat, weight)
    return in_grad, wgrad.reshape(27 * C, C)


AXES = ("gy", "gx_1", "gx_0")
TILE_AT = (0, 16, 32, 38)
HOLDS = ((0,), (1,), (2, 3))


def scatter_kernel(part, out, local, s_a, r_a, *rest):
    s_b, r_b, s_c, r_c, s_d, r_d = (rest[3 * i : 3 * i + 3] for i in range(6))
    load_sem, a_sem, b_sem, c_sem, d_sem = rest[18:]
    pos = [lax.axis_index(a) for a in AXES]
    core = lax.axis_index("gx_2")
    z = pos[2]

    def around(i):
        return lax.rem(z + 1 + i, 4)

    loads = []
    for i in range(4):
        rows = pl.ds(pl.multiple_of(around(i) * 1728, 64), 1728)
        loads.append(pltpu.make_async_copy(part.at[rows, :], local.at[i], load_sem.at[i]))
        loads[-1].start()

    barrier = pltpu.get_barrier_semaphore()
    pl.semaphore_signal(barrier, 1, device_id={"gx_2": 1 - core}, device_id_type=MESH)
    for axis, at in zip(AXES, pos):
        for d in range(1, 4):
            peer = {axis: lax.rem(at + d, 4)}
            pl.semaphore_signal(barrier, 1, device_id=peer, device_id_type=MESH)

    def block(i, y, x, side, t):
        skip = (x * 54 + TILE_AT[t]) % 8
        base = (y * 2 + side) * 216 + x * 54 + TILE_AT[t] - skip
        rows = local[i, pl.ds(pl.multiple_of(base, 8), 24 if skip else 16), :]
        return rows[skip : skip + 16]

    sends = []

    def send(src, dst, sems, at, device):
        copy = pltpu.make_async_remote_copy(
            src_ref=src,
            dst_ref=dst,
            send_sem=sems.at[(0,) + at],
            recv_sem=sems.at[(1,) + at],
            device_id=device,
            device_id_type=MESH,
        )
        copy.start()
        sends.append(copy)
        return copy

    first = []
    for i in range(4):
        loads[i].wait()

        @pl.loop(0, 4)
        def _(y):
            for x in range(4):
                for t in range(4):
                    mine = block(i, y, x, 1 - core, t)
                    s_a[i, y * 4 + x, t] = mine.astype(jnp.bfloat16)

        if i == 0:
            pl.semaphore_wait(barrier, 10)
        first.append(send(s_a.at[i], r_a.at[i], a_sem, (i,), {"gx_2": 1 - core}))

    def spread(p, stage, sems, src, dst):
        axis = (p + stage) % 3
        return [
            send(
                src.at[lax.rem(pos[axis] + d, 4)],
                dst.at[d - 1],
                sems,
                (p, d - 1),
                {AXES[axis]: lax.rem(pos[axis] + d, 4)},
            )
            for d in range(1, 4)
        ]

    second = [None, None, []]
    for i in range(4):
        first[i].wait_recv()
        z_of = around(i)

        @pl.loop(0, 4)
        def _(y):
            for x in range(4):
                for t in range(4):
                    both = block(i, y, x, core, t) + r_a[i, y * 4 + x, t].astype(jnp.float32)
                    both = both.astype(jnp.bfloat16)
                    if t == 0:
                        s_b[0][x, y * 4 + z_of, 0] = both
                    elif t == 1:
                        s_b[1][y, z_of * 4 + x, 0] = both
                    else:
                        s_b[2][z_of, x * 4 + y, t - 2] = both

        if i < 3:
            second[2].append(
                send(s_b[2].at[z_of], r_b[2].at[i], b_sem, (2, i), {"gx_0": z_of})
            )
    for p in range(2):
        second[p] = spread(p, 0, b_sem, s_b[p], r_b[p])

    def total(own, came, at):
        kind = jnp.float32
        return (own[at].astype(kind) + came[(0,) + at[1:]].astype(kind)) + (
            came[(1,) + at[1:]].astype(kind) + came[(2,) + at[1:]].astype(kind)
        )

    third = []
    for p in range(3):
        for copy in second[p]:
            copy.wait_recv()
        me = pos[p]

        @pl.loop(0, 16)
        def _(j):
            for t in range(len(HOLDS[p])):
                s_c[p][j // 4, j % 4, t] = total(s_b[p], r_b[p], (me, j, t)).astype(jnp.bfloat16)

        third.append(spread(p, 1, c_sem, s_c[p], r_c[p]))

    fourth = []
    for p in range(3):
        for copy in third[p]:
            copy.wait_recv()
        me = pos[(p + 1) % 3]

        @pl.loop(0, 4)
        def _(j):
            for t in range(len(HOLDS[p])):
                s_d[p][j, t] = total(s_c[p], r_c[p], (me, j, t))

        fourth.append(spread(p, 2, d_sem, s_d[p], r_d[p]))

    for p in range(3):
        for copy in fourth[p]:
            copy.wait_recv()
        me = pos[(p + 2) % 3]
        for t, which in enumerate(HOLDS[p]):
            out[TILE_AT[which] : TILE_AT[which] + 16, :] = total(s_d[p], r_d[p], (me, t))

    for copy in sends:
        copy.wait_send()


def scatter_sum(part):
    def stage(lead, kind):
        return [pltpu.VMEM(lead + (len(h), 16, C), kind) for h in HOLDS]

    half, full = jnp.bfloat16, jnp.float32
    return pl.pallas_call(
        scatter_kernel,
        out_shape=jax.ShapeDtypeStruct((54, C), jnp.float32),
        in_specs=[pl.BlockSpec(memory_space=pl.ANY)],
        out_specs=pl.BlockSpec(memory_space=pltpu.VMEM),
        scratch_shapes=[
            pltpu.VMEM((4, 1728, C), jnp.float32),
            pltpu.VMEM((4, 16, 4, 16, C), jnp.bfloat16),
            pltpu.VMEM((4, 16, 4, 16, C), jnp.bfloat16),
            *stage((4, 16), half),
            *stage((3, 16), half),
            *stage((4, 4), half),
            *stage((3, 4), half),
            *stage((4,), full),
            *stage((3,), full),
            pltpu.SemaphoreType.DMA((4,)),
            pltpu.SemaphoreType.DMA((2, 4)),
            pltpu.SemaphoreType.DMA((2, 3, 3)),
            pltpu.SemaphoreType.DMA((2, 3, 3)),
            pltpu.SemaphoreType.DMA((2, 3, 3)),
        ],
        compiler_params=pltpu.CompilerParams(
            collective_id=1, has_side_effects=True, vmem_limit_bytes=24 * 1024 * 1024
        ),
        cost_estimate=pl.CostEstimate(flops=10_000_000, bytes_accessed=7_000_000, transcendentals=0),
        name="scatter_sum",
    )(part)


HB = 704
ROWS = NROW + WIN


def seg(b):
    return R + b * HB


def front_kernel(
    count, pre, cot, gamma, beta, links, border,
    table, columns, starts, gamma_grad, beta_grad,
    grad, pick, near, far, near_sem, far_sem, halo_sem,
):
    f32 = jnp.float32
    z, y, core, x = (lax.axis_index(a) for a in GX_GY)
    slab = (z * 4 + y) * 2 + core
    me_near, me_far = x * 2 + core, z * 4 + y

    def near_id(p):
        return {"gy": p // 2, "gx_2": lax.rem(p, 2)}

    def far_id(p):
        return {"gx_0": p // 4, "gx_1": lax.rem(p, 4)}

    def slab_id(s):
        return {"gx_0": s // 8, "gx_1": lax.rem(s // 2, 4), "gx_2": lax.rem(s, 2)}

    barrier = pltpu.get_barrier_semaphore()
    for d in range(1, 8):
        pl.semaphore_signal(
            barrier, 1, device_id=near_id(lax.rem(me_near + d, 8)), device_id_type=MESH
        )
    for d in range(1, 16):
        pl.semaphore_signal(
            barrier, 1, device_id=far_id(lax.rem(me_far + d, 16)), device_id_type=MESH
        )
    up, down = (core == 1) & (slab < 31), (core == 0) & (slab > 0)

    @pl.when(up)
    def _():
        pl.semaphore_signal(barrier, 1, device_id=slab_id(slab + 1), device_id_type=MESH)

    @pl.when(down)
    def _():
        pl.semaphore_signal(barrier, 1, device_id=slab_id(slab - 1), device_id_type=MESH)

    live_rows = count[0, 0]
    block = 128

    def live_at(t):
        row = lax.broadcasted_iota(jnp.int32, (block, C), 0) + t * block
        return row < live_rows

    def rows_at(t):
        return pl.ds(pl.multiple_of(t * block, block), block)

    def fold(a):
        return jnp.sum(a.reshape(block // 8, 8, C), axis=0)

    def first_sums(t, sums):
        zval = pre[rows_at(t), :].astype(f32)
        zlive = jnp.where(live_at(t), zval, 0.0)
        return sums[0] + fold(zlive), sums[1] + fold(zlive * zval)

    zero = jnp.zeros((8, C), f32)
    line = lax.broadcasted_iota(jnp.int32, (8, C), 0)

    def stacked(a, b, c):
        a, b = jnp.sum(a, axis=0, keepdims=True), jnp.sum(b, axis=0, keepdims=True)
        return jnp.where(line == 0, a, jnp.where(line == 1, b, jnp.where(line == 2, c, 0.0)))

    def exchange(slots, me, size, sems, turn, ids):
        copies = []
        for d in range(1, size):
            copies.append(
                pltpu.make_async_remote_copy(
                    src_ref=slots.at[turn, me],
                    dst_ref=slots.at[turn, me],
                    send_sem=sems.at[turn, 0, d - 1],
                    recv_sem=sems.at[turn, 1, d - 1],
                    device_id=ids(lax.rem(me + d, size)),
                    device_id_type=MESH,
                )
            )
            copies[-1].start()
        return copies

    def add_up(slots, size, turn, copies):
        for copy in copies:
            copy.wait_recv()
        total = slots[turn, 0]
        for i in range(1, size):
            total = total + slots[turn, i]
        return total

    def all_sum(turn, value, meanwhile):
        near[turn, me_near] = value
        one = exchange(near, me_near, 8, near_sem, turn, near_id)
        meanwhile()
        far[turn, me_far] = add_up(near, 8, turn, one)
        two = exchange(far, me_far, 16, far_sem, turn, far_id)
        total = add_up(far, 16, turn, two)
        for copy in one + two:
            copy.wait_send()
        return total

    def plan():
        lane = lax.broadcasted_iota(jnp.int32, (1, 128), 1)
        third = lax.rem(lane, 3)

        @pl.loop(0, R // SUB)
        def _(j):
            at = pl.ds(pl.multiple_of(j * SUB, SUB), SUB)
            idx = links[:, at]
            idx = jnp.where(idx < NROW, idx, jnp.int32(FAR)).astype(f32)
            idx = jnp.concatenate([idx, jnp.full((101, SUB), FAR, f32)], axis=0).T
            columns[at, :] = idx
            begin = []
            for w in range(3):
                low = jnp.min(idx, axis=0, keepdims=True)
                low = jnp.minimum(low, jnp.minimum(pltpu.roll(low, 127, 1), pltpu.roll(low, 126, 1)))
                low = jnp.where(
                    third == 0,
                    low,
                    jnp.where(third == 1, pltpu.roll(low, 1, 1), pltpu.roll(low, 2, 1)),
                )
                start = jnp.where(low < NROW, jnp.floor(low * 0.0625) * 16.0, FAR)
                idx = jnp.where(idx >= start + WIN, idx, FAR)
                begin.append(jnp.minimum(start, float(NROW)) if w < 2 else start)
            begin = [jnp.broadcast_to(b, (8, 128)) for b in begin]
            row = lax.broadcasted_iota(jnp.int32, (8, 128), 0)
            begin = jnp.where(row == 0, begin[0], jnp.where(row == 1, begin[1], begin[2]))
            starts[pl.ds(pl.multiple_of(j * 8, 8), 8), :] = begin.astype(jnp.int32)

    def choose():
        @pl.loop(0, 11)
        def _(t):
            at = pl.ds(pl.multiple_of(t * 64, 64), 64)
            wanted = jnp.broadcast_to(border[at, :], (64, R))
            row = lax.broadcasted_iota(jnp.int32, (64, R), 1)
            pick[at, :] = jnp.where(wanted == row, 1.0, 0.0).astype(jnp.bfloat16)

        def clear(at, size):
            table[at : at + size, :] = jnp.zeros((size, C), jnp.bfloat16)

        clear(NROW, WIN)

        @pl.when(slab == 0)
        def _():
            for b in (0, 1, 2):
                clear(seg(b), HB)

        @pl.when(slab == 31)
        def _():
            for b in (6, 7, 8):
                clear(seg(b), WIN)

        for b in (6, 7, 8):
            clear(seg(b) + WIN, HB - WIN)

        for edge, db in ((0, 0), (3, 2)):
            @pl.when(x == edge)
            def _():
                clear(seg(3 + db), HB)

                @pl.when(slab > 0)
                def _():
                    clear(seg(db), HB)

                @pl.when(slab < 31)
                def _():
                    clear(seg(6 + db), WIN)

    sum_z, sum_sq = lax.fori_loop(0, R // block, first_sums, (zero, zero))
    extra = jnp.where(up | down, 1, 0)
    pl.semaphore_wait(barrier, 22 + extra)
    whole = all_sum(0, stacked(sum_z, sum_sq, live_rows.astype(f32)), plan)
    amount = whole[2:3]
    mean = whole[0:1] / amount
    var = whole[1:2] / amount - mean * mean
    rstd = lax.rsqrt(var + 1e-05)
    gain, shift = gamma[...], beta[...]

    def second_sums(t, sums):
        zhat = (pre[rows_at(t), :].astype(f32) - mean) * rstd
        act = gain * zhat + shift
        sig = jax.nn.sigmoid(act)
        g = cot[rows_at(t), :].astype(f32) * sig * (1.0 + act * (1.0 - sig))
        g = jnp.where(live_at(t), g, 0.0)
        grad[rows_at(t), :] = g
        return sums[0] + fold(g), sums[1] + fold(g * zhat)

    sum_g, sum_gz = lax.fori_loop(0, R // block, second_sums, (zero, zero))
    whole = all_sum(1, stacked(sum_g, sum_gz, 0.0), choose)
    beta_grad[...] = whole[0:1]
    gamma_grad[...] = whole[1:2]
    scale = gain * rstd
    part_g, part_gz = whole[0:1] / amount, whole[1:2] / amount

    @pl.loop(0, R // block)
    def _(t):
        zhat = (pre[rows_at(t), :].astype(f32) - mean) * rstd
        dz = scale * (grad[rows_at(t), :] - part_g - zhat * part_gz)
        table[rows_at(t), :] = jnp.where(live_at(t), dz, 0.0).astype(jnp.bfloat16)

    @pl.loop(0, 4)
    def _(t):
        at = pl.multiple_of(t * 176, 16)
        rows = dot(pick[pl.ds(at, 176), :], table[0:R, :], ((1,), (0,)))
        table[pl.ds(pl.multiple_of(seg(4) + at, 16), 176), :] = rows.astype(jnp.bfloat16)

    def hop(source, target, size, device):
        return pltpu.make_async_remote_copy(
            src_ref=table.at[pl.ds(seg(source), size), :],
            dst_ref=table.at[pl.ds(seg(target), size), :],
            send_sem=halo_sem.at[0, target],
            recv_sem=halo_sem.at[1, target],
            device_id=device,
            device_id_type=MESH,
        )

    def right():
        return hop(4, 3, HB, {"gy": x + 1})

    def left():
        return hop(4, 5, HB, {"gy": x - 1})

    def ahead(db):
        return hop(3 + db, db, HB, slab_id(slab + 1))

    def behind(db):
        return hop(3 + db, 6 + db, WIN, slab_id(slab - 1))

    has_right, has_left, has_next, has_last = x < 3, x > 0, slab < 31, slab > 0

    def when(cond, act):
        @pl.when(cond)
        def _():
            act()

    when(has_right, lambda: right().start())
    when(has_left, lambda: left().start())
    when(has_next, lambda: ahead(1).start())
    when(has_last, lambda: behind(1).start())
    for db, there, came in ((0, has_left, right), (2, has_right, left)):
        when(there, lambda: came().wait_recv())
        when(there & has_next, lambda: ahead(db).start())
        when(there & has_last, lambda: behind(db).start())
    for db, there in ((1, True), (0, has_left), (2, has_right)):
        when(has_last & there, lambda: ahead(db).wait_recv())
        when(has_next & there, lambda: behind(db).wait_recv())
    when(has_right, lambda: right().wait_send())
    when(has_left, lambda: left().wait_send())
    for db, there in ((1, True), (0, has_left), (2, has_right)):
        when(has_next & there, lambda: ahead(db).wait_send())
        when(has_last & there, lambda: behind(db).wait_send())


def front(counts, pre_norm, out_grad, gamma, beta, links, border):
    vmem = pl.BlockSpec(memory_space=pltpu.VMEM)
    return pl.pallas_call(
        front_kernel,
        out_shape=(
            jax.ShapeDtypeStruct((ROWS, C), jnp.bfloat16),
            jax.ShapeDtypeStruct((R, 128), jnp.float32),
            jax.ShapeDtypeStruct((R // SUB * 8, 128), jnp.int32),
            jax.ShapeDtypeStruct((1, C), jnp.float32),
            jax.ShapeDtypeStruct((1, C), jnp.float32),
        ),
        in_specs=[pl.BlockSpec(memory_space=pltpu.SMEM)] + [vmem] * 6,
        out_specs=(vmem,) * 5,
        scratch_shapes=[
            pltpu.VMEM((R, C), jnp.float32),
            pltpu.VMEM((HB, R), jnp.bfloat16),
            pltpu.VMEM((2, 8, 8, C), jnp.float32),
            pltpu.VMEM((2, 16, 8, C), jnp.float32),
            pltpu.SemaphoreType.DMA((2, 2, 7)),
            pltpu.SemaphoreType.DMA((2, 2, 15)),
            pltpu.SemaphoreType.DMA((2, 9)),
        ],
        compiler_params=pltpu.CompilerParams(
            collective_id=0, has_side_effects=True, vmem_limit_bytes=24 * 1024 * 1024
        ),
        cost_estimate=pl.CostEstimate(
            flops=1_000_000_000, bytes_accessed=10_000_000, transcendentals=1_000_000
        ),
        name="front",
    )(counts, pre_norm, out_grad, gamma, beta, links, border)


def body(features, pre_norm, out_grad, weight, gamma, beta, neighbors, boundary, counts):
    table, columns, starts, gamma_grad, beta_grad = front(
        counts,
        pre_norm[0, 0],
        out_grad[0, 0],
        gamma[None],
        beta[None],
        neighbors[0, 0],
        boundary[0, 0][:, None],
    )
    in_grad, local_wgrad = convolve(starts, columns, table, features[0, 0], weight)
    weight_grad = scatter_sum(local_wgrad)
    return (in_grad[None, None], weight_grad, gamma_grad[0], beta_grad[0])


def solution(mesh):
    torus = Mesh(mesh.devices.reshape(4, 4, 2, mesh.shape["gy"]), ("gx_0", "gx_1", "gx_2", "gy"))
    return jax.shard_map(
        body,
        mesh=torus,
        in_specs=(
            P(GX, "gy", None, None),
            P(GX, "gy", None, None),
            P(GX, "gy", None, None),
            P(),
            P(),
            P(),
            P(GX, "gy", None, None),
            P(GX, "gy", None),
            P(GX, "gy"),
        ),
        out_specs=(P(GX, "gy", None, None), P(GX_GY, None), P(), P()),
        check_vma=False,
    )
```

```python
import jax
import jax.numpy as jnp
from jax import lax
from jax.experimental import pallas as pl
from jax.experimental.pallas import tpu as pltpu
from jax.sharding import Mesh
from jax.sharding import PartitionSpec as P

GX_GY = ("gx_0", "gx_1", "gx_2", "gy")
GX = ("gx_0", "gx_1", "gx_2")
MESH = pl.DeviceIdType.MESH


C = 256
R = 2048
SUB = 128
WIN = 256
NROW = 8384
FAR = 1.0e6


def dot(a, b, dims):
    return lax.dot_general(a, b, (dims, ((), ())), preferred_element_type=jnp.float32)


def one_hot(columns, start):
    lanes = lax.broadcasted_iota(jnp.int32, (SUB, WIN), 1).astype(jnp.float32)
    place = columns - start.astype(jnp.float32)
    return jnp.where(place == lanes, 1.0, 0.0).astype(jnp.bfloat16)

def conv_kernel(starts, idx, table, feat_t, turned, in_grad, wgrad, acc, picked):
    step = pl.program_id(0)
    lane0 = 24 - 3 * step

    @pl.when(step == 0)
    def _():
        acc[...] = jnp.zeros_like(acc)

    def columns_at(row):
        columns = pltpu.roll(idx[pl.ds(row, SUB), :], 128 - lane0, 1)
        return columns

    def window(columns, start):
        hot = [
            one_hot(jnp.broadcast_to(columns[:, 2 - i : 3 - i], (SUB, WIN)), start)
            for i in range(3)
        ]
        return jnp.concatenate(hot, axis=0)

    def gather(j):
        row = j * SUB
        columns = columns_at(row)
        s = [pl.multiple_of(starts[j * 8 + w, lane0], 16) for w in range(2)]
        hots = [window(columns, a) for a in s]
        tabs = [table[pl.ds(a, WIN), :] for a in s]
        total = dot(jnp.concatenate(hots, axis=1), jnp.concatenate(tabs, axis=0), ((1,), (0,)))
        total = total.astype(jnp.bfloat16)
        for i in range(3):
            picked[pl.ds(row, SUB), i * C : (i + 1) * C] = total[i * SUB : (i + 1) * SUB]

    def gather_rest(j):
        row = j * SUB

        def more(start):
            columns = columns_at(row)
            start = pl.multiple_of(start, 16)
            part = dot(window(columns, start), table[pl.ds(start, WIN), :], ((1,), (0,)))
            part = part.astype(jnp.bfloat16)
            for i in range(3):
                picked[pl.ds(row, SUB), i * C : (i + 1) * C] += part[i * SUB : (i + 1) * SUB]
            lane = lax.broadcasted_iota(jnp.int32, (SUB, 128), 1)
            ahead = (lane < 3) & (columns >= (start + WIN).astype(jnp.float32))
            low = jnp.min(jnp.where(ahead, columns, FAR)).astype(jnp.int32)
            return jnp.where(low < NROW, low // 16 * 16, jnp.int32(FAR))

        lax.while_loop(lambda start: start < NROW, more, starts[j * 8 + 2, lane0])

    for j in range(R // SUB):
        gather(j)
    for j in range(R // SUB):
        gather_rest(j)
    for i in range(3):
        wgrad[i] = dot(feat_t[...], picked[:, i * C : (i + 1) * C], ((1,), (0,)))
    acc[...] += dot(picked[...], turned[0], ((1,), (0,)))

    @pl.when(step == 8)
    def _():
        in_grad[...] = acc[...].astype(jnp.bfloat16)


def convolve(starts, idx, table, feat_t, turned):
    whole = pl.BlockSpec(memory_space=pltpu.VMEM)
    in_grad, wgrad = pl.pallas_call(
        conv_kernel,
        grid=(9,),
        out_shape=(
            jax.ShapeDtypeStruct((R, C), jnp.bfloat16),
            jax.ShapeDtypeStruct((27, C, C), jnp.float32),
        ),
        in_specs=[
            pl.BlockSpec(memory_space=pltpu.SMEM),
            whole,
            whole,
            whole,
            pl.BlockSpec((1, 3 * C, C), lambda g: (g, 0, 0)),
        ],
        out_specs=(whole, pl.BlockSpec((3, C, C), lambda g: (g, 0, 0))),
        scratch_shapes=[
            pltpu.VMEM((R, C), jnp.float32),
            pltpu.VMEM((R, 3 * C), jnp.bfloat16),
        ],
        compiler_params=pltpu.CompilerParams(vmem_limit_bytes=28 * 1024 * 1024),
        cost_estimate=pl.CostEstimate(
            flops=30_000_000_000, bytes_accessed=20_000_000, transcendentals=0
        ),
        name="conv_backward",
    )(starts, idx, table, feat_t, turned)
    return in_grad, wgrad.reshape(27 * C, C)


AXES = ("gy", "gx_1", "gx_0")
TILE_AT = (0, 16, 32, 38)
HOLDS = (((0, 0), (0, 1), (3, 0)), ((1, 0), (1, 1), (3, 1)), ((2, 0), (2, 1)))


def scatter_kernel(part, out, s_a, r_a, *rest):
    s_b, r_b, s_c, r_c, s_d, r_d = (rest[3 * i : 3 * i + 3] for i in range(6))
    a_sem, b_sem, c_sem, d_sem = rest[18:]
    pos = [lax.axis_index(a) for a in AXES]
    core = lax.axis_index("gx_2")
    z = pos[2]

    def around(i):
        return lax.rem(z + 1 + i, 4)

    barrier = pltpu.get_barrier_semaphore()
    pl.semaphore_signal(barrier, 1, device_id={"gx_2": 1 - core}, device_id_type=MESH)
    for axis, at in zip(AXES, pos):
        for d in range(1, 4):
            peer = {axis: lax.rem(at + d, 4)}
            pl.semaphore_signal(barrier, 1, device_id=peer, device_id_type=MESH)

    def block(i, y, x, side, t):
        skip = (x * 54 + TILE_AT[t]) % 8
        base = around(i) * 1728 + (y * 2 + side) * 216 + x * 54 + TILE_AT[t] - skip
        rows = part[pl.ds(pl.multiple_of(base, 8), 24 if skip else 16), :]
        return rows[skip : skip + 16]

    sends = []

    def send(src, dst, sems, at, device):
        copy = pltpu.make_async_remote_copy(
            src_ref=src,
            dst_ref=dst,
            send_sem=sems.at[(0,) + at],
            recv_sem=sems.at[(1,) + at],
            device_id=device,
            device_id_type=MESH,
        )
        copy.start()
        sends.append(copy)
        return copy

    first = []
    for i in range(4):
        @pl.loop(0, 4)
        def _(y):
            for x in range(4):
                for t in range(4):
                    mine = block(i, y, x, 1 - core, t)
                    s_a[i, y * 4 + x, t] = mine.astype(jnp.bfloat16)

        if i == 0:
            pl.semaphore_wait(barrier, 10)
        first.append(send(s_a.at[i], r_a.at[i], a_sem, (i,), {"gx_2": 1 - core}))

    def spread(p, stage, sems, src, dst):
        axis = (p + stage) % 3
        return [
            send(
                src.at[lax.rem(pos[axis] + d, 4)],
                dst.at[d - 1],
                sems,
                (p, d - 1),
                {AXES[axis]: lax.rem(pos[axis] + d, 4)},
            )
            for d in range(1, 4)
        ]

    second = [None, None, []]
    for i in range(4):
        first[i].wait_recv()
        z_of = around(i)

        @pl.loop(0, 4)
        def _(y):
            for x in range(4):
                for t in range(4):
                    both = block(i, y, x, core, t) + r_a[i, y * 4 + x, t].astype(jnp.float32)
                    both = both.astype(jnp.bfloat16)
                    for p, holds in enumerate(HOLDS):
                        for n, (tile, side) in enumerate(holds):
                            if tile != t:
                                continue
                            piece = both[:, side * 128 : (side + 1) * 128]
                            if p == 0:
                                s_b[0][x, y * 4 + z_of, n] = piece
                            elif p == 1:
                                s_b[1][y, z_of * 4 + x, n] = piece
                            else:
                                s_b[2][z_of, x * 4 + y, n] = piece

        if i < 3:
            second[2].append(
                send(s_b[2].at[z_of], r_b[2].at[i], b_sem, (2, i), {"gx_0": z_of})
            )
    for p in range(2):
        second[p] = spread(p, 0, b_sem, s_b[p], r_b[p])

    def total(own, came, at):
        kind = jnp.float32
        return (own[at].astype(kind) + came[(0,) + at[1:]].astype(kind)) + (
            came[(1,) + at[1:]].astype(kind) + came[(2,) + at[1:]].astype(kind)
        )

    third = []
    for p in range(3):
        for copy in second[p]:
            copy.wait_recv()
        me = pos[p]

        @pl.loop(0, 16)
        def _(j):
            for t in range(len(HOLDS[p])):
                s_c[p][j // 4, j % 4, t] = total(s_b[p], r_b[p], (me, j, t)).astype(jnp.bfloat16)

        third.append(spread(p, 1, c_sem, s_c[p], r_c[p]))

    fourth = []
    for p in range(3):
        for copy in third[p]:
            copy.wait_recv()
        me = pos[(p + 1) % 3]

        @pl.loop(0, 4)
        def _(j):
            for t in range(len(HOLDS[p])):
                s_d[p][j, t] = total(s_c[p], r_c[p], (me, j, t))

        fourth.append(spread(p, 2, d_sem, s_d[p], r_d[p]))

    for p in range(3):
        for copy in fourth[p]:
            copy.wait_recv()
        me = pos[(p + 2) % 3]
        for n, (tile, side) in enumerate(HOLDS[p]):
            rows = pl.ds(TILE_AT[tile], 16)
            out[rows, side * 128 : (side + 1) * 128] = total(s_d[p], r_d[p], (me, n))

    for copy in sends:
        copy.wait_send()


def scatter_sum(part):
    def stage(lead, kind):
        return [pltpu.VMEM(lead + (len(h), 16, 128), kind) for h in HOLDS]

    half, full = jnp.bfloat16, jnp.float32
    return pl.pallas_call(
        scatter_kernel,
        out_shape=jax.ShapeDtypeStruct((54, C), jnp.float32),
        in_specs=[pl.BlockSpec(memory_space=pltpu.VMEM)],
        out_specs=pl.BlockSpec(memory_space=pltpu.VMEM),
        scratch_shapes=[
            pltpu.VMEM((4, 16, 4, 16, C), jnp.bfloat16),
            pltpu.VMEM((4, 16, 4, 16, C), jnp.bfloat16),
            *stage((4, 16), half),
            *stage((3, 16), half),
            *stage((4, 4), half),
            *stage((3, 4), half),
            *stage((4,), full),
            *stage((3,), full),
            pltpu.SemaphoreType.DMA((2, 4)),
            pltpu.SemaphoreType.DMA((2, 3, 3)),
            pltpu.SemaphoreType.DMA((2, 3, 3)),
            pltpu.SemaphoreType.DMA((2, 3, 3)),
        ],
        compiler_params=pltpu.CompilerParams(
            collective_id=1, has_side_effects=True, vmem_limit_bytes=24 * 1024 * 1024
        ),
        cost_estimate=pl.CostEstimate(flops=10_000_000, bytes_accessed=7_000_000, transcendentals=0),
        name="scatter_sum",
    )(part)


HB = 704
HIGH = 272
ROWS = NROW + WIN


def seg(b):
    return R + b * HB


def front_kernel(
    count, pre_in, cot_in, gamma_in, beta_in, links_in, border_in, feat_in, weight_in,
    table, columns, starts, gamma_grad, beta_grad, feat_t, turned,
    pre, cot, gamma, beta, links, border, feat, weight,
    grad, pick, near, far, list_left, list_own, list_right, high,
    note_own, note_left, note_right, note_out, note_in,
    load_sem, near_sem, far_sem, halo_sem, note_sem,
):
    f32 = jnp.float32
    z, y, core, x = (lax.axis_index(a) for a in GX_GY)
    slab = (z * 4 + y) * 2 + core
    me_near, me_far = x * 2 + core, z * 4 + y

    def near_id(p):
        return {"gy": p // 2, "gx_2": lax.rem(p, 2)}

    def far_id(p):
        return {"gx_0": p // 4, "gx_1": lax.rem(p, 4)}

    def slab_id(s):
        return {"gx_0": s // 8, "gx_1": lax.rem(s // 2, 4), "gx_2": lax.rem(s, 2)}

    loads = []
    for source, target in (
        (pre_in, pre),
        (border_in, border),
        (cot_in, cot),
        (gamma_in, gamma),
        (beta_in, beta),
        (links_in, links),
        (feat_in, feat),
        (weight_in, weight),
    ):
        loads.append(pltpu.make_async_copy(source, target, load_sem.at[len(loads)]))
        loads[-1].start()

    barrier = pltpu.get_barrier_semaphore()
    for d in range(1, 8):
        pl.semaphore_signal(
            barrier, 1, device_id=near_id(lax.rem(me_near + d, 8)), device_id_type=MESH
        )
    for d in range(1, 16):
        pl.semaphore_signal(
            barrier, 1, device_id=far_id(lax.rem(me_far + d, 16)), device_id_type=MESH
        )
    up, down = (core == 1) & (slab < 31), (core == 0) & (slab > 0)

    @pl.when(up)
    def _():
        pl.semaphore_signal(barrier, 1, device_id=slab_id(slab + 1), device_id_type=MESH)

    @pl.when(down)
    def _():
        pl.semaphore_signal(barrier, 1, device_id=slab_id(slab - 1), device_id_type=MESH)

    live_rows = count[0, 0]
    block = 128

    def live_at(t):
        row = lax.broadcasted_iota(jnp.int32, (block, C), 0) + t * block
        return row < live_rows

    def rows_at(t):
        return pl.ds(pl.multiple_of(t * block, block), block)

    def fold(a):
        return jnp.sum(a.reshape(block // 8, 8, C), axis=0)

    def first_sums(t, sums):
        zval = pre[rows_at(t), :].astype(f32)
        zlive = jnp.where(live_at(t), zval, 0.0)
        return sums[0] + fold(zlive), sums[1] + fold(zlive * zval)

    zero = jnp.zeros((8, C), f32)
    line = lax.broadcasted_iota(jnp.int32, (8, C), 0)

    def stacked(a, b, c):
        a, b = jnp.sum(a, axis=0, keepdims=True), jnp.sum(b, axis=0, keepdims=True)
        return jnp.where(line == 0, a, jnp.where(line == 1, b, jnp.where(line == 2, c, 0.0)))

    def exchange(slots, me, size, sems, turn, ids):
        copies = []
        for d in range(1, size):
            copies.append(
                pltpu.make_async_remote_copy(
                    src_ref=slots.at[turn, me],
                    dst_ref=slots.at[turn, me],
                    send_sem=sems.at[turn, 0, d - 1],
                    recv_sem=sems.at[turn, 1, d - 1],
                    device_id=ids(lax.rem(me + d, size)),
                    device_id_type=MESH,
                )
            )
            copies[-1].start()
        return copies

    def add_up(slots, size, turn, copies):
        for copy in copies:
            copy.wait_recv()
        total = slots[turn, 0]
        for i in range(1, size):
            total = total + slots[turn, i]
        return total

    def all_sum(turn, value, meanwhile):
        near[turn, me_near] = value
        one = exchange(near, me_near, 8, near_sem, turn, near_id)
        meanwhile()
        far[turn, me_far] = add_up(near, 8, turn, one)
        two = exchange(far, me_far, 16, far_sem, turn, far_id)
        total = add_up(far, 16, turn, two)
        for copy in one + two:
            copy.wait_send()
        return total

    def when(cond, act):
        @pl.when(cond)
        def _():
            act()

    has_right, has_left, has_next, has_last = x < 3, x > 0, slab < 31, slab > 0

    def note(source, target, n, device):
        return pltpu.make_async_remote_copy(
            src_ref=source,
            dst_ref=target,
            send_sem=note_sem.at[0, n],
            recv_sem=note_sem.at[1, n],
            device_id=device,
            device_id_type=MESH,
        )

    def note_to_right():
        return note(note_own, note_left, 0, {"gy": x + 1})

    def note_to_left():
        return note(note_own, note_right, 1, {"gy": x - 1})

    def note_ahead():
        return note(note_out, note_in, 2, slab_id(slab + 1))

    def blank(ref):
        ref[...] = jnp.zeros_like(ref)

    def notes_first():
        size = jnp.sum(jnp.where(border[...] < R, 1, 0), axis=1, keepdims=True)
        first = jnp.minimum(jnp.maximum(size - WIN, 0) // 16, (HB - HIGH) // 16)
        note_own[...] = jnp.broadcast_to(first, (8, 128))
        when(~has_left, lambda: blank(note_left))
        when(~has_right, lambda: blank(note_right))
        when(~has_last, lambda: blank(note_in))

    def notes_second():
        when(has_left, lambda: note_to_right().wait_recv())
        when(has_right, lambda: note_to_left().wait_recv())
        row = lax.broadcasted_iota(jnp.int32, (8, 128), 0)
        note_out[...] = jnp.where(
            row == 0, note_left[...], jnp.where(row == 1, note_own[...], note_right[...])
        )
        when(has_next, lambda: note_ahead().start())

    def plan():
        loads[5].wait()
        when(has_last, lambda: note_ahead().wait_recv())
        moved = [note_in[b : b + 1, :] * 16 for b in range(3)]
        lane = lax.broadcasted_iota(jnp.int32, (1, 128), 1)
        third = lax.rem(lane, 3)

        @pl.loop(0, R // SUB)
        def _(j):
            at = pl.ds(pl.multiple_of(j * SUB, SUB), SUB)
            idx = links[:, 0, at]
            for b in range(3):
                inside = (idx >= seg(b)) & (idx < seg(b + 1))
                idx = jnp.where(inside, idx - moved[b], idx)
            idx = jnp.where(idx < NROW, idx, jnp.int32(FAR)).astype(f32)
            idx = jnp.concatenate([idx, jnp.full((101, SUB), FAR, f32)], axis=0).T
            columns[at, :] = idx
            begin = []
            for w in range(3):
                low = jnp.min(idx, axis=0, keepdims=True)
                low = jnp.minimum(low, jnp.minimum(pltpu.roll(low, 127, 1), pltpu.roll(low, 126, 1)))
                low = jnp.where(
                    third == 0,
                    low,
                    jnp.where(third == 1, pltpu.roll(low, 1, 1), pltpu.roll(low, 2, 1)),
                )
                start = jnp.where(low < NROW, jnp.floor(low * 0.0625) * 16.0, FAR)
                idx = jnp.where(idx >= start + WIN, idx, FAR)
                begin.append(jnp.minimum(start, float(NROW)) if w < 2 else start)
            begin = [jnp.broadcast_to(b, (8, 128)) for b in begin]
            row = lax.broadcasted_iota(jnp.int32, (8, 128), 0)
            begin = jnp.where(row == 0, begin[0], jnp.where(row == 1, begin[1], begin[2]))
            starts[pl.ds(pl.multiple_of(j * 8, 8), 8), :] = begin.astype(jnp.int32)

    def choose():
        lane = lax.broadcasted_iota(jnp.int32, (128, 128), 1)
        for t in range(6):
            width = min(128, HB - t * 128)
            names = border[:, t * 128 : t * 128 + width].astype(f32)
            if width < 128:
                names = jnp.concatenate([names, jnp.full((1, 128 - width), FAR, f32)], axis=1)
            names = jnp.broadcast_to(names, (128, 128)).T[:width]
            for c in range(R // 128):
                row = (lane[:width] + c * 128).astype(f32)
                pick[t * 128 : t * 128 + width, c * 128 : (c + 1) * 128] = jnp.where(
                    names == row, 1.0, 0.0
                ).astype(jnp.bfloat16)

        def clear(at, size):
            table[at : at + size, :] = jnp.zeros((size, C), jnp.bfloat16)

        clear(NROW, WIN)

        @pl.when(slab == 0)
        def _():
            for b in (0, 1, 2):
                clear(seg(b), HIGH)

        @pl.when(slab == 31)
        def _():
            for b in (6, 7, 8):
                clear(seg(b), WIN)

        for b in (0, 1, 2):
            clear(seg(b) + HIGH, HB - HIGH)

        for b in (6, 7, 8):
            clear(seg(b) + WIN, HB - WIN)

        for edge, db, missing in ((0, 0, list_left), (3, 2, list_right)):
            @pl.when(x == edge)
            def _():
                blank(missing)

                @pl.when(slab > 0)
                def _():
                    clear(seg(db), HIGH)

                @pl.when(slab < 31)
                def _():
                    clear(seg(6 + db), WIN)

    loads[0].wait()
    sum_z, sum_sq = lax.fori_loop(0, R // block, first_sums, (zero, zero))
    loads[1].wait()
    notes_first()
    extra = jnp.where(up | down, 1, 0)
    pl.semaphore_wait(barrier, 22 + extra)
    when(has_right, lambda: note_to_right().start())
    when(has_left, lambda: note_to_left().start())

    def during_first():
        choose()
        notes_second()

    whole = all_sum(0, stacked(sum_z, sum_sq, live_rows.astype(f32)), during_first)
    amount = whole[2:3]
    mean = whole[0:1] / amount
    var = whole[1:2] / amount - mean * mean
    rstd = lax.rsqrt(var + 1e-05)
    for load in loads[2:5]:
        load.wait()
    gain, shift = gamma[...], beta[...]

    def second_sums(t, sums):
        zhat = (pre[rows_at(t), :].astype(f32) - mean) * rstd
        act = gain * zhat + shift
        sig = jax.nn.sigmoid(act)
        g = cot[rows_at(t), :].astype(f32) * sig * (1.0 + act * (1.0 - sig))
        g = jnp.where(live_at(t), g, 0.0)
        grad[rows_at(t), :] = g
        return sums[0] + fold(g), sums[1] + fold(g * zhat)

    sum_g, sum_gz = lax.fori_loop(0, R // block, second_sums, (zero, zero))
    whole = all_sum(1, stacked(sum_g, sum_gz, 0.0), plan)
    beta_grad[...] = whole[0:1]
    gamma_grad[...] = whole[1:2]
    scale = gain * rstd
    part_g, part_gz = whole[0:1] / amount, whole[1:2] / amount

    @pl.loop(0, R // block)
    def _(t):
        zhat = (pre[rows_at(t), :].astype(f32) - mean) * rstd
        dz = scale * (grad[rows_at(t), :] - part_g - zhat * part_gz)
        table[rows_at(t), :] = jnp.where(live_at(t), dz, 0.0).astype(jnp.bfloat16)

    @pl.loop(0, 4)
    def _(t):
        at = pl.multiple_of(t * 176, 16)
        rows = dot(pick[pl.ds(at, 176), :], table[0:R, :], ((1,), (0,)))
        list_own[pl.ds(at, 176), :] = rows.astype(jnp.bfloat16)

    def hop(source, target, n, device):
        return pltpu.make_async_remote_copy(
            src_ref=source,
            dst_ref=target,
            send_sem=halo_sem.at[0, n],
            recv_sem=halo_sem.at[1, n],
            device_id=device,
            device_id_type=MESH,
        )

    lists = (list_left, list_own, list_right)

    def right():
        return hop(list_own, list_left, 3, {"gy": x + 1})

    def left():
        return hop(list_own, list_right, 5, {"gy": x - 1})

    def ahead(db):
        return hop(high.at[db], table.at[pl.ds(seg(db), HIGH), :], db, slab_id(slab + 1))

    def behind(db):
        target = table.at[pl.ds(seg(6 + db), WIN), :]
        return hop(lists[db].at[pl.ds(0, WIN), :], target, 6 + db, slab_id(slab - 1))

    def pass_on(db, mark):
        at = jnp.max(mark[...]) * 16
        high[db] = lists[db][pl.ds(at, HIGH), :]
        when(has_next, lambda: ahead(db).start())
        when(has_last, lambda: behind(db).start())

    when(has_right, lambda: right().start())
    when(has_left, lambda: left().start())
    pass_on(1, note_own)
    table[seg(4) : seg(5), :] = list_own[...]
    loads[6].wait()
    for t in range(8):
        feat_t[:, t * 256 : (t + 1) * 256] = feat[t * 256 : (t + 1) * 256, :].T
    loads[7].wait()
    for db, there, came, mark in (
        (0, has_left, right, note_left),
        (2, has_right, left, note_right),
    ):
        when(there, lambda: came().wait_recv())
        when(there, lambda: pass_on(db, mark))
        table[seg(3 + db) : seg(4 + db), :] = lists[db][...]

    @pl.loop(0, 9)
    def _(g):
        for i in range(3):
            turned[g, i * C : (i + 1) * C, :] = weight[g * 3 + i].T

    for db, there in ((1, True), (0, has_left), (2, has_right)):
        when(has_last & there, lambda: ahead(db).wait_recv())
        when(has_next & there, lambda: behind(db).wait_recv())
    when(has_right, lambda: right().wait_send())
    when(has_left, lambda: left().wait_send())
    for db, there in ((1, True), (0, has_left), (2, has_right)):
        when(has_next & there, lambda: ahead(db).wait_send())
        when(has_last & there, lambda: behind(db).wait_send())
    when(has_right, lambda: note_to_right().wait_send())
    when(has_left, lambda: note_to_left().wait_send())
    when(has_next, lambda: note_ahead().wait_send())


def front(counts, *arrays):
    vmem = pl.BlockSpec(memory_space=pltpu.VMEM)
    return pl.pallas_call(
        front_kernel,
        out_shape=(
            jax.ShapeDtypeStruct((ROWS, C), jnp.bfloat16),
            jax.ShapeDtypeStruct((R, 128), jnp.float32),
            jax.ShapeDtypeStruct((R // SUB * 8, 128), jnp.int32),
            jax.ShapeDtypeStruct((1, C), jnp.float32),
            jax.ShapeDtypeStruct((1, C), jnp.float32),
            jax.ShapeDtypeStruct((C, R), jnp.bfloat16),
            jax.ShapeDtypeStruct((9, 3 * C, C), jnp.bfloat16),
        ),
        in_specs=[pl.BlockSpec(memory_space=pltpu.SMEM)]
        + [pl.BlockSpec(memory_space=pltpu.HBM)] * 8,
        out_specs=(vmem,) * 7,
        scratch_shapes=[pltpu.VMEM(a.shape, a.dtype) for a in arrays]
        + [
            pltpu.VMEM((R, C), jnp.float32),
            pltpu.VMEM((HB, R), jnp.bfloat16),
            pltpu.VMEM((2, 8, 8, C), jnp.float32),
            pltpu.VMEM((2, 16, 8, C), jnp.float32),
            pltpu.VMEM((HB, C), jnp.bfloat16),
            pltpu.VMEM((HB, C), jnp.bfloat16),
            pltpu.VMEM((HB, C), jnp.bfloat16),
            pltpu.VMEM((3, HIGH, C), jnp.bfloat16),
            *[pltpu.VMEM((8, 128), jnp.int32)] * 5,
            pltpu.SemaphoreType.DMA((8,)),
            pltpu.SemaphoreType.DMA((2, 2, 7)),
            pltpu.SemaphoreType.DMA((2, 2, 15)),
            pltpu.SemaphoreType.DMA((2, 9)),
            pltpu.SemaphoreType.DMA((2, 3)),
        ],
        compiler_params=pltpu.CompilerParams(
            collective_id=0, has_side_effects=True, vmem_limit_bytes=24 * 1024 * 1024
        ),
        cost_estimate=pl.CostEstimate(
            flops=1_000_000_000, bytes_accessed=10_000_000, transcendentals=1_000_000
        ),
        name="front",
    )(counts, *arrays)


def body(features, pre_norm, out_grad, weight, gamma, beta, neighbors, boundary, counts):
    table, columns, starts, gamma_grad, beta_grad, feat_t, turned = front(
        counts,
        pre_norm[0, 0],
        out_grad[0, 0],
        gamma[None],
        beta[None],
        neighbors.reshape(27, 1, R),
        boundary.reshape(1, HB),
        features[0, 0],
        weight,
    )
    in_grad, local_wgrad = convolve(starts, columns, table, feat_t, turned)
    weight_grad = scatter_sum(local_wgrad)
    return (in_grad[None, None], weight_grad, gamma_grad[0], beta_grad[0])


def solution(mesh):
    torus = Mesh(mesh.devices.reshape(4, 4, 2, mesh.shape["gy"]), ("gx_0", "gx_1", "gx_2", "gy"))
    return jax.shard_map(
        body,
        mesh=torus,
        in_specs=(
            P(GX, "gy", None, None),
            P(GX, "gy", None, None),
            P(GX, "gy", None, None),
            P(),
            P(),
            P(),
            P(GX, "gy", None, None),
            P(GX, "gy", None),
            P(GX, "gy"),
        ),
        out_specs=(P(GX, "gy", None, None), P(GX_GY, None), P(), P()),
        check_vma=False,
    )
```

```python
import jax
import jax.numpy as jnp
from jax import lax
from jax.experimental import pallas as pl
from jax.experimental.pallas import tpu as pltpu
from jax.sharding import Mesh
from jax.sharding import PartitionSpec as P

GX_GY = ("gx_0", "gx_1", "gx_2", "gy")
GX = ("gx_0", "gx_1", "gx_2")
MESH = pl.DeviceIdType.MESH


C = 256
R = 2048
SUB = 128
WIN = 256
NROW = 8384
FAR = 1.0e6


def dot(a, b, dims):
    return lax.dot_general(a, b, (dims, ((), ())), preferred_element_type=jnp.float32)


def one_hot(columns, start):
    lanes = lax.broadcasted_iota(jnp.int32, (SUB, WIN), 1).astype(jnp.float32)
    place = columns - start.astype(jnp.float32)
    return jnp.where(place == lanes, 1.0, 0.0).astype(jnp.bfloat16)

def conv_kernel(
    starts, idx, table, feat_t, turned, sums_in, in_grad, wgrad, gamma_grad, beta_grad,
    acc, picked,
):
    step = pl.program_id(0)
    lane0 = 24 - 3 * step

    @pl.when(step == 0)
    def _():
        acc[...] = jnp.zeros_like(acc)
        beta_grad[...] = sums_in[0]
        gamma_grad[...] = sums_in[1]

    def columns_at(row):
        columns = pltpu.roll(idx[pl.ds(row, SUB), :], 128 - lane0, 1)
        return columns

    def window(columns, start):
        hot = [
            one_hot(jnp.broadcast_to(columns[:, 2 - i : 3 - i], (SUB, WIN)), start)
            for i in range(3)
        ]
        return jnp.concatenate(hot, axis=0)

    def gather(j):
        row = j * SUB
        columns = columns_at(row)
        s = [pl.multiple_of(starts[j * 8 + w, lane0], 16) for w in range(2)]
        hots = [window(columns, a) for a in s]
        tabs = [table[pl.ds(a, WIN), :] for a in s]
        total = dot(jnp.concatenate(hots, axis=1), jnp.concatenate(tabs, axis=0), ((1,), (0,)))
        total = total.astype(jnp.bfloat16)
        for i in range(3):
            picked[pl.ds(row, SUB), i * C : (i + 1) * C] = total[i * SUB : (i + 1) * SUB]

    def gather_rest(j):
        row = j * SUB

        def more(start):
            columns = columns_at(row)
            start = pl.multiple_of(start, 16)
            part = dot(window(columns, start), table[pl.ds(start, WIN), :], ((1,), (0,)))
            part = part.astype(jnp.bfloat16)
            for i in range(3):
                picked[pl.ds(row, SUB), i * C : (i + 1) * C] += part[i * SUB : (i + 1) * SUB]
            lane = lax.broadcasted_iota(jnp.int32, (SUB, 128), 1)
            ahead = (lane < 3) & (columns >= (start + WIN).astype(jnp.float32))
            low = jnp.min(jnp.where(ahead, columns, FAR)).astype(jnp.int32)
            return jnp.where(low < NROW, low // 16 * 16, jnp.int32(FAR))

        lax.while_loop(lambda start: start < NROW, more, starts[j * 8 + 2, lane0])

    for j in range(R // SUB):
        gather(j)
    for j in range(R // SUB):
        gather_rest(j)
    for i in range(3):
        wgrad[i] = dot(feat_t[...], picked[:, i * C : (i + 1) * C], ((1,), (0,)))
    acc[...] += dot(picked[...], turned[0], ((1,), (0,)))

    @pl.when(step == 8)
    def _():
        in_grad[...] = acc[...].astype(jnp.bfloat16)


def convolve(starts, idx, table, feat_t, turned, sums):
    whole = pl.BlockSpec(memory_space=pltpu.VMEM)
    in_grad, wgrad, gamma_grad, beta_grad = pl.pallas_call(
        conv_kernel,
        grid=(9,),
        out_shape=(
            jax.ShapeDtypeStruct((R, C), jnp.bfloat16),
            jax.ShapeDtypeStruct((27, C, C), jnp.float32),
            jax.ShapeDtypeStruct((1, C), jnp.float32),
            jax.ShapeDtypeStruct((1, C), jnp.float32),
        ),
        in_specs=[
            pl.BlockSpec(memory_space=pltpu.SMEM),
            whole,
            whole,
            whole,
            pl.BlockSpec((1, 3 * C, C), lambda g: (g, 0, 0)),
            whole,
        ],
        out_specs=(whole, pl.BlockSpec((3, C, C), lambda g: (g, 0, 0)), whole, whole),
        scratch_shapes=[
            pltpu.VMEM((R, C), jnp.float32),
            pltpu.VMEM((R, 3 * C), jnp.bfloat16),
        ],
        compiler_params=pltpu.CompilerParams(vmem_limit_bytes=28 * 1024 * 1024),
        cost_estimate=pl.CostEstimate(
            flops=30_000_000_000, bytes_accessed=20_000_000, transcendentals=0
        ),
        name="conv_backward",
    )(starts, idx, table, feat_t, turned, sums)
    return in_grad, wgrad.reshape(27 * C, C), gamma_grad, beta_grad


AXES = ("gy", "gx_1", "gx_0")
TILE_AT = (0, 16, 32, 38)
HOLDS = (((0, 0), (0, 1), (3, 0)), ((1, 0), (1, 1), (3, 1)), ((2, 0), (2, 1)))


def scatter_kernel(part, out, s_a, r_a, *rest):
    s_b, r_b, s_c, r_c, s_d, r_d = (rest[3 * i : 3 * i + 3] for i in range(6))
    a_sem, b_sem, c_sem, d_sem = rest[18:]
    pos = [lax.axis_index(a) for a in AXES]
    core = lax.axis_index("gx_2")
    z = pos[2]

    def around(i):
        return lax.rem(z + 1 + i, 4)

    barrier = pltpu.get_barrier_semaphore()
    pl.semaphore_signal(barrier, 1, device_id={"gx_2": 1 - core}, device_id_type=MESH)
    for axis, at in zip(AXES, pos):
        for d in range(1, 4):
            peer = {axis: lax.rem(at + d, 4)}
            pl.semaphore_signal(barrier, 1, device_id=peer, device_id_type=MESH)

    def block(i, y, x, side, t):
        skip = (x * 54 + TILE_AT[t]) % 8
        base = around(i) * 1728 + (y * 2 + side) * 216 + x * 54 + TILE_AT[t] - skip
        rows = part[pl.ds(pl.multiple_of(base, 8), 24 if skip else 16), :]
        return rows[skip : skip + 16]

    sends = []

    def send(src, dst, sems, at, device):
        copy = pltpu.make_async_remote_copy(
            src_ref=src,
            dst_ref=dst,
            send_sem=sems.at[(0,) + at],
            recv_sem=sems.at[(1,) + at],
            device_id=device,
            device_id_type=MESH,
        )
        copy.start()
        sends.append(copy)
        return copy

    first = []
    for i in range(4):
        @pl.loop(0, 4)
        def _(y):
            for x in range(4):
                for t in range(4):
                    mine = block(i, y, x, 1 - core, t)
                    s_a[i, y * 4 + x, t] = mine.astype(jnp.bfloat16)

        if i == 0:
            pl.semaphore_wait(barrier, 10)
        first.append(send(s_a.at[i], r_a.at[i], a_sem, (i,), {"gx_2": 1 - core}))

    def spread(p, stage, sems, src, dst):
        axis = (p + stage) % 3
        return [
            send(
                src.at[lax.rem(pos[axis] + d, 4)],
                dst.at[d - 1],
                sems,
                (p, d - 1),
                {AXES[axis]: lax.rem(pos[axis] + d, 4)},
            )
            for d in range(1, 4)
        ]

    second = [None, None, []]
    for i in range(4):
        first[i].wait_recv()
        z_of = around(i)

        @pl.loop(0, 4)
        def _(y):
            for x in range(4):
                for t in range(4):
                    both = block(i, y, x, core, t) + r_a[i, y * 4 + x, t].astype(jnp.float32)
                    both = both.astype(jnp.bfloat16)
                    for p, holds in enumerate(HOLDS):
                        for n, (tile, side) in enumerate(holds):
                            if tile != t:
                                continue
                            piece = both[:, side * 128 : (side + 1) * 128]
                            if p == 0:
                                s_b[0][x, y * 4 + z_of, n] = piece
                            elif p == 1:
                                s_b[1][y, z_of * 4 + x, n] = piece
                            else:
                                s_b[2][z_of, x * 4 + y, n] = piece

        if i < 3:
            second[2].append(
                send(s_b[2].at[z_of], r_b[2].at[i], b_sem, (2, i), {"gx_0": z_of})
            )
    for p in range(2):
        second[p] = spread(p, 0, b_sem, s_b[p], r_b[p])

    def total(own, came, at):
        kind = jnp.float32
        return (own[at].astype(kind) + came[(0,) + at[1:]].astype(kind)) + (
            came[(1,) + at[1:]].astype(kind) + came[(2,) + at[1:]].astype(kind)
        )

    third = []
    for p in range(3):
        for copy in second[p]:
            copy.wait_recv()
        me = pos[p]

        @pl.loop(0, 16)
        def _(j):
            for t in range(len(HOLDS[p])):
                s_c[p][j // 4, j % 4, t] = total(s_b[p], r_b[p], (me, j, t)).astype(jnp.bfloat16)

        third.append(spread(p, 1, c_sem, s_c[p], r_c[p]))

    fourth = []
    for p in range(3):
        for copy in third[p]:
            copy.wait_recv()
        me = pos[(p + 1) % 3]

        @pl.loop(0, 4)
        def _(j):
            for t in range(len(HOLDS[p])):
                s_d[p][j, t] = total(s_c[p], r_c[p], (me, j, t))

        fourth.append(spread(p, 2, d_sem, s_d[p], r_d[p]))

    for p in range(3):
        for copy in fourth[p]:
            copy.wait_recv()
        me = pos[(p + 2) % 3]
        for n, (tile, side) in enumerate(HOLDS[p]):
            rows = pl.ds(TILE_AT[tile], 16)
            out[rows, side * 128 : (side + 1) * 128] = total(s_d[p], r_d[p], (me, n))

    for copy in sends:
        copy.wait_send()


def scatter_sum(part):
    def stage(lead, kind):
        return [pltpu.VMEM(lead + (len(h), 16, 128), kind) for h in HOLDS]

    half, full = jnp.bfloat16, jnp.float32
    return pl.pallas_call(
        scatter_kernel,
        out_shape=jax.ShapeDtypeStruct((54, C), jnp.float32),
        in_specs=[pl.BlockSpec(memory_space=pltpu.VMEM)],
        out_specs=pl.BlockSpec(memory_space=pltpu.VMEM),
        scratch_shapes=[
            pltpu.VMEM((4, 16, 4, 16, C), jnp.bfloat16),
            pltpu.VMEM((4, 16, 4, 16, C), jnp.bfloat16),
            *stage((4, 16), half),
            *stage((3, 16), half),
            *stage((4, 4), half),
            *stage((3, 4), half),
            *stage((4,), full),
            *stage((3,), full),
            pltpu.SemaphoreType.DMA((2, 4)),
            pltpu.SemaphoreType.DMA((2, 3, 3)),
            pltpu.SemaphoreType.DMA((2, 3, 3)),
            pltpu.SemaphoreType.DMA((2, 3, 3)),
        ],
        compiler_params=pltpu.CompilerParams(
            collective_id=1, has_side_effects=True, vmem_limit_bytes=24 * 1024 * 1024
        ),
        cost_estimate=pl.CostEstimate(flops=10_000_000, bytes_accessed=7_000_000, transcendentals=0),
        name="scatter_sum",
    )(part)


HB = 704
HIGH = 272
ROWS = NROW + WIN


def seg(b):
    return R + b * HB


def front_kernel(
    count, pre_in, cot_in, gamma_in, beta_in, links_in, border_in, feat_in, weight_in,
    table, columns, starts, sums, feat_t, turned,
    pre, cot, gamma, beta, links, border, feat, weight,
    grad, pick, near, far, list_left, list_own, list_right, high,
    note_own, note_left, note_right, note_out, note_in,
    load_sem, near_sem, far_sem, halo_sem, note_sem,
):
    f32 = jnp.float32
    z, y, core, x = (lax.axis_index(a) for a in GX_GY)
    slab = (z * 4 + y) * 2 + core
    me_near, me_far = x * 2 + core, z * 4 + y

    def near_id(p):
        return {"gy": p // 2, "gx_2": lax.rem(p, 2)}

    def far_id(p):
        return {"gx_0": p // 4, "gx_1": lax.rem(p, 4)}

    def slab_id(s):
        return {"gx_0": s // 8, "gx_1": lax.rem(s // 2, 4), "gx_2": lax.rem(s, 2)}

    loads = []
    for source, target in (
        (pre_in, pre),
        (border_in, border),
        (cot_in, cot),
        (gamma_in, gamma),
        (beta_in, beta),
        (links_in, links),
        (feat_in, feat),
        (weight_in, weight),
    ):
        loads.append(pltpu.make_async_copy(source, target, load_sem.at[len(loads)]))
        loads[-1].start()

    barrier = pltpu.get_barrier_semaphore()
    for d in range(1, 8):
        pl.semaphore_signal(
            barrier, 1, device_id=near_id(lax.rem(me_near + d, 8)), device_id_type=MESH
        )
    for d in range(1, 16):
        pl.semaphore_signal(
            barrier, 1, device_id=far_id(lax.rem(me_far + d, 16)), device_id_type=MESH
        )
    up, down = (core == 1) & (slab < 31), (core == 0) & (slab > 0)

    @pl.when(up)
    def _():
        pl.semaphore_signal(barrier, 1, device_id=slab_id(slab + 1), device_id_type=MESH)

    @pl.when(down)
    def _():
        pl.semaphore_signal(barrier, 1, device_id=slab_id(slab - 1), device_id_type=MESH)

    live_rows = count[0, 0]
    block = 128

    def live_at(t):
        row = lax.broadcasted_iota(jnp.int32, (block, C), 0) + t * block
        return row < live_rows

    def rows_at(t):
        return pl.ds(pl.multiple_of(t * block, block), block)

    def fold(a):
        return jnp.sum(a.reshape(block // 8, 8, C), axis=0)

    def first_sums(t, sums):
        zval = pre[rows_at(t), :].astype(f32)
        zlive = jnp.where(live_at(t), zval, 0.0)
        return sums[0] + fold(zlive), sums[1] + fold(zlive * zval)

    zero = jnp.zeros((8, C), f32)
    line = lax.broadcasted_iota(jnp.int32, (8, C), 0)

    def stacked(a, b, c):
        a, b = jnp.sum(a, axis=0, keepdims=True), jnp.sum(b, axis=0, keepdims=True)
        return jnp.where(line == 0, a, jnp.where(line == 1, b, jnp.where(line == 2, c, 0.0)))

    def exchange(slots, me, size, sems, turn, ids):
        copies = []
        for d in range(1, size):
            copies.append(
                pltpu.make_async_remote_copy(
                    src_ref=slots.at[turn, me],
                    dst_ref=slots.at[turn, me],
                    send_sem=sems.at[turn, 0, d - 1],
                    recv_sem=sems.at[turn, 1, d - 1],
                    device_id=ids(lax.rem(me + d, size)),
                    device_id_type=MESH,
                )
            )
            copies[-1].start()
        return copies

    def add_up(slots, size, turn, copies):
        for copy in copies:
            copy.wait_recv()
        total = slots[turn, 0]
        for i in range(1, size):
            total = total + slots[turn, i]
        return total

    def all_sum(turn, value, meanwhile):
        near[turn, me_near] = value
        one = exchange(near, me_near, 8, near_sem, turn, near_id)
        meanwhile()
        far[turn, me_far] = add_up(near, 8, turn, one)
        two = exchange(far, me_far, 16, far_sem, turn, far_id)
        total = add_up(far, 16, turn, two)
        for copy in one + two:
            copy.wait_send()
        return total

    def when(cond, act):
        @pl.when(cond)
        def _():
            act()

    has_right, has_left, has_next, has_last = x < 3, x > 0, slab < 31, slab > 0

    def note(source, target, n, device):
        return pltpu.make_async_remote_copy(
            src_ref=source,
            dst_ref=target,
            send_sem=note_sem.at[0, n],
            recv_sem=note_sem.at[1, n],
            device_id=device,
            device_id_type=MESH,
        )

    def note_to_right():
        return note(note_own, note_left, 0, {"gy": x + 1})

    def note_to_left():
        return note(note_own, note_right, 1, {"gy": x - 1})

    def note_ahead():
        return note(note_out, note_in, 2, slab_id(slab + 1))

    def blank(ref):
        ref[...] = jnp.zeros_like(ref)

    def notes_first():
        size = jnp.sum(jnp.where(border[...] < R, 1, 0), axis=1, keepdims=True)
        first = jnp.minimum(jnp.maximum(size - WIN, 0) // 16, (HB - HIGH) // 16)
        note_own[...] = jnp.broadcast_to(first, (8, 128))
        when(~has_left, lambda: blank(note_left))
        when(~has_right, lambda: blank(note_right))
        when(~has_last, lambda: blank(note_in))

    def notes_second():
        when(has_left, lambda: note_to_right().wait_recv())
        when(has_right, lambda: note_to_left().wait_recv())
        row = lax.broadcasted_iota(jnp.int32, (8, 128), 0)
        note_out[...] = jnp.where(
            row == 0, note_left[...], jnp.where(row == 1, note_own[...], note_right[...])
        )
        when(has_next, lambda: note_ahead().start())

    def plan():
        loads[5].wait()
        when(has_last, lambda: note_ahead().wait_recv())
        moved = [note_in[b : b + 1, :] * 16 for b in range(3)]
        lane = lax.broadcasted_iota(jnp.int32, (1, 128), 1)
        third = lax.rem(lane, 3)

        @pl.loop(0, R // SUB)
        def _(j):
            at = pl.ds(pl.multiple_of(j * SUB, SUB), SUB)
            idx = links[:, 0, at]
            for b in range(3):
                inside = (idx >= seg(b)) & (idx < seg(b + 1))
                idx = jnp.where(inside, idx - moved[b], idx)
            idx = jnp.where(idx < NROW, idx, jnp.int32(FAR)).astype(f32)
            idx = jnp.concatenate([idx, jnp.full((101, SUB), FAR, f32)], axis=0).T
            columns[at, :] = idx
            begin = []
            for w in range(3):
                low = jnp.min(idx, axis=0, keepdims=True)
                low = jnp.minimum(low, jnp.minimum(pltpu.roll(low, 127, 1), pltpu.roll(low, 126, 1)))
                low = jnp.where(
                    third == 0,
                    low,
                    jnp.where(third == 1, pltpu.roll(low, 1, 1), pltpu.roll(low, 2, 1)),
                )
                start = jnp.where(low < NROW, jnp.floor(low * 0.0625) * 16.0, FAR)
                idx = jnp.where(idx >= start + WIN, idx, FAR)
                begin.append(jnp.minimum(start, float(NROW)) if w < 2 else start)
            begin = [jnp.broadcast_to(b, (8, 128)) for b in begin]
            row = lax.broadcasted_iota(jnp.int32, (8, 128), 0)
            begin = jnp.where(row == 0, begin[0], jnp.where(row == 1, begin[1], begin[2]))
            starts[pl.ds(pl.multiple_of(j * 8, 8), 8), :] = begin.astype(jnp.int32)

    def choose():
        lane = lax.broadcasted_iota(jnp.int32, (128, 128), 1)
        for t in range(6):
            width = min(128, HB - t * 128)
            names = border[:, t * 128 : t * 128 + width].astype(f32)
            if width < 128:
                names = jnp.concatenate([names, jnp.full((1, 128 - width), FAR, f32)], axis=1)
            names = jnp.broadcast_to(names, (128, 128)).T[:width]
            for c in range(R // 128):
                row = (lane[:width] + c * 128).astype(f32)
                pick[t * 128 : t * 128 + width, c * 128 : (c + 1) * 128] = jnp.where(
                    names == row, 1.0, 0.0
                ).astype(jnp.bfloat16)

        def clear(at, size):
            table[at : at + size, :] = jnp.zeros((size, C), jnp.bfloat16)

        clear(NROW, WIN)

        @pl.when(slab == 0)
        def _():
            for b in (0, 1, 2):
                clear(seg(b), HIGH)

        @pl.when(slab == 31)
        def _():
            for b in (6, 7, 8):
                clear(seg(b), WIN)

        for b in (0, 1, 2):
            clear(seg(b) + HIGH, HB - HIGH)

        for b in (6, 7, 8):
            clear(seg(b) + WIN, HB - WIN)

        for edge, db, missing in ((0, 0, list_left), (3, 2, list_right)):
            @pl.when(x == edge)
            def _():
                blank(missing)

                @pl.when(slab > 0)
                def _():
                    clear(seg(db), HIGH)

                @pl.when(slab < 31)
                def _():
                    clear(seg(6 + db), WIN)

    loads[0].wait()
    sum_z, sum_sq = lax.fori_loop(0, R // block, first_sums, (zero, zero))
    loads[1].wait()
    notes_first()
    extra = jnp.where(up | down, 1, 0)
    pl.semaphore_wait(barrier, 22 + extra)
    when(has_right, lambda: note_to_right().start())
    when(has_left, lambda: note_to_left().start())

    def during_first():
        choose()
        notes_second()

    whole = all_sum(0, stacked(sum_z, sum_sq, live_rows.astype(f32)), during_first)
    amount = whole[2:3]
    mean = whole[0:1] / amount
    var = whole[1:2] / amount - mean * mean
    rstd = lax.rsqrt(var + 1e-05)
    for load in loads[2:5]:
        load.wait()
    gain, shift = gamma[...], beta[...]

    def second_sums(t, sums):
        zhat = (pre[rows_at(t), :].astype(f32) - mean) * rstd
        act = gain * zhat + shift
        sig = jax.nn.sigmoid(act)
        g = cot[rows_at(t), :].astype(f32) * sig * (1.0 + act * (1.0 - sig))
        g = jnp.where(live_at(t), g, 0.0)
        grad[rows_at(t), :] = g
        return sums[0] + fold(g), sums[1] + fold(g * zhat)

    sum_g, sum_gz = lax.fori_loop(0, R // block, second_sums, (zero, zero))
    whole = all_sum(1, stacked(sum_g, sum_gz, 0.0), plan)
    sums[0] = whole[0:1]
    sums[1] = whole[1:2]
    scale = gain * rstd
    part_g, part_gz = whole[0:1] / amount, whole[1:2] / amount

    @pl.loop(0, R // block)
    def _(t):
        zhat = (pre[rows_at(t), :].astype(f32) - mean) * rstd
        dz = scale * (grad[rows_at(t), :] - part_g - zhat * part_gz)
        table[rows_at(t), :] = jnp.where(live_at(t), dz, 0.0).astype(jnp.bfloat16)

    @pl.loop(0, 4)
    def _(t):
        at = pl.multiple_of(t * 176, 16)
        rows = dot(pick[pl.ds(at, 176), :], table[0:R, :], ((1,), (0,)))
        list_own[pl.ds(at, 176), :] = rows.astype(jnp.bfloat16)

    def hop(source, target, n, device):
        return pltpu.make_async_remote_copy(
            src_ref=source,
            dst_ref=target,
            send_sem=halo_sem.at[0, n],
            recv_sem=halo_sem.at[1, n],
            device_id=device,
            device_id_type=MESH,
        )

    lists = (list_left, list_own, list_right)

    def right():
        return hop(list_own, list_left, 3, {"gy": x + 1})

    def left():
        return hop(list_own, list_right, 5, {"gy": x - 1})

    def ahead(db):
        return hop(high.at[db], table.at[pl.ds(seg(db), HIGH), :], db, slab_id(slab + 1))

    def behind(db):
        target = table.at[pl.ds(seg(6 + db), WIN), :]
        return hop(lists[db].at[pl.ds(0, WIN), :], target, 6 + db, slab_id(slab - 1))

    def pass_on(db, mark):
        at = jnp.max(mark[...]) * 16
        high[db] = lists[db][pl.ds(at, HIGH), :]
        when(has_next, lambda: ahead(db).start())
        when(has_last, lambda: behind(db).start())

    when(has_right, lambda: right().start())
    when(has_left, lambda: left().start())
    pass_on(1, note_own)
    table[seg(4) : seg(5), :] = list_own[...]
    loads[6].wait()
    for t in range(8):
        feat_t[:, t * 256 : (t + 1) * 256] = feat[t * 256 : (t + 1) * 256, :].T
    loads[7].wait()
    for db, there, came, mark in (
        (0, has_left, right, note_left),
        (2, has_right, left, note_right),
    ):
        when(there, lambda: came().wait_recv())
        when(there, lambda: pass_on(db, mark))
        table[seg(3 + db) : seg(4 + db), :] = lists[db][...]

    @pl.loop(0, 9)
    def _(g):
        for i in range(3):
            turned[g, i * C : (i + 1) * C, :] = weight[g * 3 + i].T

    for db, there in ((1, True), (0, has_left), (2, has_right)):
        when(has_last & there, lambda: ahead(db).wait_recv())
        when(has_next & there, lambda: behind(db).wait_recv())
    when(has_right, lambda: right().wait_send())
    when(has_left, lambda: left().wait_send())
    for db, there in ((1, True), (0, has_left), (2, has_right)):
        when(has_next & there, lambda: ahead(db).wait_send())
        when(has_last & there, lambda: behind(db).wait_send())
    when(has_right, lambda: note_to_right().wait_send())
    when(has_left, lambda: note_to_left().wait_send())
    when(has_next, lambda: note_ahead().wait_send())


def front(counts, *arrays):
    vmem = pl.BlockSpec(memory_space=pltpu.VMEM)
    return pl.pallas_call(
        front_kernel,
        out_shape=(
            jax.ShapeDtypeStruct((ROWS, C), jnp.bfloat16),
            jax.ShapeDtypeStruct((R, 128), jnp.float32),
            jax.ShapeDtypeStruct((R // SUB * 8, 128), jnp.int32),
            jax.ShapeDtypeStruct((2, 1, C), jnp.float32),
            jax.ShapeDtypeStruct((C, R), jnp.bfloat16),
            jax.ShapeDtypeStruct((9, 3 * C, C), jnp.bfloat16),
        ),
        in_specs=[pl.BlockSpec(memory_space=pltpu.SMEM)]
        + [pl.BlockSpec(memory_space=pltpu.HBM)] * 8,
        out_specs=(vmem,) * 6,
        scratch_shapes=[pltpu.VMEM(a.shape, a.dtype) for a in arrays]
        + [
            pltpu.VMEM((R, C), jnp.float32),
            pltpu.VMEM((HB, R), jnp.bfloat16),
            pltpu.VMEM((2, 8, 8, C), jnp.float32),
            pltpu.VMEM((2, 16, 8, C), jnp.float32),
            pltpu.VMEM((HB, C), jnp.bfloat16),
            pltpu.VMEM((HB, C), jnp.bfloat16),
            pltpu.VMEM((HB, C), jnp.bfloat16),
            pltpu.VMEM((3, HIGH, C), jnp.bfloat16),
            *[pltpu.VMEM((8, 128), jnp.int32)] * 5,
            pltpu.SemaphoreType.DMA((8,)),
            pltpu.SemaphoreType.DMA((2, 2, 7)),
            pltpu.SemaphoreType.DMA((2, 2, 15)),
            pltpu.SemaphoreType.DMA((2, 9)),
            pltpu.SemaphoreType.DMA((2, 3)),
        ],
        compiler_params=pltpu.CompilerParams(
            collective_id=0, has_side_effects=True, vmem_limit_bytes=24 * 1024 * 1024
        ),
        cost_estimate=pl.CostEstimate(
            flops=1_000_000_000, bytes_accessed=10_000_000, transcendentals=1_000_000
        ),
        name="front",
    )(counts, *[pltpu.with_memory_space_constraint(a, pltpu.HBM) for a in arrays])


def body(features, pre_norm, out_grad, weight, gamma, beta, neighbors, boundary, counts):
    table, columns, starts, sums, feat_t, turned = front(
        counts,
        pre_norm[0, 0],
        out_grad[0, 0],
        gamma[None],
        beta[None],
        neighbors.reshape(27, 1, R),
        boundary.reshape(1, HB),
        features[0, 0],
        weight,
    )
    in_grad, local_wgrad, gamma_grad, beta_grad = convolve(
        starts, columns, table, feat_t, turned, sums
    )
    weight_grad = scatter_sum(local_wgrad)
    return (in_grad[None, None], weight_grad, gamma_grad[0], beta_grad[0])


def solution(mesh):
    torus = Mesh(mesh.devices.reshape(4, 4, 2, mesh.shape["gy"]), ("gx_0", "gx_1", "gx_2", "gy"))
    return jax.shard_map(
        body,
        mesh=torus,
        in_specs=(
            P(GX, "gy", None, None),
            P(GX, "gy", None, None),
            P(GX, "gy", None, None),
            P(),
            P(),
            P(),
            P(GX, "gy", None, None),
            P(GX, "gy", None),
            P(GX, "gy"),
        ),
        out_specs=(P(GX, "gy", None, None), P(GX_GY, None), P(), P()),
        check_vma=False,
    )
```

```python
import jax
import jax.numpy as jnp
from jax import lax
from jax.experimental import pallas as pl
from jax.experimental.pallas import tpu as pltpu
from jax.sharding import Mesh
from jax.sharding import PartitionSpec as P

GX_GY = ("gx_0", "gx_1", "gx_2", "gy")
GX = ("gx_0", "gx_1", "gx_2")
MESH = pl.DeviceIdType.MESH


C = 256
R = 2048
SUB = 128
WIN = 256
NROW = 8384
FAR = 1.0e6


def dot(a, b, dims):
    return lax.dot_general(a, b, (dims, ((), ())), preferred_element_type=jnp.float32)


def one_hot(columns, start):
    lanes = lax.broadcasted_iota(jnp.int32, (SUB, WIN), 1).astype(jnp.float32)
    place = columns - start.astype(jnp.float32)
    return jnp.where(place == lanes, 1.0, 0.0).astype(jnp.bfloat16)

def conv_kernel(
    starts, idx, table, feat_t, turned, sums_in, in_grad, wgrad, gamma_grad, beta_grad,
    acc, picked,
):
    acc[...] = jnp.zeros_like(acc)
    beta_grad[...] = sums_in[0]
    gamma_grad[...] = sums_in[1]

    @pl.loop(0, 9)
    def _(step):
        conv_group(step, starts, idx, table, feat_t, turned, wgrad, acc, picked)

    in_grad[...] = acc[...].astype(jnp.bfloat16)


def conv_group(step, starts, idx, table, feat_t, turned, wgrad, acc, picked):
    lane0 = 24 - 3 * step

    def columns_at(row):
        columns = pltpu.roll(idx[pl.ds(row, SUB), :], 128 - lane0, 1)
        return columns

    def window(columns, start):
        hot = [
            one_hot(jnp.broadcast_to(columns[:, 2 - i : 3 - i], (SUB, WIN)), start)
            for i in range(3)
        ]
        return jnp.concatenate(hot, axis=0)

    def gather(j):
        row = j * SUB
        columns = columns_at(row)
        s = [pl.multiple_of(starts[j * 8 + w, lane0], 16) for w in range(2)]
        hots = [window(columns, a) for a in s]
        tabs = [table[pl.ds(a, WIN), :] for a in s]
        total = dot(jnp.concatenate(hots, axis=1), jnp.concatenate(tabs, axis=0), ((1,), (0,)))
        total = total.astype(jnp.bfloat16)
        for i in range(3):
            picked[pl.ds(row, SUB), i * C : (i + 1) * C] = total[i * SUB : (i + 1) * SUB]

    def gather_rest(j):
        row = j * SUB

        def more(start):
            columns = columns_at(row)
            start = pl.multiple_of(start, 16)
            part = dot(window(columns, start), table[pl.ds(start, WIN), :], ((1,), (0,)))
            part = part.astype(jnp.bfloat16)
            for i in range(3):
                picked[pl.ds(row, SUB), i * C : (i + 1) * C] += part[i * SUB : (i + 1) * SUB]
            lane = lax.broadcasted_iota(jnp.int32, (SUB, 128), 1)
            ahead = (lane < 3) & (columns >= (start + WIN).astype(jnp.float32))
            low = jnp.min(jnp.where(ahead, columns, FAR)).astype(jnp.int32)
            return jnp.where(low < NROW, low // 16 * 16, jnp.int32(FAR))

        lax.while_loop(lambda start: start < NROW, more, starts[j * 8 + 2, lane0])

    for j in range(R // SUB):
        gather(j)

    @pl.when(starts[3, lane0] < NROW)
    def _():
        for j in range(R // SUB):
            gather_rest(j)

    for i in range(3):
        wgrad[step * 3 + i] = dot(feat_t[...], picked[:, i * C : (i + 1) * C], ((1,), (0,)))
    acc[...] += dot(picked[...], turned[step], ((1,), (0,)))


def convolve(starts, idx, table, feat_t, turned, sums):
    whole = pl.BlockSpec(memory_space=pltpu.VMEM)
    in_grad, wgrad, gamma_grad, beta_grad = pl.pallas_call(
        conv_kernel,
        out_shape=(
            jax.ShapeDtypeStruct((R, C), jnp.bfloat16),
            jax.ShapeDtypeStruct((27, C, C), jnp.float32),
            jax.ShapeDtypeStruct((1, C), jnp.float32),
            jax.ShapeDtypeStruct((1, C), jnp.float32),
        ),
        in_specs=[
            pl.BlockSpec(memory_space=pltpu.SMEM),
            whole,
            whole,
            whole,
            whole,
            whole,
        ],
        out_specs=(whole,) * 4,
        scratch_shapes=[
            pltpu.VMEM((R, C), jnp.float32),
            pltpu.VMEM((R, 3 * C), jnp.bfloat16),
        ],
        compiler_params=pltpu.CompilerParams(vmem_limit_bytes=28 * 1024 * 1024),
        cost_estimate=pl.CostEstimate(
            flops=30_000_000_000, bytes_accessed=20_000_000, transcendentals=0
        ),
        name="conv_backward",
    )(starts, idx, table, feat_t, turned, sums)
    return in_grad, wgrad.reshape(27 * C, C), gamma_grad, beta_grad


AXES = ("gy", "gx_1", "gx_0")
TILE_AT = (0, 16, 32, 38)
HOLDS = (((0, 0), (0, 1), (3, 0)), ((1, 0), (1, 1), (3, 1)), ((2, 0), (2, 1)))


def scatter_kernel(part, out, s_a, r_a, *rest):
    s_b, r_b, s_c, r_c, s_d, r_d = (rest[3 * i : 3 * i + 3] for i in range(6))
    a_sem, b_sem, c_sem, d_sem = rest[18:]
    pos = [lax.axis_index(a) for a in AXES]
    core = lax.axis_index("gx_2")
    z = pos[2]

    def around(i):
        return lax.rem(z + 1 + i, 4)

    barrier = pltpu.get_barrier_semaphore()
    pl.semaphore_signal(barrier, 1, device_id={"gx_2": 1 - core}, device_id_type=MESH)
    for axis, at in zip(AXES, pos):
        for d in range(1, 4):
            peer = {axis: lax.rem(at + d, 4)}
            pl.semaphore_signal(barrier, 1, device_id=peer, device_id_type=MESH)

    def block(i, y, x, side, t):
        skip = (x * 54 + TILE_AT[t]) % 8
        base = around(i) * 1728 + (y * 2 + side) * 216 + x * 54 + TILE_AT[t] - skip
        rows = part[pl.ds(pl.multiple_of(base, 8), 24 if skip else 16), :]
        return rows[skip : skip + 16]

    sends = []

    def send(src, dst, sems, at, device):
        copy = pltpu.make_async_remote_copy(
            src_ref=src,
            dst_ref=dst,
            send_sem=sems.at[(0,) + at],
            recv_sem=sems.at[(1,) + at],
            device_id=device,
            device_id_type=MESH,
        )
        copy.start()
        sends.append(copy)
        return copy

    first = []
    for i in range(4):
        @pl.loop(0, 4)
        def _(y):
            for x in range(4):
                for t in range(4):
                    mine = block(i, y, x, 1 - core, t)
                    s_a[i, y * 4 + x, t] = mine.astype(jnp.bfloat16)

        if i == 0:
            pl.semaphore_wait(barrier, 10)
        first.append(send(s_a.at[i], r_a.at[i], a_sem, (i,), {"gx_2": 1 - core}))

    def spread(p, stage, sems, src, dst):
        axis = (p + stage) % 3
        return [
            send(
                src.at[lax.rem(pos[axis] + d, 4)],
                dst.at[d - 1],
                sems,
                (p, d - 1),
                {AXES[axis]: lax.rem(pos[axis] + d, 4)},
            )
            for d in range(1, 4)
        ]

    second = [None, None, []]
    for i in range(4):
        first[i].wait_recv()
        z_of = around(i)

        @pl.loop(0, 4)
        def _(y):
            for x in range(4):
                for t in range(4):
                    both = block(i, y, x, core, t) + r_a[i, y * 4 + x, t].astype(jnp.float32)
                    both = both.astype(jnp.bfloat16)
                    for p, holds in enumerate(HOLDS):
                        for n, (tile, side) in enumerate(holds):
                            if tile != t:
                                continue
                            piece = both[:, side * 128 : (side + 1) * 128]
                            if p == 0:
                                s_b[0][x, y * 4 + z_of, n] = piece
                            elif p == 1:
                                s_b[1][y, z_of * 4 + x, n] = piece
                            else:
                                s_b[2][z_of, x * 4 + y, n] = piece

        if i < 3:
            second[2].append(
                send(s_b[2].at[z_of], r_b[2].at[i], b_sem, (2, i), {"gx_0": z_of})
            )
    for p in range(2):
        second[p] = spread(p, 0, b_sem, s_b[p], r_b[p])

    def total(own, came, at):
        kind = jnp.float32
        return (own[at].astype(kind) + came[(0,) + at[1:]].astype(kind)) + (
            came[(1,) + at[1:]].astype(kind) + came[(2,) + at[1:]].astype(kind)
        )

    third = []
    for p in range(3):
        for copy in second[p]:
            copy.wait_recv()
        me = pos[p]

        @pl.loop(0, 16)
        def _(j):
            for t in range(len(HOLDS[p])):
                s_c[p][j // 4, j % 4, t] = total(s_b[p], r_b[p], (me, j, t)).astype(jnp.bfloat16)

        third.append(spread(p, 1, c_sem, s_c[p], r_c[p]))

    fourth = []
    for p in range(3):
        for copy in third[p]:
            copy.wait_recv()
        me = pos[(p + 1) % 3]

        @pl.loop(0, 4)
        def _(j):
            for t in range(len(HOLDS[p])):
                s_d[p][j, t] = total(s_c[p], r_c[p], (me, j, t))

        fourth.append(spread(p, 2, d_sem, s_d[p], r_d[p]))

    for p in range(3):
        for copy in fourth[p]:
            copy.wait_recv()
        me = pos[(p + 2) % 3]
        for n, (tile, side) in enumerate(HOLDS[p]):
            rows = pl.ds(TILE_AT[tile], 16)
            out[rows, side * 128 : (side + 1) * 128] = total(s_d[p], r_d[p], (me, n))

    for copy in sends:
        copy.wait_send()


def scatter_sum(part):
    def stage(lead, kind):
        return [pltpu.VMEM(lead + (len(h), 16, 128), kind) for h in HOLDS]

    half, full = jnp.bfloat16, jnp.float32
    return pl.pallas_call(
        scatter_kernel,
        out_shape=jax.ShapeDtypeStruct((54, C), jnp.float32),
        in_specs=[pl.BlockSpec(memory_space=pltpu.VMEM)],
        out_specs=pl.BlockSpec(memory_space=pltpu.VMEM),
        scratch_shapes=[
            pltpu.VMEM((4, 16, 4, 16, C), jnp.bfloat16),
            pltpu.VMEM((4, 16, 4, 16, C), jnp.bfloat16),
            *stage((4, 16), half),
            *stage((3, 16), half),
            *stage((4, 4), half),
            *stage((3, 4), half),
            *stage((4,), full),
            *stage((3,), full),
            pltpu.SemaphoreType.DMA((2, 4)),
            pltpu.SemaphoreType.DMA((2, 3, 3)),
            pltpu.SemaphoreType.DMA((2, 3, 3)),
            pltpu.SemaphoreType.DMA((2, 3, 3)),
        ],
        compiler_params=pltpu.CompilerParams(
            collective_id=1, has_side_effects=True, vmem_limit_bytes=24 * 1024 * 1024
        ),
        cost_estimate=pl.CostEstimate(flops=10_000_000, bytes_accessed=7_000_000, transcendentals=0),
        name="scatter_sum",
    )(part)


HB = 704
HIGH = 272
ROWS = NROW + WIN


def seg(b):
    return R + b * HB


def front_kernel(
    count, pre_in, cot_in, gamma_in, beta_in, links_in, border_in, feat_in, weight_in,
    table, columns, starts, sums, feat_t, turned,
    pre, cot, gamma, beta, links, border, feat, weight,
    grad, pick, near, far, list_left, list_own, list_right, high,
    note_own, note_left, note_right, note_out, note_in,
    load_sem, near_sem, far_sem, halo_sem, note_sem,
):
    f32 = jnp.float32
    z, y, core, x = (lax.axis_index(a) for a in GX_GY)
    slab = (z * 4 + y) * 2 + core
    me_near, me_far = x * 2 + core, z * 4 + y

    def near_id(p):
        return {"gy": p // 2, "gx_2": lax.rem(p, 2)}

    def far_id(p):
        return {"gx_0": p // 4, "gx_1": lax.rem(p, 4)}

    def slab_id(s):
        return {"gx_0": s // 8, "gx_1": lax.rem(s // 2, 4), "gx_2": lax.rem(s, 2)}

    loads = []
    for source, target in (
        (pre_in, pre),
        (border_in, border),
        (cot_in, cot),
        (gamma_in, gamma),
        (beta_in, beta),
        (links_in, links),
        (feat_in, feat),
        (weight_in, weight),
    ):
        loads.append(pltpu.make_async_copy(source, target, load_sem.at[len(loads)]))
        loads[-1].start()

    barrier = pltpu.get_barrier_semaphore()
    for d in range(1, 8):
        pl.semaphore_signal(
            barrier, 1, device_id=near_id(lax.rem(me_near + d, 8)), device_id_type=MESH
        )
    for d in range(1, 16):
        pl.semaphore_signal(
            barrier, 1, device_id=far_id(lax.rem(me_far + d, 16)), device_id_type=MESH
        )
    up, down = (core == 1) & (slab < 31), (core == 0) & (slab > 0)

    @pl.when(up)
    def _():
        pl.semaphore_signal(barrier, 1, device_id=slab_id(slab + 1), device_id_type=MESH)

    @pl.when(down)
    def _():
        pl.semaphore_signal(barrier, 1, device_id=slab_id(slab - 1), device_id_type=MESH)

    live_rows = count[0, 0]
    block = 128

    def live_at(t):
        row = lax.broadcasted_iota(jnp.int32, (block, C), 0) + t * block
        return row < live_rows

    def rows_at(t):
        return pl.ds(pl.multiple_of(t * block, block), block)

    def fold(a):
        return jnp.sum(a.reshape(block // 8, 8, C), axis=0)

    def first_sums(t, sums):
        zval = pre[rows_at(t), :].astype(f32)
        zlive = jnp.where(live_at(t), zval, 0.0)
        return sums[0] + fold(zlive), sums[1] + fold(zlive * zval)

    zero = jnp.zeros((8, C), f32)
    line = lax.broadcasted_iota(jnp.int32, (8, C), 0)

    def stacked(a, b, c):
        a, b = jnp.sum(a, axis=0, keepdims=True), jnp.sum(b, axis=0, keepdims=True)
        return jnp.where(line == 0, a, jnp.where(line == 1, b, jnp.where(line == 2, c, 0.0)))

    def exchange(slots, me, size, sems, turn, ids):
        copies = []
        for d in range(1, size):
            copies.append(
                pltpu.make_async_remote_copy(
                    src_ref=slots.at[turn, me],
                    dst_ref=slots.at[turn, me],
                    send_sem=sems.at[turn, 0, d - 1],
                    recv_sem=sems.at[turn, 1, d - 1],
                    device_id=ids(lax.rem(me + d, size)),
                    device_id_type=MESH,
                )
            )
            copies[-1].start()
        return copies

    def add_up(slots, size, turn, copies):
        for copy in copies:
            copy.wait_recv()
        total = slots[turn, 0]
        for i in range(1, size):
            total = total + slots[turn, i]
        return total

    def all_sum(turn, value, meanwhile):
        near[turn, me_near] = value
        one = exchange(near, me_near, 8, near_sem, turn, near_id)
        meanwhile()
        far[turn, me_far] = add_up(near, 8, turn, one)
        two = exchange(far, me_far, 16, far_sem, turn, far_id)
        total = add_up(far, 16, turn, two)
        for copy in one + two:
            copy.wait_send()
        return total

    def when(cond, act):
        @pl.when(cond)
        def _():
            act()

    has_right, has_left, has_next, has_last = x < 3, x > 0, slab < 31, slab > 0

    def note(source, target, n, device):
        return pltpu.make_async_remote_copy(
            src_ref=source,
            dst_ref=target,
            send_sem=note_sem.at[0, n],
            recv_sem=note_sem.at[1, n],
            device_id=device,
            device_id_type=MESH,
        )

    def note_to_right():
        return note(note_own, note_left, 0, {"gy": x + 1})

    def note_to_left():
        return note(note_own, note_right, 1, {"gy": x - 1})

    def note_ahead():
        return note(note_out, note_in, 2, slab_id(slab + 1))

    def blank(ref):
        ref[...] = jnp.zeros_like(ref)

    def notes_first():
        size = jnp.sum(jnp.where(border[...] < R, 1, 0), axis=1, keepdims=True)
        first = jnp.minimum(jnp.maximum(size - WIN, 0) // 16, (HB - HIGH) // 16)
        note_own[...] = jnp.broadcast_to(first, (8, 128))
        when(~has_left, lambda: blank(note_left))
        when(~has_right, lambda: blank(note_right))
        when(~has_last, lambda: blank(note_in))

    def notes_second():
        when(has_left, lambda: note_to_right().wait_recv())
        when(has_right, lambda: note_to_left().wait_recv())
        row = lax.broadcasted_iota(jnp.int32, (8, 128), 0)
        note_out[...] = jnp.where(
            row == 0, note_left[...], jnp.where(row == 1, note_own[...], note_right[...])
        )
        when(has_next, lambda: note_ahead().start())

    def plan(part, spare):
        moved = [note_in[b : b + 1, :] * 16 for b in range(3)]
        lane = lax.broadcasted_iota(jnp.int32, (1, 128), 1)
        third = lax.rem(lane, 3)

        def one(j, spare):
            at = pl.ds(pl.multiple_of(j * SUB, SUB), SUB)
            idx = links[:, 0, at]
            for b in range(3):
                inside = (idx >= seg(b)) & (idx < seg(b + 1))
                idx = jnp.where(inside, idx - moved[b], idx)
            idx = jnp.where(idx < NROW, idx, jnp.int32(FAR)).astype(f32)
            idx = jnp.concatenate([idx, jnp.full((101, SUB), FAR, f32)], axis=0).T
            columns[at, :] = idx
            begin = []
            for w in range(3):
                low = jnp.min(idx, axis=0, keepdims=True)
                low = jnp.minimum(low, jnp.minimum(pltpu.roll(low, 127, 1), pltpu.roll(low, 126, 1)))
                low = jnp.where(
                    third == 0,
                    low,
                    jnp.where(third == 1, pltpu.roll(low, 1, 1), pltpu.roll(low, 2, 1)),
                )
                start = jnp.where(low < NROW, jnp.floor(low * 0.0625) * 16.0, FAR)
                idx = jnp.where(idx >= start + WIN, idx, FAR)
                begin.append(jnp.minimum(start, float(NROW)) if w < 2 else start)
            spare = jnp.minimum(spare, begin[2])
            begin = [jnp.broadcast_to(b, (8, 128)) for b in begin]
            row = lax.broadcasted_iota(jnp.int32, (8, 128), 0)
            begin = jnp.where(row == 0, begin[0], jnp.where(row == 1, begin[1], begin[2]))
            starts[pl.ds(pl.multiple_of(j * 8, 8), 8), :] = begin.astype(jnp.int32)
            return spare

        def some(n, spare):
            for u in range(4):
                spare = one(part * 8 + n * 4 + u, spare)
            return spare

        return lax.fori_loop(0, 2, some, spare)

    def choose():
        lane = lax.broadcasted_iota(jnp.int32, (128, 128), 1)
        for t in range(6):
            width = min(128, HB - t * 128)
            names = border[:, t * 128 : t * 128 + width].astype(f32)
            if width < 128:
                names = jnp.concatenate([names, jnp.full((1, 128 - width), FAR, f32)], axis=1)
            names = jnp.broadcast_to(names, (128, 128)).T[:width]
            for c in range(R // 128):
                row = (lane[:width] + c * 128).astype(f32)
                pick[t * 128 : t * 128 + width, c * 128 : (c + 1) * 128] = jnp.where(
                    names == row, 1.0, 0.0
                ).astype(jnp.bfloat16)

        def clear(at, size):
            table[at : at + size, :] = jnp.zeros((size, C), jnp.bfloat16)

        clear(NROW, WIN)

        @pl.when(slab == 0)
        def _():
            for b in (0, 1, 2):
                clear(seg(b), HIGH)

        @pl.when(slab == 31)
        def _():
            for b in (6, 7, 8):
                clear(seg(b), WIN)

        for b in (0, 1, 2):
            clear(seg(b) + HIGH, HB - HIGH)

        for b in (6, 7, 8):
            clear(seg(b) + WIN, HB - WIN)

        for edge, db, missing in ((0, 0, list_left), (3, 2, list_right)):
            @pl.when(x == edge)
            def _():
                blank(missing)

                @pl.when(slab > 0)
                def _():
                    clear(seg(db), HIGH)

                @pl.when(slab < 31)
                def _():
                    clear(seg(6 + db), WIN)

    loads[0].wait()
    sum_z, sum_sq = lax.fori_loop(0, R // block, first_sums, (zero, zero))
    loads[1].wait()
    notes_first()
    extra = jnp.where(up | down, 1, 0)
    pl.semaphore_wait(barrier, 22 + extra)
    when(has_right, lambda: note_to_right().start())
    when(has_left, lambda: note_to_left().start())

    def during_first():
        choose()
        notes_second()

    whole = all_sum(0, stacked(sum_z, sum_sq, live_rows.astype(f32)), during_first)
    amount = whole[2:3]
    mean = whole[0:1] / amount
    var = whole[1:2] / amount - mean * mean
    rstd = lax.rsqrt(var + 1e-05)
    for load in loads[2:5]:
        load.wait()
    gain, shift = gamma[...], beta[...]

    def during_second():
        loads[6].wait()
        for t in range(8):
            feat_t[:, t * 256 : (t + 1) * 256] = feat[t * 256 : (t + 1) * 256, :].T
        loads[5].wait()
        when(has_last, lambda: note_ahead().wait_recv())

    def second_sums(t, sums):
        zhat = (pre[rows_at(t), :].astype(f32) - mean) * rstd
        act = gain * zhat + shift
        sig = jax.nn.sigmoid(act)
        g = cot[rows_at(t), :].astype(f32) * sig * (1.0 + act * (1.0 - sig))
        g = jnp.where(live_at(t), g, 0.0)
        grad[rows_at(t), :] = g
        return sums[0] + fold(g), sums[1] + fold(g * zhat)

    sum_g, sum_gz = lax.fori_loop(0, R // block, second_sums, (zero, zero))
    whole = all_sum(1, stacked(sum_g, sum_gz, 0.0), during_second)
    sums[0] = whole[0:1]
    sums[1] = whole[1:2]
    scale = gain * rstd
    part_g, part_gz = whole[0:1] / amount, whole[1:2] / amount

    @pl.loop(0, R // block)
    def _(t):
        zhat = (pre[rows_at(t), :].astype(f32) - mean) * rstd
        dz = scale * (grad[rows_at(t), :] - part_g - zhat * part_gz)
        table[rows_at(t), :] = jnp.where(live_at(t), dz, 0.0).astype(jnp.bfloat16)

    @pl.loop(0, 4)
    def _(t):
        at = pl.multiple_of(t * 176, 16)
        rows = dot(pick[pl.ds(at, 176), :], table[0:R, :], ((1,), (0,)))
        list_own[pl.ds(at, 176), :] = rows.astype(jnp.bfloat16)

    def hop(source, target, n, device):
        return pltpu.make_async_remote_copy(
            src_ref=source,
            dst_ref=target,
            send_sem=halo_sem.at[0, n],
            recv_sem=halo_sem.at[1, n],
            device_id=device,
            device_id_type=MESH,
        )

    lists = (list_left, list_own, list_right)

    def right():
        return hop(list_own, list_left, 3, {"gy": x + 1})

    def left():
        return hop(list_own, list_right, 5, {"gy": x - 1})

    def ahead(db):
        return hop(high.at[db], table.at[pl.ds(seg(db), HIGH), :], db, slab_id(slab + 1))

    def behind(db):
        target = table.at[pl.ds(seg(6 + db), WIN), :]
        return hop(lists[db].at[pl.ds(0, WIN), :], target, 6 + db, slab_id(slab - 1))

    def pass_on(db, mark):
        at = jnp.max(mark[...]) * 16
        high[db] = lists[db][pl.ds(at, HIGH), :]
        when(has_next, lambda: ahead(db).start())
        when(has_last, lambda: behind(db).start())

    when(has_right, lambda: right().start())
    when(has_left, lambda: left().start())
    pass_on(1, note_own)
    table[seg(4) : seg(5), :] = list_own[...]
    spare = plan(0, jnp.full((1, 128), FAR, f32))
    loads[7].wait()
    for db, there, came, mark in (
        (0, has_left, right, note_left),
        (2, has_right, left, note_right),
    ):
        when(there, lambda: came().wait_recv())
        when(there, lambda: pass_on(db, mark))
        table[seg(3 + db) : seg(4 + db), :] = lists[db][...]

    spare = plan(1, spare)
    row = lax.broadcasted_iota(jnp.int32, (8, 128), 0)
    starts[0:8, :] = jnp.where(row == 3, spare.astype(jnp.int32), starts[0:8, :])

    @pl.loop(0, 9)
    def _(g):
        for i in range(3):
            turned[g, i * C : (i + 1) * C, :] = weight[g * 3 + i].T

    for db, there in ((1, True), (0, has_left), (2, has_right)):
        when(has_last & there, lambda: ahead(db).wait_recv())
        when(has_next & there, lambda: behind(db).wait_recv())
    when(has_right, lambda: right().wait_send())
    when(has_left, lambda: left().wait_send())
    for db, there in ((1, True), (0, has_left), (2, has_right)):
        when(has_next & there, lambda: ahead(db).wait_send())
        when(has_last & there, lambda: behind(db).wait_send())
    when(has_right, lambda: note_to_right().wait_send())
    when(has_left, lambda: note_to_left().wait_send())
    when(has_next, lambda: note_ahead().wait_send())


def front(counts, *arrays):
    vmem = pl.BlockSpec(memory_space=pltpu.VMEM)
    return pl.pallas_call(
        front_kernel,
        out_shape=(
            jax.ShapeDtypeStruct((ROWS, C), jnp.bfloat16),
            jax.ShapeDtypeStruct((R, 128), jnp.float32),
            jax.ShapeDtypeStruct((R // SUB * 8, 128), jnp.int32),
            jax.ShapeDtypeStruct((2, 1, C), jnp.float32),
            jax.ShapeDtypeStruct((C, R), jnp.bfloat16),
            jax.ShapeDtypeStruct((9, 3 * C, C), jnp.bfloat16),
        ),
        in_specs=[pl.BlockSpec(memory_space=pltpu.SMEM)]
        + [pl.BlockSpec(memory_space=pltpu.HBM)] * 8,
        out_specs=(vmem,) * 6,
        scratch_shapes=[pltpu.VMEM(a.shape, a.dtype) for a in arrays]
        + [
            pltpu.VMEM((R, C), jnp.float32),
            pltpu.VMEM((HB, R), jnp.bfloat16),
            pltpu.VMEM((2, 8, 8, C), jnp.float32),
            pltpu.VMEM((2, 16, 8, C), jnp.float32),
            pltpu.VMEM((HB, C), jnp.bfloat16),
            pltpu.VMEM((HB, C), jnp.bfloat16),
            pltpu.VMEM((HB, C), jnp.bfloat16),
            pltpu.VMEM((3, HIGH, C), jnp.bfloat16),
            *[pltpu.VMEM((8, 128), jnp.int32)] * 5,
            pltpu.SemaphoreType.DMA((8,)),
            pltpu.SemaphoreType.DMA((2, 2, 7)),
            pltpu.SemaphoreType.DMA((2, 2, 15)),
            pltpu.SemaphoreType.DMA((2, 9)),
            pltpu.SemaphoreType.DMA((2, 3)),
        ],
        compiler_params=pltpu.CompilerParams(
            collective_id=0, has_side_effects=True, vmem_limit_bytes=24 * 1024 * 1024
        ),
        cost_estimate=pl.CostEstimate(
            flops=1_000_000_000, bytes_accessed=10_000_000, transcendentals=1_000_000
        ),
        name="front",
    )(counts, *[pltpu.with_memory_space_constraint(a, pltpu.HBM) for a in arrays])


def body(features, pre_norm, out_grad, weight, gamma, beta, neighbors, boundary, counts):
    table, columns, starts, sums, feat_t, turned = front(
        counts,
        pre_norm[0, 0],
        out_grad[0, 0],
        gamma[None],
        beta[None],
        neighbors.reshape(27, 1, R),
        boundary.reshape(1, HB),
        features[0, 0],
        weight,
    )
    in_grad, local_wgrad, gamma_grad, beta_grad = convolve(
        starts, columns, table, feat_t, turned, sums
    )
    weight_grad = scatter_sum(local_wgrad)
    return (in_grad[None, None], weight_grad, gamma_grad[0], beta_grad[0])


def solution(mesh):
    torus = Mesh(mesh.devices.reshape(4, 4, 2, mesh.shape["gy"]), ("gx_0", "gx_1", "gx_2", "gy"))
    return jax.shard_map(
        body,
        mesh=torus,
        in_specs=(
            P(GX, "gy", None, None),
            P(GX, "gy", None, None),
            P(GX, "gy", None, None),
            P(),
            P(),
            P(),
            P(GX, "gy", None, None),
            P(GX, "gy", None),
            P(GX, "gy"),
        ),
        out_specs=(P(GX, "gy", None, None), P(GX_GY, None), P(), P()),
        check_vma=False,
    )
```

```python
import jax
import jax.numpy as jnp
from jax import lax
from jax.experimental import pallas as pl
from jax.experimental.pallas import tpu as pltpu
from jax.sharding import Mesh
from jax.sharding import PartitionSpec as P

GX_GY = ("gx_0", "gx_1", "gx_2", "gy")
GX = ("gx_0", "gx_1", "gx_2")
MESH = pl.DeviceIdType.MESH


C = 256
R = 2048
SUB = 128
WIN = 256
NROW = 8384
FAR = 1.0e6


def dot(a, b, dims):
    return lax.dot_general(a, b, (dims, ((), ())), preferred_element_type=jnp.float32)


def one_hot(columns, start):
    lanes = lax.broadcasted_iota(jnp.int32, (SUB, WIN), 1).astype(jnp.float32)
    place = columns - start.astype(jnp.float32)
    return jnp.where(place == lanes, 1.0, 0.0).astype(jnp.bfloat16)

def conv_kernel(
    starts, idx, table, feat_t, turned, sums_in, in_grad, wgrad, gamma_grad, beta_grad,
    acc, picked,
):
    acc[...] = jnp.zeros_like(acc)
    beta_grad[...] = sums_in[0]
    gamma_grad[...] = sums_in[1]

    @pl.loop(0, 9)
    def _(step):
        conv_group(step, starts, idx, table, feat_t, turned, wgrad, acc, picked)

    in_grad[...] = acc[...].astype(jnp.bfloat16)


def conv_group(step, starts, idx, table, feat_t, turned, wgrad, acc, picked):
    lane0 = 24 - 3 * step

    def columns_at(row):
        columns = pltpu.roll(idx[pl.ds(row, SUB), :], 128 - lane0, 1)
        return columns

    def window(columns, start):
        hot = [
            one_hot(jnp.broadcast_to(columns[:, 2 - i : 3 - i], (SUB, WIN)), start)
            for i in range(3)
        ]
        return jnp.concatenate(hot, axis=0)

    def gather(j):
        row = j * SUB
        columns = columns_at(row)
        s = [pl.multiple_of(starts[j * 8 + w, lane0], 16) for w in range(2)]
        hots = [window(columns, a) for a in s]
        tabs = [table[pl.ds(a, WIN), :] for a in s]
        total = dot(jnp.concatenate(hots, axis=1), jnp.concatenate(tabs, axis=0), ((1,), (0,)))
        total = total.astype(jnp.bfloat16)
        for i in range(3):
            picked[pl.ds(row, SUB), i * C : (i + 1) * C] = total[i * SUB : (i + 1) * SUB]

    def gather_rest(j):
        row = j * SUB

        def more(start):
            columns = columns_at(row)
            start = pl.multiple_of(start, 16)
            part = dot(window(columns, start), table[pl.ds(start, WIN), :], ((1,), (0,)))
            part = part.astype(jnp.bfloat16)
            for i in range(3):
                picked[pl.ds(row, SUB), i * C : (i + 1) * C] += part[i * SUB : (i + 1) * SUB]
            lane = lax.broadcasted_iota(jnp.int32, (SUB, 128), 1)
            ahead = (lane < 3) & (columns >= (start + WIN).astype(jnp.float32))
            low = jnp.min(jnp.where(ahead, columns, FAR)).astype(jnp.int32)
            return jnp.where(low < NROW, low // 16 * 16, jnp.int32(FAR))

        lax.while_loop(lambda start: start < NROW, more, starts[j * 8 + 2, lane0])

    for j in range(R // SUB):
        gather(j)

    @pl.when(starts[3, lane0] < NROW)
    def _():
        for j in range(R // SUB):
            gather_rest(j)

    for i in range(3):
        wgrad[step * 3 + i] = dot(feat_t[...], picked[:, i * C : (i + 1) * C], ((1,), (0,)))
    acc[...] += dot(picked[...], turned[step], ((1,), (0,)))


def convolve(starts, idx, table, feat_t, turned, sums):
    whole = pl.BlockSpec(memory_space=pltpu.VMEM)
    in_grad, wgrad, gamma_grad, beta_grad = pl.pallas_call(
        conv_kernel,
        out_shape=(
            jax.ShapeDtypeStruct((R, C), jnp.bfloat16),
            jax.ShapeDtypeStruct((27, C, C), jnp.float32),
            jax.ShapeDtypeStruct((1, C), jnp.float32),
            jax.ShapeDtypeStruct((1, C), jnp.float32),
        ),
        in_specs=[
            pl.BlockSpec(memory_space=pltpu.SMEM),
            whole,
            whole,
            whole,
            whole,
            whole,
        ],
        out_specs=(whole,) * 4,
        scratch_shapes=[
            pltpu.VMEM((R, C), jnp.float32),
            pltpu.VMEM((R, 3 * C), jnp.bfloat16),
        ],
        compiler_params=pltpu.CompilerParams(vmem_limit_bytes=28 * 1024 * 1024),
        cost_estimate=pl.CostEstimate(
            flops=30_000_000_000, bytes_accessed=20_000_000, transcendentals=0
        ),
        name="conv_backward",
    )(starts, idx, table, feat_t, turned, sums)
    return in_grad, wgrad.reshape(27 * C, C), gamma_grad, beta_grad


AXES = ("gy", "gx_1", "gx_0")
TILE_AT = (0, 16, 32, 38)
HOLDS = (((0, 0), (0, 1), (3, 0)), ((1, 0), (1, 1), (3, 1)), ((2, 0), (2, 1)))


def scatter_kernel(part, out, s_a, r_a, *rest):
    s_b, r_b, s_c, r_c, s_d, r_d = (rest[3 * i : 3 * i + 3] for i in range(6))
    a_sem, b_sem, c_sem, d_sem = rest[18:]
    pos = [lax.axis_index(a) for a in AXES]
    core = lax.axis_index("gx_2")
    z = pos[2]

    def around(i):
        return lax.rem(z + 1 + i, 4)

    barrier = pltpu.get_barrier_semaphore()
    pl.semaphore_signal(barrier, 1, device_id={"gx_2": 1 - core}, device_id_type=MESH)
    for axis, at in zip(AXES, pos):
        for d in range(1, 4):
            peer = {axis: lax.rem(at + d, 4)}
            pl.semaphore_signal(barrier, 1, device_id=peer, device_id_type=MESH)

    def block(i, y, x, side, t):
        skip = (x * 54 + TILE_AT[t]) % 8
        base = around(i) * 1728 + (y * 2 + side) * 216 + x * 54 + TILE_AT[t] - skip
        rows = part[pl.ds(pl.multiple_of(base, 8), 24 if skip else 16), :]
        return rows[skip : skip + 16]

    sends = []

    def send(src, dst, sems, at, device):
        copy = pltpu.make_async_remote_copy(
            src_ref=src,
            dst_ref=dst,
            send_sem=sems.at[(0,) + at],
            recv_sem=sems.at[(1,) + at],
            device_id=device,
            device_id_type=MESH,
        )
        copy.start()
        sends.append(copy)
        return copy

    first = []
    for i in range(4):
        @pl.loop(0, 4)
        def _(y):
            for x in range(4):
                for t in range(4):
                    mine = block(i, y, x, 1 - core, t)
                    s_a[i, y * 4 + x, t] = mine.astype(jnp.bfloat16)

        if i == 0:
            pl.semaphore_wait(barrier, 10)
        first.append(send(s_a.at[i], r_a.at[i], a_sem, (i,), {"gx_2": 1 - core}))

    def spread(p, stage, sems, src, dst):
        axis = (p + stage) % 3
        return [
            send(
                src.at[lax.rem(pos[axis] + d, 4)],
                dst.at[d - 1],
                sems,
                (p, d - 1),
                {AXES[axis]: lax.rem(pos[axis] + d, 4)},
            )
            for d in range(1, 4)
        ]

    second = [None, None, []]
    for i in range(4):
        first[i].wait_recv()
        z_of = around(i)

        @pl.loop(0, 4)
        def _(y):
            for x in range(4):
                for t in range(4):
                    both = block(i, y, x, core, t) + r_a[i, y * 4 + x, t].astype(jnp.float32)
                    both = both.astype(jnp.bfloat16)
                    for p, holds in enumerate(HOLDS):
                        for n, (tile, side) in enumerate(holds):
                            if tile != t:
                                continue
                            piece = both[:, side * 128 : (side + 1) * 128]
                            if p == 0:
                                s_b[0][x, y * 4 + z_of, n] = piece
                            elif p == 1:
                                s_b[1][y, z_of * 4 + x, n] = piece
                            else:
                                s_b[2][z_of, x * 4 + y, n] = piece

        if i < 3:
            second[2].append(
                send(s_b[2].at[z_of], r_b[2].at[i], b_sem, (2, i), {"gx_0": z_of})
            )
    for p in range(2):
        second[p] = spread(p, 0, b_sem, s_b[p], r_b[p])

    def total(own, came, at):
        kind = jnp.float32
        return (own[at].astype(kind) + came[(0,) + at[1:]].astype(kind)) + (
            came[(1,) + at[1:]].astype(kind) + came[(2,) + at[1:]].astype(kind)
        )

    third = [None] * 3
    for p in (2, 0, 1):
        for copy in second[p]:
            copy.wait_recv()
        me = pos[p]

        @pl.loop(0, 16)
        def _(j):
            for t in range(len(HOLDS[p])):
                s_c[p][j // 4, j % 4, t] = total(s_b[p], r_b[p], (me, j, t)).astype(jnp.bfloat16)

        third[p] = spread(p, 1, c_sem, s_c[p], r_c[p])

    fourth = [None] * 3
    for p in (2, 0, 1):
        for copy in third[p]:
            copy.wait_recv()
        me = pos[(p + 1) % 3]

        @pl.loop(0, 4)
        def _(j):
            for t in range(len(HOLDS[p])):
                s_d[p][j, t] = total(s_c[p], r_c[p], (me, j, t))

        fourth[p] = spread(p, 2, d_sem, s_d[p], r_d[p])

    for p in (2, 0, 1):
        for copy in fourth[p]:
            copy.wait_recv()
        me = pos[(p + 2) % 3]
        for n, (tile, side) in enumerate(HOLDS[p]):
            rows = pl.ds(TILE_AT[tile], 16)
            out[rows, side * 128 : (side + 1) * 128] = total(s_d[p], r_d[p], (me, n))

    for copy in sends:
        copy.wait_send()


def scatter_sum(part):
    def stage(lead, kind):
        return [pltpu.VMEM(lead + (len(h), 16, 128), kind) for h in HOLDS]

    half, full = jnp.bfloat16, jnp.float32
    return pl.pallas_call(
        scatter_kernel,
        out_shape=jax.ShapeDtypeStruct((54, C), jnp.float32),
        in_specs=[pl.BlockSpec(memory_space=pltpu.VMEM)],
        out_specs=pl.BlockSpec(memory_space=pltpu.VMEM),
        scratch_shapes=[
            pltpu.VMEM((4, 16, 4, 16, C), jnp.bfloat16),
            pltpu.VMEM((4, 16, 4, 16, C), jnp.bfloat16),
            *stage((4, 16), half),
            *stage((3, 16), half),
            *stage((4, 4), half),
            *stage((3, 4), half),
            *stage((4,), full),
            *stage((3,), full),
            pltpu.SemaphoreType.DMA((2, 4)),
            pltpu.SemaphoreType.DMA((2, 3, 3)),
            pltpu.SemaphoreType.DMA((2, 3, 3)),
            pltpu.SemaphoreType.DMA((2, 3, 3)),
        ],
        compiler_params=pltpu.CompilerParams(
            collective_id=1, has_side_effects=True, vmem_limit_bytes=24 * 1024 * 1024
        ),
        cost_estimate=pl.CostEstimate(flops=10_000_000, bytes_accessed=7_000_000, transcendentals=0),
        name="scatter_sum",
    )(part)


HB = 704
HIGH = 272
ROWS = NROW + WIN


def seg(b):
    return R + b * HB


def front_kernel(
    count, pre_in, cot_in, gamma_in, beta_in, links_in, border_in, feat_in, weight_in,
    table, columns, starts, sums, feat_t, turned,
    pre, cot, gamma, beta, links, border, feat, weight,
    grad, pick, near, far, list_left, list_own, list_right, high,
    note_own, note_left, note_right, note_out, note_in,
    load_sem, near_sem, far_sem, halo_sem, note_sem,
):
    f32 = jnp.float32
    z, y, core, x = (lax.axis_index(a) for a in GX_GY)
    slab = (z * 4 + y) * 2 + core
    me_near, me_far = x * 2 + core, z * 4 + y

    def near_id(p):
        return {"gy": p // 2, "gx_2": lax.rem(p, 2)}

    def far_id(p):
        return {"gx_0": p // 4, "gx_1": lax.rem(p, 4)}

    def slab_id(s):
        return {"gx_0": s // 8, "gx_1": lax.rem(s // 2, 4), "gx_2": lax.rem(s, 2)}

    loads = []
    for source, target in (
        (pre_in, pre),
        (border_in, border),
        (cot_in, cot),
        (gamma_in, gamma),
        (beta_in, beta),
        (links_in, links),
        (feat_in, feat),
        (weight_in, weight),
    ):
        loads.append(pltpu.make_async_copy(source, target, load_sem.at[len(loads)]))
        loads[-1].start()

    barrier = pltpu.get_barrier_semaphore()
    for d in range(1, 8):
        pl.semaphore_signal(
            barrier, 1, device_id=near_id(lax.rem(me_near + d, 8)), device_id_type=MESH
        )
    for d in range(1, 16):
        pl.semaphore_signal(
            barrier, 1, device_id=far_id(lax.rem(me_far + d, 16)), device_id_type=MESH
        )
    up, down = (core == 1) & (slab < 31), (core == 0) & (slab > 0)

    @pl.when(up)
    def _():
        pl.semaphore_signal(barrier, 1, device_id=slab_id(slab + 1), device_id_type=MESH)

    @pl.when(down)
    def _():
        pl.semaphore_signal(barrier, 1, device_id=slab_id(slab - 1), device_id_type=MESH)

    live_rows = count[0, 0]
    block = 128

    def live_at(t):
        row = lax.broadcasted_iota(jnp.int32, (block, C), 0) + t * block
        return row < live_rows

    def rows_at(t):
        return pl.ds(pl.multiple_of(t * block, block), block)

    def fold(a):
        return jnp.sum(a.reshape(block // 8, 8, C), axis=0)

    def first_sums(t, sums):
        zval = pre[rows_at(t), :].astype(f32)
        zlive = jnp.where(live_at(t), zval, 0.0)
        return sums[0] + fold(zlive), sums[1] + fold(zlive * zval)

    zero = jnp.zeros((8, C), f32)

    def stacked(a, b, *more):
        a, b = jnp.sum(a, axis=0, keepdims=True), jnp.sum(b, axis=0, keepdims=True)
        return jnp.concatenate([a, b] + [jnp.full((1, C), c, f32) for c in more], axis=1)

    def exchange(slots, me, size, sems, turn, ids):
        copies = []
        for d in range(1, size):
            copies.append(
                pltpu.make_async_remote_copy(
                    src_ref=slots.at[turn, me],
                    dst_ref=slots.at[turn, me],
                    send_sem=sems.at[turn, 0, d - 1],
                    recv_sem=sems.at[turn, 1, d - 1],
                    device_id=ids(lax.rem(me + d, size)),
                    device_id_type=MESH,
                )
            )
            copies[-1].start()
        return copies

    def add_up(slots, size, turn, copies):
        for copy in copies:
            copy.wait_recv()
        total = slots[turn, 0]
        for i in range(1, size):
            total = total + slots[turn, i]
        return total

    pending = []

    def all_sum(turn, value, meanwhile):
        near[turn, me_near] = value
        one = exchange(near, me_near, 8, near_sem, turn, near_id)
        meanwhile()
        far[turn, me_far] = add_up(near, 8, turn, one)
        two = exchange(far, me_far, 16, far_sem, turn, far_id)
        pending.extend(one + two)
        return add_up(far, 16, turn, two)

    def when(cond, act):
        @pl.when(cond)
        def _():
            act()

    has_right, has_left, has_next, has_last = x < 3, x > 0, slab < 31, slab > 0

    def note(source, target, n, device):
        return pltpu.make_async_remote_copy(
            src_ref=source,
            dst_ref=target,
            send_sem=note_sem.at[0, n],
            recv_sem=note_sem.at[1, n],
            device_id=device,
            device_id_type=MESH,
        )

    def note_to_right():
        return note(note_own, note_left, 0, {"gy": x + 1})

    def note_to_left():
        return note(note_own, note_right, 1, {"gy": x - 1})

    def note_ahead():
        return note(note_out, note_in, 2, slab_id(slab + 1))

    def blank(ref):
        ref[...] = jnp.zeros_like(ref)

    def notes_first():
        size = jnp.sum(jnp.where(border[...] < R, 1, 0), axis=1, keepdims=True)
        first = jnp.minimum(jnp.maximum(size - WIN, 0) // 16, (HB - HIGH) // 16)
        note_own[...] = jnp.broadcast_to(first, (8, 128))
        when(~has_left, lambda: blank(note_left))
        when(~has_right, lambda: blank(note_right))
        when(~has_last, lambda: blank(note_in))

    def notes_second():
        when(has_left, lambda: note_to_right().wait_recv())
        when(has_right, lambda: note_to_left().wait_recv())
        row = lax.broadcasted_iota(jnp.int32, (8, 128), 0)
        note_out[...] = jnp.where(
            row == 0, note_left[...], jnp.where(row == 1, note_own[...], note_right[...])
        )
        when(has_next, lambda: note_ahead().start())

    def plan(part, spare):
        moved = [note_in[b : b + 1, :] * 16 for b in range(3)]
        lane = lax.broadcasted_iota(jnp.int32, (1, 128), 1)
        third = lax.rem(lane, 3)

        def one(j, spare):
            at = pl.ds(pl.multiple_of(j * SUB, SUB), SUB)
            idx = links[:, 0, at]
            for b in range(3):
                inside = (idx >= seg(b)) & (idx < seg(b + 1))
                idx = jnp.where(inside, idx - moved[b], idx)
            idx = jnp.where(idx < NROW, idx, jnp.int32(FAR)).astype(f32)
            idx = jnp.concatenate([idx, jnp.full((101, SUB), FAR, f32)], axis=0).T
            columns[at, :] = idx
            begin = []
            for w in range(3):
                low = jnp.min(idx, axis=0, keepdims=True)
                low = jnp.minimum(low, jnp.minimum(pltpu.roll(low, 127, 1), pltpu.roll(low, 126, 1)))
                low = jnp.where(
                    third == 0,
                    low,
                    jnp.where(third == 1, pltpu.roll(low, 1, 1), pltpu.roll(low, 2, 1)),
                )
                start = jnp.where(low < NROW, jnp.floor(low * 0.0625) * 16.0, FAR)
                idx = jnp.where(idx >= start + WIN, idx, FAR)
                begin.append(jnp.minimum(start, float(NROW)) if w < 2 else start)
            spare = jnp.minimum(spare, begin[2])
            begin = [jnp.broadcast_to(b, (8, 128)) for b in begin]
            row = lax.broadcasted_iota(jnp.int32, (8, 128), 0)
            begin = jnp.where(row == 0, begin[0], jnp.where(row == 1, begin[1], begin[2]))
            starts[pl.ds(pl.multiple_of(j * 8, 8), 8), :] = begin.astype(jnp.int32)
            return spare

        def some(n, spare):
            for u in range(4):
                spare = one(part * 8 + n * 4 + u, spare)
            return spare

        return lax.fori_loop(0, 2, some, spare)

    def choose():
        lane = lax.broadcasted_iota(jnp.int32, (128, 128), 1)
        for t in range(6):
            width = min(128, HB - t * 128)
            names = border[:, t * 128 : t * 128 + width].astype(f32)
            if width < 128:
                names = jnp.concatenate([names, jnp.full((1, 128 - width), FAR, f32)], axis=1)
            names = jnp.broadcast_to(names, (128, 128)).T[:width]
            for c in range(R // 128):
                row = (lane[:width] + c * 128).astype(f32)
                pick[t * 128 : t * 128 + width, c * 128 : (c + 1) * 128] = jnp.where(
                    names == row, 1.0, 0.0
                ).astype(jnp.bfloat16)

        def clear(at, size):
            table[at : at + size, :] = jnp.zeros((size, C), jnp.bfloat16)

        clear(NROW, WIN)

        @pl.when(slab == 0)
        def _():
            for b in (0, 1, 2):
                clear(seg(b), HIGH)

        @pl.when(slab == 31)
        def _():
            for b in (6, 7, 8):
                clear(seg(b), WIN)

        for b in (0, 1, 2):
            clear(seg(b) + HIGH, HB - HIGH)

        for b in (6, 7, 8):
            clear(seg(b) + WIN, HB - WIN)

        for edge, db, missing in ((0, 0, list_left), (3, 2, list_right)):
            @pl.when(x == edge)
            def _():
                blank(missing)

                @pl.when(slab > 0)
                def _():
                    clear(seg(db), HIGH)

                @pl.when(slab < 31)
                def _():
                    clear(seg(6 + db), WIN)

    loads[0].wait()
    sum_z, sum_sq = lax.fori_loop(0, R // block, first_sums, (zero, zero))
    loads[1].wait()
    notes_first()
    extra = jnp.where(up | down, 1, 0)
    pl.semaphore_wait(barrier, 22 + extra)
    when(has_right, lambda: note_to_right().start())
    when(has_left, lambda: note_to_left().start())

    def during_first():
        choose()
        notes_second()

    whole = all_sum(0, stacked(sum_z, sum_sq, live_rows.astype(f32)), during_first)
    amount = whole[:, 2 * C :]
    mean = whole[:, :C] / amount
    var = whole[:, C : 2 * C] / amount - mean * mean
    rstd = lax.rsqrt(var + 1e-05)
    for load in loads[2:5]:
        load.wait()
    gain, shift = gamma[...], beta[...]

    def during_second():
        loads[6].wait()
        for t in range(8):
            feat_t[:, t * 256 : (t + 1) * 256] = feat[t * 256 : (t + 1) * 256, :].T
        loads[5].wait()
        when(has_last, lambda: note_ahead().wait_recv())

    def second_sums(t, sums):
        zhat = (pre[rows_at(t), :].astype(f32) - mean) * rstd
        act = gain * zhat + shift
        sig = jax.nn.sigmoid(act)
        g = cot[rows_at(t), :].astype(f32) * sig * (1.0 + act * (1.0 - sig))
        g = jnp.where(live_at(t), g, 0.0)
        grad[rows_at(t), :] = g
        return sums[0] + fold(g), sums[1] + fold(g * zhat)

    sum_g, sum_gz = lax.fori_loop(0, R // block, second_sums, (zero, zero))
    whole = all_sum(1, stacked(sum_g, sum_gz, 0.0), during_second)
    sums[0] = whole[:, :C]
    sums[1] = whole[:, C : 2 * C]
    scale = gain * rstd
    part_g, part_gz = whole[:, :C] / amount, whole[:, C : 2 * C] / amount

    @pl.loop(0, R // block)
    def _(t):
        zhat = (pre[rows_at(t), :].astype(f32) - mean) * rstd
        dz = scale * (grad[rows_at(t), :] - part_g - zhat * part_gz)
        table[rows_at(t), :] = jnp.where(live_at(t), dz, 0.0).astype(jnp.bfloat16)

    @pl.loop(0, 4)
    def _(t):
        at = pl.multiple_of(t * 176, 16)
        rows = dot(pick[pl.ds(at, 176), :], table[0:R, :], ((1,), (0,)))
        list_own[pl.ds(at, 176), :] = rows.astype(jnp.bfloat16)

    def hop(source, target, n, device):
        return pltpu.make_async_remote_copy(
            src_ref=source,
            dst_ref=target,
            send_sem=halo_sem.at[0, n],
            recv_sem=halo_sem.at[1, n],
            device_id=device,
            device_id_type=MESH,
        )

    lists = (list_left, list_own, list_right)

    def right():
        return hop(list_own, list_left, 3, {"gy": x + 1})

    def left():
        return hop(list_own, list_right, 5, {"gy": x - 1})

    def ahead(db):
        return hop(high.at[db], table.at[pl.ds(seg(db), HIGH), :], db, slab_id(slab + 1))

    def behind(db):
        target = table.at[pl.ds(seg(6 + db), WIN), :]
        return hop(lists[db].at[pl.ds(0, WIN), :], target, 6 + db, slab_id(slab - 1))

    def pass_on(db, mark):
        at = jnp.max(mark[...]) * 16
        high[db] = lists[db][pl.ds(at, HIGH), :]
        when(has_next, lambda: ahead(db).start())
        when(has_last, lambda: behind(db).start())

    when(has_right, lambda: right().start())
    when(has_left, lambda: left().start())
    pass_on(1, note_own)
    table[seg(4) : seg(5), :] = list_own[...]
    spare = plan(0, jnp.full((1, 128), FAR, f32))
    loads[7].wait()
    for db, there, came, mark in (
        (0, has_left, right, note_left),
        (2, has_right, left, note_right),
    ):
        when(there, lambda: came().wait_recv())
        when(there, lambda: pass_on(db, mark))
        table[seg(3 + db) : seg(4 + db), :] = lists[db][...]

    spare = plan(1, spare)
    row = lax.broadcasted_iota(jnp.int32, (8, 128), 0)
    starts[0:8, :] = jnp.where(row == 3, spare.astype(jnp.int32), starts[0:8, :])

    @pl.loop(0, 9)
    def _(g):
        for i in range(3):
            turned[g, i * C : (i + 1) * C, :] = weight[g * 3 + i].T

    for db, there in ((1, True), (0, has_left), (2, has_right)):
        when(has_last & there, lambda: ahead(db).wait_recv())
        when(has_next & there, lambda: behind(db).wait_recv())
    when(has_right, lambda: right().wait_send())
    when(has_left, lambda: left().wait_send())
    for db, there in ((1, True), (0, has_left), (2, has_right)):
        when(has_next & there, lambda: ahead(db).wait_send())
        when(has_last & there, lambda: behind(db).wait_send())
    when(has_right, lambda: note_to_right().wait_send())
    when(has_left, lambda: note_to_left().wait_send())
    when(has_next, lambda: note_ahead().wait_send())
    for copy in pending:
        copy.wait_send()


def front(counts, *arrays):
    vmem = pl.BlockSpec(memory_space=pltpu.VMEM)
    return pl.pallas_call(
        front_kernel,
        out_shape=(
            jax.ShapeDtypeStruct((ROWS, C), jnp.bfloat16),
            jax.ShapeDtypeStruct((R, 128), jnp.float32),
            jax.ShapeDtypeStruct((R // SUB * 8, 128), jnp.int32),
            jax.ShapeDtypeStruct((2, 1, C), jnp.float32),
            jax.ShapeDtypeStruct((C, R), jnp.bfloat16),
            jax.ShapeDtypeStruct((9, 3 * C, C), jnp.bfloat16),
        ),
        in_specs=[pl.BlockSpec(memory_space=pltpu.SMEM)]
        + [pl.BlockSpec(memory_space=pltpu.HBM)] * 8,
        out_specs=(vmem,) * 6,
        scratch_shapes=[pltpu.VMEM(a.shape, a.dtype) for a in arrays]
        + [
            pltpu.VMEM((R, C), jnp.float32),
            pltpu.VMEM((HB, R), jnp.bfloat16),
            pltpu.VMEM((2, 8, 1, 3 * C), jnp.float32),
            pltpu.VMEM((2, 16, 1, 3 * C), jnp.float32),
            pltpu.VMEM((HB, C), jnp.bfloat16),
            pltpu.VMEM((HB, C), jnp.bfloat16),
            pltpu.VMEM((HB, C), jnp.bfloat16),
            pltpu.VMEM((3, HIGH, C), jnp.bfloat16),
            *[pltpu.VMEM((8, 128), jnp.int32)] * 5,
            pltpu.SemaphoreType.DMA((8,)),
            pltpu.SemaphoreType.DMA((2, 2, 7)),
            pltpu.SemaphoreType.DMA((2, 2, 15)),
            pltpu.SemaphoreType.DMA((2, 9)),
            pltpu.SemaphoreType.DMA((2, 3)),
        ],
        compiler_params=pltpu.CompilerParams(
            collective_id=0, has_side_effects=True, vmem_limit_bytes=24 * 1024 * 1024
        ),
        cost_estimate=pl.CostEstimate(
            flops=1_000_000_000, bytes_accessed=10_000_000, transcendentals=1_000_000
        ),
        name="front",
    )(counts, *[pltpu.with_memory_space_constraint(a, pltpu.HBM) for a in arrays])


def body(features, pre_norm, out_grad, weight, gamma, beta, neighbors, boundary, counts):
    table, columns, starts, sums, feat_t, turned = front(
        counts,
        pre_norm[0, 0],
        out_grad[0, 0],
        gamma[None],
        beta[None],
        neighbors.reshape(27, 1, R),
        boundary.reshape(1, HB),
        features[0, 0],
        weight,
    )
    in_grad, local_wgrad, gamma_grad, beta_grad = convolve(
        starts, columns, table, feat_t, turned, sums
    )
    weight_grad = scatter_sum(local_wgrad)
    return (in_grad[None, None], weight_grad, gamma_grad[0], beta_grad[0])


def solution(mesh):
    torus = Mesh(mesh.devices.reshape(4, 4, 2, mesh.shape["gy"]), ("gx_0", "gx_1", "gx_2", "gy"))
    return jax.shard_map(
        body,
        mesh=torus,
        in_specs=(
            P(GX, "gy", None, None),
            P(GX, "gy", None, None),
            P(GX, "gy", None, None),
            P(),
            P(),
            P(),
            P(GX, "gy", None, None),
            P(GX, "gy", None),
            P(GX, "gy"),
        ),
        out_specs=(P(GX, "gy", None, None), P(GX_GY, None), P(), P()),
        check_vma=False,
    )
```

```python
import jax
import jax.numpy as jnp
from jax import lax
from jax.experimental import pallas as pl
from jax.experimental.pallas import tpu as pltpu
from jax.sharding import Mesh
from jax.sharding import PartitionSpec as P

GX_GY = ("gx_0", "gx_1", "gx_2", "gy")
GX = ("gx_0", "gx_1", "gx_2")
MESH = pl.DeviceIdType.MESH


C = 256
R = 2048
SUB = 128
WIN = 256
NROW = 8384
FAR = 1.0e6


def dot(a, b, dims):
    return lax.dot_general(a, b, (dims, ((), ())), preferred_element_type=jnp.float32)


def one_hot(columns, start):
    lanes = lax.broadcasted_iota(jnp.int32, (SUB, WIN), 1).astype(jnp.float32)
    place = columns - start.astype(jnp.float32)
    return jnp.where(place == lanes, 1.0, 0.0).astype(jnp.bfloat16)

def conv_kernel(
    starts, idx, table, feat_t, turned, sums_in, in_grad, wgrad, gamma_grad, beta_grad,
    acc, picked,
):
    acc[...] = jnp.zeros_like(acc)
    beta_grad[...] = sums_in[0]
    gamma_grad[...] = sums_in[1]

    @pl.loop(0, 9)
    def _(step):
        conv_group(step, starts, idx, table, feat_t, turned, wgrad, acc, picked)

    in_grad[...] = acc[...].astype(jnp.bfloat16)


def conv_group(step, starts, idx, table, feat_t, turned, wgrad, acc, picked):
    lane0 = 24 - 3 * step

    def columns_at(row):
        return idx[step, pl.ds(row, SUB), :]

    def window(columns, start):
        hot = [
            one_hot(jnp.broadcast_to(columns[:, 2 - i : 3 - i], (SUB, WIN)), start)
            for i in range(3)
        ]
        return jnp.concatenate(hot, axis=0)

    def gather(j):
        row = j * SUB
        columns = columns_at(row)
        s = [pl.multiple_of(starts[j * 8 + w, lane0], 16) for w in range(2)]
        hots = [window(columns, a) for a in s]
        tabs = [table[pl.ds(a, WIN), :] for a in s]
        total = dot(jnp.concatenate(hots, axis=1), jnp.concatenate(tabs, axis=0), ((1,), (0,)))
        total = total.astype(jnp.bfloat16)
        for i in range(3):
            picked[pl.ds(row, SUB), i * C : (i + 1) * C] = total[i * SUB : (i + 1) * SUB]

    def gather_rest(j):
        row = j * SUB

        def more(start):
            columns = columns_at(row)
            start = pl.multiple_of(start, 16)
            part = dot(window(columns, start), table[pl.ds(start, WIN), :], ((1,), (0,)))
            part = part.astype(jnp.bfloat16)
            for i in range(3):
                picked[pl.ds(row, SUB), i * C : (i + 1) * C] += part[i * SUB : (i + 1) * SUB]
            lane = lax.broadcasted_iota(jnp.int32, (SUB, 128), 1)
            ahead = (lane < 3) & (columns >= (start + WIN).astype(jnp.float32))
            low = jnp.min(jnp.where(ahead, columns, FAR)).astype(jnp.int32)
            return jnp.where(low < NROW, low // 16 * 16, jnp.int32(FAR))

        lax.while_loop(lambda start: start < NROW, more, starts[j * 8 + 2, lane0])

    for j in range(R // SUB):
        gather(j)

    @pl.when(starts[3, lane0] < NROW)
    def _():
        for j in range(R // SUB):
            gather_rest(j)

    for i in range(3):
        wgrad[step * 3 + i] = dot(feat_t[...], picked[:, i * C : (i + 1) * C], ((1,), (0,)))
    acc[...] += dot(picked[...], turned[step], ((1,), (0,)))


def convolve(starts, idx, table, feat_t, turned, sums):
    whole = pl.BlockSpec(memory_space=pltpu.VMEM)
    in_grad, wgrad, gamma_grad, beta_grad = pl.pallas_call(
        conv_kernel,
        out_shape=(
            jax.ShapeDtypeStruct((R, C), jnp.bfloat16),
            jax.ShapeDtypeStruct((27, C, C), jnp.float32),
            jax.ShapeDtypeStruct((1, C), jnp.float32),
            jax.ShapeDtypeStruct((1, C), jnp.float32),
        ),
        in_specs=[
            pl.BlockSpec(memory_space=pltpu.SMEM),
            whole,
            whole,
            whole,
            whole,
            whole,
        ],
        out_specs=(whole,) * 4,
        scratch_shapes=[
            pltpu.VMEM((R, C), jnp.float32),
            pltpu.VMEM((R, 3 * C), jnp.bfloat16),
        ],
        compiler_params=pltpu.CompilerParams(vmem_limit_bytes=20 * 1024 * 1024),
        cost_estimate=pl.CostEstimate(
            flops=30_000_000_000, bytes_accessed=20_000_000, transcendentals=0
        ),
        name="conv_backward",
    )(starts, idx, table, feat_t, turned, sums)
    return in_grad, wgrad.reshape(27 * C, C), gamma_grad, beta_grad


AXES = ("gy", "gx_1", "gx_0")
TILE_AT = (0, 16, 32, 38)
HOLDS = (((0, 0), (0, 1), (3, 0)), ((1, 0), (1, 1), (3, 1)), ((2, 0), (2, 1)))


def scatter_kernel(part, out, s_a, r_a, *rest):
    s_b, r_b, s_c, r_c, s_d, r_d = (rest[3 * i : 3 * i + 3] for i in range(6))
    a_sem, b_sem, c_sem, d_sem = rest[18:]
    pos = [lax.axis_index(a) for a in AXES]
    core = lax.axis_index("gx_2")
    z = pos[2]

    def around(i):
        return lax.rem(z + 1 + i, 4)

    barrier = pltpu.get_barrier_semaphore()
    pl.semaphore_signal(barrier, 1, device_id={"gx_2": 1 - core}, device_id_type=MESH)
    for axis, at in zip(AXES, pos):
        for d in range(1, 4):
            peer = {axis: lax.rem(at + d, 4)}
            pl.semaphore_signal(barrier, 1, device_id=peer, device_id_type=MESH)

    def block(i, y, x, side, t):
        skip = (x * 54 + TILE_AT[t]) % 8
        base = around(i) * 1728 + (y * 2 + side) * 216 + x * 54 + TILE_AT[t] - skip
        rows = part[pl.ds(pl.multiple_of(base, 8), 24 if skip else 16), :]
        return rows[skip : skip + 16]

    sends = []

    def send(src, dst, sems, at, device):
        copy = pltpu.make_async_remote_copy(
            src_ref=src,
            dst_ref=dst,
            send_sem=sems.at[(0,) + at],
            recv_sem=sems.at[(1,) + at],
            device_id=device,
            device_id_type=MESH,
        )
        copy.start()
        sends.append(copy)
        return copy

    first = []
    for i in range(4):
        @pl.loop(0, 4)
        def _(y):
            for x in range(4):
                for t in range(4):
                    mine = block(i, y, x, 1 - core, t)
                    s_a[i, y * 4 + x, t] = mine.astype(jnp.bfloat16)

        if i == 0:
            pl.semaphore_wait(barrier, 10)
        first.append(send(s_a.at[i], r_a.at[i], a_sem, (i,), {"gx_2": 1 - core}))

    def spread(p, stage, sems, src, dst):
        axis = (p + stage) % 3
        return [
            send(
                src.at[lax.rem(pos[axis] + d, 4)],
                dst.at[d - 1],
                sems,
                (p, d - 1),
                {AXES[axis]: lax.rem(pos[axis] + d, 4)},
            )
            for d in range(1, 4)
        ]

    second = [None, None, []]
    for i in range(4):
        first[i].wait_recv()
        z_of = around(i)

        @pl.loop(0, 4)
        def _(y):
            for x in range(4):
                for t in range(4):
                    both = block(i, y, x, core, t) + r_a[i, y * 4 + x, t].astype(jnp.float32)
                    both = both.astype(jnp.bfloat16)
                    for p, holds in enumerate(HOLDS):
                        for n, (tile, side) in enumerate(holds):
                            if tile != t:
                                continue
                            piece = both[:, side * 128 : (side + 1) * 128]
                            if p == 0:
                                s_b[0][x, y * 4 + z_of, n] = piece
                            elif p == 1:
                                s_b[1][y, z_of * 4 + x, n] = piece
                            else:
                                s_b[2][z_of, x * 4 + y, n] = piece

        if i < 3:
            second[2].append(
                send(s_b[2].at[z_of], r_b[2].at[i], b_sem, (2, i), {"gx_0": z_of})
            )
    for p in range(2):
        second[p] = spread(p, 0, b_sem, s_b[p], r_b[p])

    def total(own, came, at):
        kind = jnp.float32
        return (own[at].astype(kind) + came[(0,) + at[1:]].astype(kind)) + (
            came[(1,) + at[1:]].astype(kind) + came[(2,) + at[1:]].astype(kind)
        )

    third = [None] * 3
    for p in (2, 0, 1):
        for copy in second[p]:
            copy.wait_recv()
        me = pos[p]

        @pl.loop(0, 16)
        def _(j):
            for t in range(len(HOLDS[p])):
                s_c[p][j // 4, j % 4, t] = total(s_b[p], r_b[p], (me, j, t)).astype(jnp.bfloat16)

        third[p] = spread(p, 1, c_sem, s_c[p], r_c[p])

    fourth = [None] * 3
    for p in (2, 0, 1):
        for copy in third[p]:
            copy.wait_recv()
        me = pos[(p + 1) % 3]

        @pl.loop(0, 4)
        def _(j):
            for t in range(len(HOLDS[p])):
                s_d[p][j, t] = total(s_c[p], r_c[p], (me, j, t))

        fourth[p] = spread(p, 2, d_sem, s_d[p], r_d[p])

    for p in (2, 0, 1):
        for copy in fourth[p]:
            copy.wait_recv()
        me = pos[(p + 2) % 3]
        for n, (tile, side) in enumerate(HOLDS[p]):
            rows = pl.ds(TILE_AT[tile], 16)
            out[rows, side * 128 : (side + 1) * 128] = total(s_d[p], r_d[p], (me, n))

    for copy in sends:
        copy.wait_send()


def scatter_sum(part):
    def stage(lead, kind):
        return [pltpu.VMEM(lead + (len(h), 16, 128), kind) for h in HOLDS]

    half, full = jnp.bfloat16, jnp.float32
    return pl.pallas_call(
        scatter_kernel,
        out_shape=jax.ShapeDtypeStruct((54, C), jnp.float32),
        in_specs=[pl.BlockSpec(memory_space=pltpu.VMEM)],
        out_specs=pl.BlockSpec(memory_space=pltpu.VMEM),
        scratch_shapes=[
            pltpu.VMEM((4, 16, 4, 16, C), jnp.bfloat16),
            pltpu.VMEM((4, 16, 4, 16, C), jnp.bfloat16),
            *stage((4, 16), half),
            *stage((3, 16), half),
            *stage((4, 4), half),
            *stage((3, 4), half),
            *stage((4,), full),
            *stage((3,), full),
            pltpu.SemaphoreType.DMA((2, 4)),
            pltpu.SemaphoreType.DMA((2, 3, 3)),
            pltpu.SemaphoreType.DMA((2, 3, 3)),
            pltpu.SemaphoreType.DMA((2, 3, 3)),
        ],
        compiler_params=pltpu.CompilerParams(
            collective_id=1, has_side_effects=True, vmem_limit_bytes=24 * 1024 * 1024
        ),
        cost_estimate=pl.CostEstimate(flops=10_000_000, bytes_accessed=7_000_000, transcendentals=0),
        name="scatter_sum",
    )(part)


HB = 704
HIGH = 272
ROWS = NROW + WIN


def seg(b):
    return R + b * HB


def front_kernel(
    count, pre_in, cot_in, gamma_in, beta_in, links_in, border_in, feat_in, weight_in,
    table, columns, starts, sums, feat_t, turned,
    pre, cot, gamma, beta, links, border, feat, weight,
    grad, pick, near, far, list_left, list_own, list_right, high,
    note_own, note_left, note_right, note_out, note_in,
    load_sem, near_sem, far_sem, halo_sem, note_sem,
):
    f32 = jnp.float32
    z, y, core, x = (lax.axis_index(a) for a in GX_GY)
    slab = (z * 4 + y) * 2 + core
    me_near, me_far = x * 2 + core, z * 4 + y

    def near_id(p):
        return {"gy": p // 2, "gx_2": lax.rem(p, 2)}

    def far_id(p):
        return {"gx_0": p // 4, "gx_1": lax.rem(p, 4)}

    def slab_id(s):
        return {"gx_0": s // 8, "gx_1": lax.rem(s // 2, 4), "gx_2": lax.rem(s, 2)}

    loads = []
    for source, target in (
        (pre_in, pre),
        (border_in, border),
        (cot_in, cot),
        (gamma_in, gamma),
        (beta_in, beta),
        (links_in, links),
        (feat_in, feat),
        (weight_in, weight),
    ):
        loads.append(pltpu.make_async_copy(source, target, load_sem.at[len(loads)]))
        loads[-1].start()

    barrier = pltpu.get_barrier_semaphore()
    for d in range(1, 8):
        pl.semaphore_signal(
            barrier, 1, device_id=near_id(lax.rem(me_near + d, 8)), device_id_type=MESH
        )
    for d in range(1, 16):
        pl.semaphore_signal(
            barrier, 1, device_id=far_id(lax.rem(me_far + d, 16)), device_id_type=MESH
        )
    up, down = (core == 1) & (slab < 31), (core == 0) & (slab > 0)

    @pl.when(up)
    def _():
        pl.semaphore_signal(barrier, 1, device_id=slab_id(slab + 1), device_id_type=MESH)

    @pl.when(down)
    def _():
        pl.semaphore_signal(barrier, 1, device_id=slab_id(slab - 1), device_id_type=MESH)

    live_rows = count[0, 0]
    block = 128

    def live_at(t):
        row = lax.broadcasted_iota(jnp.int32, (block, C), 0) + t * block
        return row < live_rows

    def rows_at(t):
        return pl.ds(pl.multiple_of(t * block, block), block)

    def fold(a):
        return jnp.sum(a.reshape(block // 8, 8, C), axis=0)

    def first_sums(t, sums):
        zval = pre[rows_at(t), :].astype(f32)
        zlive = jnp.where(live_at(t), zval, 0.0)
        return sums[0] + fold(zlive), sums[1] + fold(zlive * zval)

    zero = jnp.zeros((8, C), f32)

    def stacked(a, b, *more):
        a, b = jnp.sum(a, axis=0, keepdims=True), jnp.sum(b, axis=0, keepdims=True)
        return jnp.concatenate([a, b] + [jnp.full((1, C), c, f32) for c in more], axis=1)

    def exchange(slots, me, size, sems, turn, ids):
        copies = []
        for d in range(1, size):
            copies.append(
                pltpu.make_async_remote_copy(
                    src_ref=slots.at[turn, me],
                    dst_ref=slots.at[turn, me],
                    send_sem=sems.at[turn, 0, d - 1],
                    recv_sem=sems.at[turn, 1, d - 1],
                    device_id=ids(lax.rem(me + d, size)),
                    device_id_type=MESH,
                )
            )
            copies[-1].start()
        return copies

    def add_up(slots, size, turn, copies):
        for copy in copies:
            copy.wait_recv()
        total = slots[turn, 0]
        for i in range(1, size):
            total = total + slots[turn, i]
        return total

    pending = []

    def all_sum(turn, value, meanwhile):
        near[turn, me_near] = value
        one = exchange(near, me_near, 8, near_sem, turn, near_id)
        meanwhile()
        far[turn, me_far] = add_up(near, 8, turn, one)
        two = exchange(far, me_far, 16, far_sem, turn, far_id)
        pending.extend(one + two)
        return add_up(far, 16, turn, two)

    def when(cond, act):
        @pl.when(cond)
        def _():
            act()

    has_right, has_left, has_next, has_last = x < 3, x > 0, slab < 31, slab > 0

    def note(source, target, n, device):
        return pltpu.make_async_remote_copy(
            src_ref=source,
            dst_ref=target,
            send_sem=note_sem.at[0, n],
            recv_sem=note_sem.at[1, n],
            device_id=device,
            device_id_type=MESH,
        )

    def note_to_right():
        return note(note_own, note_left, 0, {"gy": x + 1})

    def note_to_left():
        return note(note_own, note_right, 1, {"gy": x - 1})

    def note_ahead():
        return note(note_out, note_in, 2, slab_id(slab + 1))

    def blank(ref):
        ref[...] = jnp.zeros_like(ref)

    def notes_first():
        size = jnp.sum(jnp.where(border[...] < R, 1, 0), axis=1, keepdims=True)
        first = jnp.minimum(jnp.maximum(size - WIN, 0) // 16, (HB - HIGH) // 16)
        note_own[...] = jnp.broadcast_to(first, (8, 128))
        when(~has_left, lambda: blank(note_left))
        when(~has_right, lambda: blank(note_right))
        when(~has_last, lambda: blank(note_in))

    def notes_second():
        when(has_left, lambda: note_to_right().wait_recv())
        when(has_right, lambda: note_to_left().wait_recv())
        row = lax.broadcasted_iota(jnp.int32, (8, 128), 0)
        note_out[...] = jnp.where(
            row == 0, note_left[...], jnp.where(row == 1, note_own[...], note_right[...])
        )
        when(has_next, lambda: note_ahead().start())

    def plan(part, spare):
        moved = [note_in[b : b + 1, :] * 16 for b in range(3)]
        lane = lax.broadcasted_iota(jnp.int32, (1, 128), 1)
        third = lax.rem(lane, 3)

        def one(j, spare):
            at = pl.ds(pl.multiple_of(j * SUB, SUB), SUB)
            idx = links[:, 0, at]
            for b in range(3):
                inside = (idx >= seg(b)) & (idx < seg(b + 1))
                idx = jnp.where(inside, idx - moved[b], idx)
            idx = jnp.where(idx < NROW, idx, jnp.int32(FAR)).astype(f32)
            idx = jnp.concatenate([idx, jnp.full((101, SUB), FAR, f32)], axis=0).T
            for g in range(9):
                shift = (104 + 3 * g) % 128
                columns[g, at, :] = pltpu.roll(idx, shift, 1)
            begin = []
            for w in range(3):
                low = jnp.min(idx, axis=0, keepdims=True)
                low = jnp.minimum(low, jnp.minimum(pltpu.roll(low, 127, 1), pltpu.roll(low, 126, 1)))
                low = jnp.where(
                    third == 0,
                    low,
                    jnp.where(third == 1, pltpu.roll(low, 1, 1), pltpu.roll(low, 2, 1)),
                )
                start = jnp.where(low < NROW, jnp.floor(low * 0.0625) * 16.0, FAR)
                idx = jnp.where(idx >= start + WIN, idx, FAR)
                begin.append(jnp.minimum(start, float(NROW)) if w < 2 else start)
            spare = jnp.minimum(spare, begin[2])
            begin = [jnp.broadcast_to(b, (8, 128)) for b in begin]
            row = lax.broadcasted_iota(jnp.int32, (8, 128), 0)
            begin = jnp.where(row == 0, begin[0], jnp.where(row == 1, begin[1], begin[2]))
            starts[pl.ds(pl.multiple_of(j * 8, 8), 8), :] = begin.astype(jnp.int32)
            return spare

        def some(n, spare):
            for u in range(4):
                spare = one(part * 8 + n * 4 + u, spare)
            return spare

        return lax.fori_loop(0, 2, some, spare)

    def choose():
        lane = lax.broadcasted_iota(jnp.int32, (128, 128), 1)
        for t in range(6):
            width = min(128, HB - t * 128)
            names = border[:, t * 128 : t * 128 + width].astype(f32)
            if width < 128:
                names = jnp.concatenate([names, jnp.full((1, 128 - width), FAR, f32)], axis=1)
            names = jnp.broadcast_to(names, (128, 128)).T[:width]
            for c in range(R // 128):
                row = (lane[:width] + c * 128).astype(f32)
                pick[t * 128 : t * 128 + width, c * 128 : (c + 1) * 128] = jnp.where(
                    names == row, 1.0, 0.0
                ).astype(jnp.bfloat16)

        def clear(at, size):
            table[at : at + size, :] = jnp.zeros((size, C), jnp.bfloat16)

        clear(NROW, WIN)

        @pl.when(slab == 0)
        def _():
            for b in (0, 1, 2):
                clear(seg(b), HIGH)

        @pl.when(slab == 31)
        def _():
            for b in (6, 7, 8):
                clear(seg(b), WIN)

        for b in (0, 1, 2):
            clear(seg(b) + HIGH, HB - HIGH)

        for b in (6, 7, 8):
            clear(seg(b) + WIN, HB - WIN)

        for edge, db, missing in ((0, 0, list_left), (3, 2, list_right)):
            @pl.when(x == edge)
            def _():
                blank(missing)

                @pl.when(slab > 0)
                def _():
                    clear(seg(db), HIGH)

                @pl.when(slab < 31)
                def _():
                    clear(seg(6 + db), WIN)

    loads[0].wait()
    sum_z, sum_sq = lax.fori_loop(0, R // block, first_sums, (zero, zero))
    loads[1].wait()
    notes_first()
    extra = jnp.where(up | down, 1, 0)
    pl.semaphore_wait(barrier, 22 + extra)
    when(has_right, lambda: note_to_right().start())
    when(has_left, lambda: note_to_left().start())

    def during_first():
        choose()
        notes_second()

    whole = all_sum(0, stacked(sum_z, sum_sq, live_rows.astype(f32)), during_first)
    amount = whole[:, 2 * C :]
    mean = whole[:, :C] / amount
    var = whole[:, C : 2 * C] / amount - mean * mean
    rstd = lax.rsqrt(var + 1e-05)
    for load in loads[2:5]:
        load.wait()
    gain, shift = gamma[...], beta[...]

    def during_second():
        loads[6].wait()
        for t in range(8):
            feat_t[:, t * 256 : (t + 1) * 256] = feat[t * 256 : (t + 1) * 256, :].T
        loads[5].wait()
        when(has_last, lambda: note_ahead().wait_recv())

    def second_sums(t, sums):
        zhat = (pre[rows_at(t), :].astype(f32) - mean) * rstd
        act = gain * zhat + shift
        sig = jax.nn.sigmoid(act)
        g = cot[rows_at(t), :].astype(f32) * sig * (1.0 + act * (1.0 - sig))
        g = jnp.where(live_at(t), g, 0.0)
        grad[rows_at(t), :] = g
        return sums[0] + fold(g), sums[1] + fold(g * zhat)

    sum_g, sum_gz = lax.fori_loop(0, R // block, second_sums, (zero, zero))
    whole = all_sum(1, stacked(sum_g, sum_gz, 0.0), during_second)
    sums[0] = whole[:, :C]
    sums[1] = whole[:, C : 2 * C]
    scale = gain * rstd
    part_g, part_gz = whole[:, :C] / amount, whole[:, C : 2 * C] / amount

    @pl.loop(0, R // block)
    def _(t):
        zhat = (pre[rows_at(t), :].astype(f32) - mean) * rstd
        dz = scale * (grad[rows_at(t), :] - part_g - zhat * part_gz)
        table[rows_at(t), :] = jnp.where(live_at(t), dz, 0.0).astype(jnp.bfloat16)

    @pl.loop(0, 4)
    def _(t):
        at = pl.multiple_of(t * 176, 16)
        rows = dot(pick[pl.ds(at, 176), :], table[0:R, :], ((1,), (0,)))
        list_own[pl.ds(at, 176), :] = rows.astype(jnp.bfloat16)

    def hop(source, target, n, device):
        return pltpu.make_async_remote_copy(
            src_ref=source,
            dst_ref=target,
            send_sem=halo_sem.at[0, n],
            recv_sem=halo_sem.at[1, n],
            device_id=device,
            device_id_type=MESH,
        )

    lists = (list_left, list_own, list_right)

    def right():
        return hop(list_own, list_left, 3, {"gy": x + 1})

    def left():
        return hop(list_own, list_right, 5, {"gy": x - 1})

    def ahead(db):
        return hop(high.at[db], table.at[pl.ds(seg(db), HIGH), :], db, slab_id(slab + 1))

    def behind(db):
        target = table.at[pl.ds(seg(6 + db), WIN), :]
        return hop(lists[db].at[pl.ds(0, WIN), :], target, 6 + db, slab_id(slab - 1))

    def pass_on(db, mark):
        at = jnp.max(mark[...]) * 16
        high[db] = lists[db][pl.ds(at, HIGH), :]
        when(has_next, lambda: ahead(db).start())
        when(has_last, lambda: behind(db).start())

    when(has_right, lambda: right().start())
    when(has_left, lambda: left().start())
    pass_on(1, note_own)
    table[seg(4) : seg(5), :] = list_own[...]
    spare = plan(0, jnp.full((1, 128), FAR, f32))
    loads[7].wait()
    for db, there, came, mark in (
        (0, has_left, right, note_left),
        (2, has_right, left, note_right),
    ):
        when(there, lambda: came().wait_recv())
        when(there, lambda: pass_on(db, mark))
        table[seg(3 + db) : seg(4 + db), :] = lists[db][...]

    spare = plan(1, spare)
    row = lax.broadcasted_iota(jnp.int32, (8, 128), 0)
    starts[0:8, :] = jnp.where(row == 3, spare.astype(jnp.int32), starts[0:8, :])

    @pl.loop(0, 9)
    def _(g):
        for i in range(3):
            turned[g, i * C : (i + 1) * C, :] = weight[g * 3 + i].T

    for db, there in ((1, True), (0, has_left), (2, has_right)):
        when(has_last & there, lambda: ahead(db).wait_recv())
        when(has_next & there, lambda: behind(db).wait_recv())
    when(has_right, lambda: right().wait_send())
    when(has_left, lambda: left().wait_send())
    for db, there in ((1, True), (0, has_left), (2, has_right)):
        when(has_next & there, lambda: ahead(db).wait_send())
        when(has_last & there, lambda: behind(db).wait_send())
    when(has_right, lambda: note_to_right().wait_send())
    when(has_left, lambda: note_to_left().wait_send())
    when(has_next, lambda: note_ahead().wait_send())
    for copy in pending:
        copy.wait_send()


def front(counts, *arrays):
    vmem = pl.BlockSpec(memory_space=pltpu.VMEM)
    return pl.pallas_call(
        front_kernel,
        out_shape=(
            jax.ShapeDtypeStruct((ROWS, C), jnp.bfloat16),
            jax.ShapeDtypeStruct((9, R, 128), jnp.float32),
            jax.ShapeDtypeStruct((R // SUB * 8, 128), jnp.int32),
            jax.ShapeDtypeStruct((2, 1, C), jnp.float32),
            jax.ShapeDtypeStruct((C, R), jnp.bfloat16),
            jax.ShapeDtypeStruct((9, 3 * C, C), jnp.bfloat16),
        ),
        in_specs=[pl.BlockSpec(memory_space=pltpu.SMEM)]
        + [pl.BlockSpec(memory_space=pltpu.HBM)] * 8,
        out_specs=(vmem,) * 6,
        scratch_shapes=[pltpu.VMEM(a.shape, a.dtype) for a in arrays]
        + [
            pltpu.VMEM((R, C), jnp.float32),
            pltpu.VMEM((HB, R), jnp.bfloat16),
            pltpu.VMEM((2, 8, 1, 3 * C), jnp.float32),
            pltpu.VMEM((2, 16, 1, 3 * C), jnp.float32),
            pltpu.VMEM((HB, C), jnp.bfloat16),
            pltpu.VMEM((HB, C), jnp.bfloat16),
            pltpu.VMEM((HB, C), jnp.bfloat16),
            pltpu.VMEM((3, HIGH, C), jnp.bfloat16),
            *[pltpu.VMEM((8, 128), jnp.int32)] * 5,
            pltpu.SemaphoreType.DMA((8,)),
            pltpu.SemaphoreType.DMA((2, 2, 7)),
            pltpu.SemaphoreType.DMA((2, 2, 15)),
            pltpu.SemaphoreType.DMA((2, 9)),
            pltpu.SemaphoreType.DMA((2, 3)),
        ],
        compiler_params=pltpu.CompilerParams(
            collective_id=0, has_side_effects=True, vmem_limit_bytes=24 * 1024 * 1024
        ),
        cost_estimate=pl.CostEstimate(
            flops=1_000_000_000, bytes_accessed=10_000_000, transcendentals=1_000_000
        ),
        name="front",
    )(counts, *[pltpu.with_memory_space_constraint(a, pltpu.HBM) for a in arrays])


def body(features, pre_norm, out_grad, weight, gamma, beta, neighbors, boundary, counts):
    table, columns, starts, sums, feat_t, turned = front(
        counts,
        pre_norm[0, 0],
        out_grad[0, 0],
        gamma[None],
        beta[None],
        neighbors.reshape(27, 1, R),
        boundary.reshape(1, HB),
        features[0, 0],
        weight,
    )
    in_grad, local_wgrad, gamma_grad, beta_grad = convolve(
        starts, columns, table, feat_t, turned, sums
    )
    weight_grad = scatter_sum(local_wgrad)
    return (in_grad[None, None], weight_grad, gamma_grad[0], beta_grad[0])


def solution(mesh):
    torus = Mesh(mesh.devices.reshape(4, 4, 2, mesh.shape["gy"]), ("gx_0", "gx_1", "gx_2", "gy"))
    return jax.shard_map(
        body,
        mesh=torus,
        in_specs=(
            P(GX, "gy", None, None),
            P(GX, "gy", None, None),
            P(GX, "gy", None, None),
            P(),
            P(),
            P(),
            P(GX, "gy", None, None),
            P(GX, "gy", None),
            P(GX, "gy"),
        ),
        out_specs=(P(GX, "gy", None, None), P(GX_GY, None), P(), P()),
        check_vma=False,
    )
```

```python
import jax
import jax.numpy as jnp
from jax import lax
from jax.experimental import pallas as pl
from jax.experimental.pallas import tpu as pltpu
from jax.sharding import Mesh
from jax.sharding import PartitionSpec as P

GX_GY = ("gx_0", "gx_1", "gx_2", "gy")
GX = ("gx_0", "gx_1", "gx_2")
MESH = pl.DeviceIdType.MESH


C = 256
R = 2048
SUB = 128
WIN = 256
NROW = 8384
FAR = 1.0e6


def dot(a, b, dims):
    return lax.dot_general(a, b, (dims, ((), ())), preferred_element_type=jnp.float32)


def one_hot(columns, start):
    lanes = lax.broadcasted_iota(jnp.int32, (SUB, WIN), 1).astype(jnp.float32)
    place = columns - start.astype(jnp.float32)
    return jnp.where(place == lanes, 1.0, 0.0).astype(jnp.bfloat16)

def conv_kernel(
    starts, idx, table, feat_t, turned, sums_in, in_grad, wgrad, gamma_grad, beta_grad,
    acc, picked,
):
    acc[...] = jnp.zeros_like(acc)
    beta_grad[...] = sums_in[0]
    gamma_grad[...] = sums_in[1]

    @pl.loop(0, 9)
    def _(step):
        conv_group(step, starts, idx, table, feat_t, turned, wgrad, acc, picked)

    in_grad[...] = acc[...].astype(jnp.bfloat16)


def conv_group(step, starts, idx, table, feat_t, turned, wgrad, acc, picked):
    lane0 = 24 - 3 * step

    def columns_at(row):
        return idx[step, pl.ds(row, SUB), :]

    def window(columns, start):
        hot = [
            one_hot(jnp.broadcast_to(columns[:, 2 - i : 3 - i], (SUB, WIN)), start)
            for i in range(3)
        ]
        return jnp.concatenate(hot, axis=0)

    def gather(j):
        row = j * SUB
        columns = columns_at(row)
        s = [pl.multiple_of(starts[j * 8 + w, lane0], 16) for w in range(2)]
        hots = [window(columns, a) for a in s]
        tabs = [table[pl.ds(a, WIN), :] for a in s]
        total = dot(jnp.concatenate(hots, axis=1), jnp.concatenate(tabs, axis=0), ((1,), (0,)))
        total = total.astype(jnp.bfloat16)
        for i in range(3):
            picked[pl.ds(row, SUB), i * C : (i + 1) * C] = total[i * SUB : (i + 1) * SUB]

    def gather_rest(j):
        row = j * SUB

        def more(start):
            columns = columns_at(row)
            start = pl.multiple_of(start, 16)
            part = dot(window(columns, start), table[pl.ds(start, WIN), :], ((1,), (0,)))
            part = part.astype(jnp.bfloat16)
            for i in range(3):
                picked[pl.ds(row, SUB), i * C : (i + 1) * C] += part[i * SUB : (i + 1) * SUB]
            lane = lax.broadcasted_iota(jnp.int32, (SUB, 128), 1)
            ahead = (lane < 3) & (columns >= (start + WIN).astype(jnp.float32))
            low = jnp.min(jnp.where(ahead, columns, FAR)).astype(jnp.int32)
            return jnp.where(low < NROW, low // 16 * 16, jnp.int32(FAR))

        lax.while_loop(lambda start: start < NROW, more, starts[j * 8 + 2, lane0])

    for j in range(R // SUB):
        gather(j)

    @pl.when(starts[3, lane0] < NROW)
    def _():
        for j in range(R // SUB):
            gather_rest(j)

    for i in range(3):
        wgrad[step * 3 + i] = dot(feat_t[...], picked[:, i * C : (i + 1) * C], ((1,), (0,)))
    acc[...] += dot(picked[...], turned[step], ((1,), (0,)))


def convolve(starts, idx, table, feat_t, turned, sums):
    whole = pl.BlockSpec(memory_space=pltpu.VMEM)
    in_grad, wgrad, gamma_grad, beta_grad = pl.pallas_call(
        conv_kernel,
        out_shape=(
            jax.ShapeDtypeStruct((R, C), jnp.bfloat16),
            jax.ShapeDtypeStruct((27, C, C), jnp.float32),
            jax.ShapeDtypeStruct((1, C), jnp.float32),
            jax.ShapeDtypeStruct((1, C), jnp.float32),
        ),
        in_specs=[
            pl.BlockSpec(memory_space=pltpu.SMEM),
            whole,
            whole,
            whole,
            whole,
            whole,
        ],
        out_specs=(whole,) * 4,
        scratch_shapes=[
            pltpu.VMEM((R, C), jnp.float32),
            pltpu.VMEM((R, 3 * C), jnp.bfloat16),
        ],
        compiler_params=pltpu.CompilerParams(vmem_limit_bytes=20 * 1024 * 1024),
        cost_estimate=pl.CostEstimate(
            flops=30_000_000_000, bytes_accessed=20_000_000, transcendentals=0
        ),
        name="conv_backward",
    )(starts, idx, table, feat_t, turned, sums)
    return in_grad, wgrad.reshape(27 * C, C), gamma_grad, beta_grad


AXES = ("gy", "gx_1", "gx_0")
TILE_AT = (0, 16, 32, 38)
HOLDS = (((0, 0), (0, 1), (3, 0)), ((1, 0), (1, 1), (3, 1)), ((2, 0), (2, 1)))


def scatter_kernel(part, out, s_a, r_a, *rest):
    s_b, r_b, s_c, r_c, s_d, r_d = (rest[3 * i : 3 * i + 3] for i in range(6))
    a_sem, b_sem, c_sem, d_sem = rest[18:]
    pos = [lax.axis_index(a) for a in AXES]
    core = lax.axis_index("gx_2")
    z = pos[2]

    def around(i):
        return lax.rem(z + 1 + i, 4)

    barrier = pltpu.get_barrier_semaphore()
    pl.semaphore_signal(barrier, 1, device_id={"gx_2": 1 - core}, device_id_type=MESH)
    for axis, at in zip(AXES, pos):
        for d in range(1, 4):
            peer = {axis: lax.rem(at + d, 4)}
            pl.semaphore_signal(barrier, 1, device_id=peer, device_id_type=MESH)

    def block(i, y, x, side, t):
        skip = (x * 54 + TILE_AT[t]) % 8
        base = around(i) * 1728 + (y * 2 + side) * 216 + x * 54 + TILE_AT[t] - skip
        rows = part[pl.ds(pl.multiple_of(base, 8), 24 if skip else 16), :]
        return rows[skip : skip + 16]

    sends = []

    def send(src, dst, sems, at, device):
        copy = pltpu.make_async_remote_copy(
            src_ref=src,
            dst_ref=dst,
            send_sem=sems.at[(0,) + at],
            recv_sem=sems.at[(1,) + at],
            device_id=device,
            device_id_type=MESH,
        )
        copy.start()
        sends.append(copy)
        return copy

    first = []
    for i in range(4):
        @pl.loop(0, 4)
        def _(y):
            for x in range(4):
                for t in range(4):
                    mine = block(i, y, x, 1 - core, t)
                    s_a[i, y * 4 + x, t] = mine.astype(jnp.bfloat16)

        if i == 0:
            pl.semaphore_wait(barrier, 10)
        first.append(send(s_a.at[i], r_a.at[i], a_sem, (i,), {"gx_2": 1 - core}))

    def spread(p, stage, sems, src, dst):
        axis = (p + stage) % 3
        return [
            send(
                src.at[lax.rem(pos[axis] + d, 4)],
                dst.at[d - 1],
                sems,
                (p, d - 1),
                {AXES[axis]: lax.rem(pos[axis] + d, 4)},
            )
            for d in range(1, 4)
        ]

    second = [None, None, []]
    for i in range(4):
        first[i].wait_recv()
        z_of = around(i)

        @pl.loop(0, 4)
        def _(y):
            for x in range(4):
                for t in range(4):
                    both = block(i, y, x, core, t) + r_a[i, y * 4 + x, t].astype(jnp.float32)
                    both = both.astype(jnp.bfloat16)
                    for p, holds in enumerate(HOLDS):
                        for n, (tile, side) in enumerate(holds):
                            if tile != t:
                                continue
                            piece = both[:, side * 128 : (side + 1) * 128]
                            if p == 0:
                                s_b[0][x, y * 4 + z_of, n] = piece
                            elif p == 1:
                                s_b[1][y, z_of * 4 + x, n] = piece
                            else:
                                s_b[2][z_of, x * 4 + y, n] = piece

        if i < 3:
            second[2].append(
                send(s_b[2].at[z_of], r_b[2].at[i], b_sem, (2, i), {"gx_0": z_of})
            )
    for p in range(2):
        second[p] = spread(p, 0, b_sem, s_b[p], r_b[p])

    def total(own, came, at):
        kind = jnp.float32
        return (own[at].astype(kind) + came[(0,) + at[1:]].astype(kind)) + (
            came[(1,) + at[1:]].astype(kind) + came[(2,) + at[1:]].astype(kind)
        )

    third = [None] * 3
    for p in (2, 0, 1):
        for copy in second[p]:
            copy.wait_recv()
        me = pos[p]

        @pl.loop(0, 16, unroll=4)
        def _(j):
            for t in range(len(HOLDS[p])):
                s_c[p][j // 4, j % 4, t] = total(s_b[p], r_b[p], (me, j, t)).astype(jnp.bfloat16)

        third[p] = spread(p, 1, c_sem, s_c[p], r_c[p])

    fourth = [None] * 3
    for p in (2, 0, 1):
        for copy in third[p]:
            copy.wait_recv()
        me = pos[(p + 1) % 3]

        @pl.loop(0, 4, unroll=4)
        def _(j):
            for t in range(len(HOLDS[p])):
                s_d[p][j, t] = total(s_c[p], r_c[p], (me, j, t))

        fourth[p] = spread(p, 2, d_sem, s_d[p], r_d[p])

    for p in (2, 0, 1):
        for copy in fourth[p]:
            copy.wait_recv()
        me = pos[(p + 2) % 3]
        for n, (tile, side) in enumerate(HOLDS[p]):
            rows = pl.ds(TILE_AT[tile], 16)
            out[rows, side * 128 : (side + 1) * 128] = total(s_d[p], r_d[p], (me, n))

    for copy in sends:
        copy.wait_send()


def scatter_sum(part):
    def stage(lead, kind):
        return [pltpu.VMEM(lead + (len(h), 16, 128), kind) for h in HOLDS]

    half, full = jnp.bfloat16, jnp.float32
    return pl.pallas_call(
        scatter_kernel,
        out_shape=jax.ShapeDtypeStruct((54, C), jnp.float32),
        in_specs=[pl.BlockSpec(memory_space=pltpu.VMEM)],
        out_specs=pl.BlockSpec(memory_space=pltpu.VMEM),
        scratch_shapes=[
            pltpu.VMEM((4, 16, 4, 16, C), jnp.bfloat16),
            pltpu.VMEM((4, 16, 4, 16, C), jnp.bfloat16),
            *stage((4, 16), half),
            *stage((3, 16), half),
            *stage((4, 4), half),
            *stage((3, 4), half),
            *stage((4,), full),
            *stage((3,), full),
            pltpu.SemaphoreType.DMA((2, 4)),
            pltpu.SemaphoreType.DMA((2, 3, 3)),
            pltpu.SemaphoreType.DMA((2, 3, 3)),
            pltpu.SemaphoreType.DMA((2, 3, 3)),
        ],
        compiler_params=pltpu.CompilerParams(
            collective_id=1, has_side_effects=True, vmem_limit_bytes=24 * 1024 * 1024
        ),
        cost_estimate=pl.CostEstimate(flops=10_000_000, bytes_accessed=7_000_000, transcendentals=0),
        name="scatter_sum",
    )(part)


HB = 704
HIGH = 272
ROWS = NROW + WIN


def seg(b):
    return R + b * HB


def front_kernel(
    count, pre_in, cot_in, gamma_in, beta_in, links_in, border_in, feat_in, weight_in,
    table, columns, starts, sums, feat_t, turned,
    pre, cot, gamma, beta, links, border, feat, weight,
    grad, pick, near, far, list_left, list_own, list_right, high,
    note_own, note_left, note_right, note_out, note_in,
    load_sem, near_sem, far_sem, halo_sem, note_sem,
):
    f32 = jnp.float32
    z, y, core, x = (lax.axis_index(a) for a in GX_GY)
    slab = (z * 4 + y) * 2 + core
    me_near, me_far = x * 2 + core, z * 4 + y

    def near_id(p):
        return {"gy": p // 2, "gx_2": lax.rem(p, 2)}

    def far_id(p):
        return {"gx_0": p // 4, "gx_1": lax.rem(p, 4)}

    def slab_id(s):
        return {"gx_0": s // 8, "gx_1": lax.rem(s // 2, 4), "gx_2": lax.rem(s, 2)}

    loads = []
    for source, target in (
        (pre_in, pre),
        (border_in, border),
        (cot_in, cot),
        (gamma_in, gamma),
        (beta_in, beta),
        (links_in, links),
        (feat_in, feat),
        (weight_in, weight),
    ):
        loads.append(pltpu.make_async_copy(source, target, load_sem.at[len(loads)]))
        loads[-1].start()

    barrier = pltpu.get_barrier_semaphore()
    for d in range(1, 8):
        pl.semaphore_signal(
            barrier, 1, device_id=near_id(lax.rem(me_near + d, 8)), device_id_type=MESH
        )
    for d in range(1, 16):
        pl.semaphore_signal(
            barrier, 1, device_id=far_id(lax.rem(me_far + d, 16)), device_id_type=MESH
        )
    up, down = (core == 1) & (slab < 31), (core == 0) & (slab > 0)

    @pl.when(up)
    def _():
        pl.semaphore_signal(barrier, 1, device_id=slab_id(slab + 1), device_id_type=MESH)

    @pl.when(down)
    def _():
        pl.semaphore_signal(barrier, 1, device_id=slab_id(slab - 1), device_id_type=MESH)

    live_rows = count[0, 0]
    block = 128

    def live_at(t):
        row = lax.broadcasted_iota(jnp.int32, (block, C), 0) + t * block
        return row < live_rows

    def rows_at(t):
        return pl.ds(pl.multiple_of(t * block, block), block)

    def fold(a):
        return jnp.sum(a.reshape(block // 8, 8, C), axis=0)

    def first_sums(t, sums):
        zval = pre[rows_at(t), :].astype(f32)
        zlive = jnp.where(live_at(t), zval, 0.0)
        return sums[0] + fold(zlive), sums[1] + fold(zlive * zval)

    zero = jnp.zeros((8, C), f32)

    def stacked(a, b, *more):
        a, b = jnp.sum(a, axis=0, keepdims=True), jnp.sum(b, axis=0, keepdims=True)
        return jnp.concatenate([a, b] + [jnp.full((1, C), c, f32) for c in more], axis=1)

    def exchange(slots, me, size, sems, turn, ids):
        copies = []
        for d in range(1, size):
            copies.append(
                pltpu.make_async_remote_copy(
                    src_ref=slots.at[turn, me],
                    dst_ref=slots.at[turn, me],
                    send_sem=sems.at[turn, 0, d - 1],
                    recv_sem=sems.at[turn, 1, d - 1],
                    device_id=ids(lax.rem(me + d, size)),
                    device_id_type=MESH,
                )
            )
            copies[-1].start()
        return copies

    def add_up(slots, size, turn, copies):
        for copy in copies:
            copy.wait_recv()
        total = slots[turn, 0]
        for i in range(1, size):
            total = total + slots[turn, i]
        return total

    pending = []

    def all_sum(turn, value, meanwhile):
        near[turn, me_near] = value
        one = exchange(near, me_near, 8, near_sem, turn, near_id)
        meanwhile()
        far[turn, me_far] = add_up(near, 8, turn, one)
        two = exchange(far, me_far, 16, far_sem, turn, far_id)
        pending.extend(one + two)
        return add_up(far, 16, turn, two)

    def when(cond, act):
        @pl.when(cond)
        def _():
            act()

    has_right, has_left, has_next, has_last = x < 3, x > 0, slab < 31, slab > 0

    def note(source, target, n, device):
        return pltpu.make_async_remote_copy(
            src_ref=source,
            dst_ref=target,
            send_sem=note_sem.at[0, n],
            recv_sem=note_sem.at[1, n],
            device_id=device,
            device_id_type=MESH,
        )

    def note_to_right():
        return note(note_own, note_left, 0, {"gy": x + 1})

    def note_to_left():
        return note(note_own, note_right, 1, {"gy": x - 1})

    def note_ahead():
        return note(note_out, note_in, 2, slab_id(slab + 1))

    def blank(ref):
        ref[...] = jnp.zeros_like(ref)

    def notes_first():
        size = jnp.sum(jnp.where(border[...] < R, 1, 0), axis=1, keepdims=True)
        first = jnp.minimum(jnp.maximum(size - WIN, 0) // 16, (HB - HIGH) // 16)
        note_own[...] = jnp.broadcast_to(first, (8, 128))
        when(~has_left, lambda: blank(note_left))
        when(~has_right, lambda: blank(note_right))
        when(~has_last, lambda: blank(note_in))

    def notes_second():
        when(has_left, lambda: note_to_right().wait_recv())
        when(has_right, lambda: note_to_left().wait_recv())
        row = lax.broadcasted_iota(jnp.int32, (8, 128), 0)
        note_out[...] = jnp.where(
            row == 0, note_left[...], jnp.where(row == 1, note_own[...], note_right[...])
        )
        when(has_next, lambda: note_ahead().start())

    def plan(part, spare):
        moved = [note_in[b : b + 1, :] * 16 for b in range(3)]
        lane = lax.broadcasted_iota(jnp.int32, (1, 128), 1)
        third = lax.rem(lane, 3)

        def one(j, spare):
            at = pl.ds(pl.multiple_of(j * SUB, SUB), SUB)
            idx = links[:, 0, at]
            for b in range(3):
                inside = (idx >= seg(b)) & (idx < seg(b + 1))
                idx = jnp.where(inside, idx - moved[b], idx)
            idx = jnp.where(idx < NROW, idx, jnp.int32(FAR)).astype(f32)
            idx = jnp.concatenate([idx, jnp.full((101, SUB), FAR, f32)], axis=0).T
            for g in range(9):
                shift = (104 + 3 * g) % 128
                columns[g, at, :] = pltpu.roll(idx, shift, 1)
            begin = []
            for w in range(3):
                low = jnp.min(idx, axis=0, keepdims=True)
                low = jnp.minimum(low, jnp.minimum(pltpu.roll(low, 127, 1), pltpu.roll(low, 126, 1)))
                low = jnp.where(
                    third == 0,
                    low,
                    jnp.where(third == 1, pltpu.roll(low, 1, 1), pltpu.roll(low, 2, 1)),
                )
                start = jnp.where(low < NROW, jnp.floor(low * 0.0625) * 16.0, FAR)
                idx = jnp.where(idx >= start + WIN, idx, FAR)
                begin.append(jnp.minimum(start, float(NROW)) if w < 2 else start)
            spare = jnp.minimum(spare, begin[2])
            begin = [jnp.broadcast_to(b, (8, 128)) for b in begin]
            row = lax.broadcasted_iota(jnp.int32, (8, 128), 0)
            begin = jnp.where(row == 0, begin[0], jnp.where(row == 1, begin[1], begin[2]))
            starts[pl.ds(pl.multiple_of(j * 8, 8), 8), :] = begin.astype(jnp.int32)
            return spare

        def some(n, spare):
            for u in range(4):
                spare = one(part * 8 + n * 4 + u, spare)
            return spare

        return lax.fori_loop(0, 2, some, spare)

    def choose():
        lane = lax.broadcasted_iota(jnp.int32, (128, 128), 1)
        for t in range(6):
            width = min(128, HB - t * 128)
            names = border[:, t * 128 : t * 128 + width].astype(f32)
            if width < 128:
                names = jnp.concatenate([names, jnp.full((1, 128 - width), FAR, f32)], axis=1)
            names = jnp.broadcast_to(names, (128, 128)).T[:width]
            for c in range(R // 128):
                row = (lane[:width] + c * 128).astype(f32)
                pick[t * 128 : t * 128 + width, c * 128 : (c + 1) * 128] = jnp.where(
                    names == row, 1.0, 0.0
                ).astype(jnp.bfloat16)

        def clear(at, size):
            table[at : at + size, :] = jnp.zeros((size, C), jnp.bfloat16)

        clear(NROW, WIN)

        @pl.when(slab == 0)
        def _():
            for b in (0, 1, 2):
                clear(seg(b), HIGH)

        @pl.when(slab == 31)
        def _():
            for b in (6, 7, 8):
                clear(seg(b), WIN)

        for b in (0, 1, 2):
            clear(seg(b) + HIGH, HB - HIGH)

        for b in (6, 7, 8):
            clear(seg(b) + WIN, HB - WIN)

        for edge, db, missing in ((0, 0, list_left), (3, 2, list_right)):
            @pl.when(x == edge)
            def _():
                blank(missing)

                @pl.when(slab > 0)
                def _():
                    clear(seg(db), HIGH)

                @pl.when(slab < 31)
                def _():
                    clear(seg(6 + db), WIN)

    loads[0].wait()
    sum_z, sum_sq = lax.fori_loop(0, R // block, first_sums, (zero, zero))
    loads[1].wait()
    notes_first()
    extra = jnp.where(up | down, 1, 0)
    pl.semaphore_wait(barrier, 22 + extra)
    when(has_right, lambda: note_to_right().start())
    when(has_left, lambda: note_to_left().start())

    def during_first():
        choose()
        notes_second()

    whole = all_sum(0, stacked(sum_z, sum_sq, live_rows.astype(f32)), during_first)
    amount = whole[:, 2 * C :]
    mean = whole[:, :C] / amount
    var = whole[:, C : 2 * C] / amount - mean * mean
    rstd = lax.rsqrt(var + 1e-05)
    for load in loads[2:5]:
        load.wait()
    gain, shift = gamma[...], beta[...]

    def during_second():
        loads[6].wait()
        for t in range(8):
            feat_t[:, t * 256 : (t + 1) * 256] = feat[t * 256 : (t + 1) * 256, :].T
        loads[5].wait()
        when(has_last, lambda: note_ahead().wait_recv())

    def second_sums(t, sums):
        zhat = (pre[rows_at(t), :].astype(f32) - mean) * rstd
        act = gain * zhat + shift
        sig = jax.nn.sigmoid(act)
        g = cot[rows_at(t), :].astype(f32) * sig * (1.0 + act * (1.0 - sig))
        g = jnp.where(live_at(t), g, 0.0)
        grad[rows_at(t), :] = g
        return sums[0] + fold(g), sums[1] + fold(g * zhat)

    sum_g, sum_gz = lax.fori_loop(0, R // block, second_sums, (zero, zero))
    whole = all_sum(1, stacked(sum_g, sum_gz, 0.0), during_second)
    sums[0] = whole[:, :C]
    sums[1] = whole[:, C : 2 * C]
    scale = gain * rstd
    part_g, part_gz = whole[:, :C] / amount, whole[:, C : 2 * C] / amount

    @pl.loop(0, R // block)
    def _(t):
        zhat = (pre[rows_at(t), :].astype(f32) - mean) * rstd
        dz = scale * (grad[rows_at(t), :] - part_g - zhat * part_gz)
        table[rows_at(t), :] = jnp.where(live_at(t), dz, 0.0).astype(jnp.bfloat16)

    @pl.loop(0, 4)
    def _(t):
        at = pl.multiple_of(t * 176, 16)
        rows = dot(pick[pl.ds(at, 176), :], table[0:R, :], ((1,), (0,)))
        list_own[pl.ds(at, 176), :] = rows.astype(jnp.bfloat16)

    def hop(source, target, n, device):
        return pltpu.make_async_remote_copy(
            src_ref=source,
            dst_ref=target,
            send_sem=halo_sem.at[0, n],
            recv_sem=halo_sem.at[1, n],
            device_id=device,
            device_id_type=MESH,
        )

    lists = (list_left, list_own, list_right)

    def right():
        return hop(list_own, list_left, 3, {"gy": x + 1})

    def left():
        return hop(list_own, list_right, 5, {"gy": x - 1})

    def ahead(db):
        return hop(high.at[db], table.at[pl.ds(seg(db), HIGH), :], db, slab_id(slab + 1))

    def behind(db):
        target = table.at[pl.ds(seg(6 + db), WIN), :]
        return hop(lists[db].at[pl.ds(0, WIN), :], target, 6 + db, slab_id(slab - 1))

    def pass_on(db, mark):
        at = jnp.max(mark[...]) * 16
        high[db] = lists[db][pl.ds(at, HIGH), :]
        when(has_next, lambda: ahead(db).start())
        when(has_last, lambda: behind(db).start())

    when(has_right, lambda: right().start())
    when(has_left, lambda: left().start())
    pass_on(1, note_own)
    table[seg(4) : seg(5), :] = list_own[...]
    spare = plan(0, jnp.full((1, 128), FAR, f32))
    loads[7].wait()
    for db, there, came, mark in (
        (0, has_left, right, note_left),
        (2, has_right, left, note_right),
    ):
        when(there, lambda: came().wait_recv())
        when(there, lambda: pass_on(db, mark))
        table[seg(3 + db) : seg(4 + db), :] = lists[db][...]

    spare = plan(1, spare)
    row = lax.broadcasted_iota(jnp.int32, (8, 128), 0)
    starts[0:8, :] = jnp.where(row == 3, spare.astype(jnp.int32), starts[0:8, :])

    @pl.loop(0, 9)
    def _(g):
        for i in range(3):
            turned[g, i * C : (i + 1) * C, :] = weight[g * 3 + i].T

    for db, there in ((1, True), (0, has_left), (2, has_right)):
        when(has_last & there, lambda: ahead(db).wait_recv())
        when(has_next & there, lambda: behind(db).wait_recv())
    when(has_right, lambda: right().wait_send())
    when(has_left, lambda: left().wait_send())
    for db, there in ((1, True), (0, has_left), (2, has_right)):
        when(has_next & there, lambda: ahead(db).wait_send())
        when(has_last & there, lambda: behind(db).wait_send())
    when(has_right, lambda: note_to_right().wait_send())
    when(has_left, lambda: note_to_left().wait_send())
    when(has_next, lambda: note_ahead().wait_send())
    for copy in pending:
        copy.wait_send()


def front(counts, *arrays):
    vmem = pl.BlockSpec(memory_space=pltpu.VMEM)
    return pl.pallas_call(
        front_kernel,
        out_shape=(
            jax.ShapeDtypeStruct((ROWS, C), jnp.bfloat16),
            jax.ShapeDtypeStruct((9, R, 128), jnp.float32),
            jax.ShapeDtypeStruct((R // SUB * 8, 128), jnp.int32),
            jax.ShapeDtypeStruct((2, 1, C), jnp.float32),
            jax.ShapeDtypeStruct((C, R), jnp.bfloat16),
            jax.ShapeDtypeStruct((9, 3 * C, C), jnp.bfloat16),
        ),
        in_specs=[pl.BlockSpec(memory_space=pltpu.SMEM)]
        + [pl.BlockSpec(memory_space=pltpu.HBM)] * 8,
        out_specs=(vmem,) * 6,
        scratch_shapes=[pltpu.VMEM(a.shape, a.dtype) for a in arrays]
        + [
            pltpu.VMEM((R, C), jnp.float32),
            pltpu.VMEM((HB, R), jnp.bfloat16),
            pltpu.VMEM((2, 8, 1, 3 * C), jnp.float32),
            pltpu.VMEM((2, 16, 1, 3 * C), jnp.float32),
            pltpu.VMEM((HB, C), jnp.bfloat16),
            pltpu.VMEM((HB, C), jnp.bfloat16),
            pltpu.VMEM((HB, C), jnp.bfloat16),
            pltpu.VMEM((3, HIGH, C), jnp.bfloat16),
            *[pltpu.VMEM((8, 128), jnp.int32)] * 5,
            pltpu.SemaphoreType.DMA((8,)),
            pltpu.SemaphoreType.DMA((2, 2, 7)),
            pltpu.SemaphoreType.DMA((2, 2, 15)),
            pltpu.SemaphoreType.DMA((2, 9)),
            pltpu.SemaphoreType.DMA((2, 3)),
        ],
        compiler_params=pltpu.CompilerParams(
            collective_id=0, has_side_effects=True, vmem_limit_bytes=24 * 1024 * 1024
        ),
        cost_estimate=pl.CostEstimate(
            flops=1_000_000_000, bytes_accessed=10_000_000, transcendentals=1_000_000
        ),
        name="front",
    )(counts, *[pltpu.with_memory_space_constraint(a, pltpu.HBM) for a in arrays])


def body(features, pre_norm, out_grad, weight, gamma, beta, neighbors, boundary, counts):
    table, columns, starts, sums, feat_t, turned = front(
        counts,
        pre_norm[0, 0],
        out_grad[0, 0],
        gamma[None],
        beta[None],
        neighbors.reshape(27, 1, R),
        boundary.reshape(1, HB),
        features[0, 0],
        weight,
    )
    in_grad, local_wgrad, gamma_grad, beta_grad = convolve(
        starts, columns, table, feat_t, turned, sums
    )
    weight_grad = scatter_sum(local_wgrad)
    return (in_grad[None, None], weight_grad, gamma_grad[0], beta_grad[0])


def solution(mesh):
    torus = Mesh(mesh.devices.reshape(4, 4, 2, mesh.shape["gy"]), ("gx_0", "gx_1", "gx_2", "gy"))
    return jax.shard_map(
        body,
        mesh=torus,
        in_specs=(
            P(GX, "gy", None, None),
            P(GX, "gy", None, None),
            P(GX, "gy", None, None),
            P(),
            P(),
            P(),
            P(GX, "gy", None, None),
            P(GX, "gy", None),
            P(GX, "gy"),
        ),
        out_specs=(P(GX, "gy", None, None), P(GX_GY, None), P(), P()),
        check_vma=False,
    )
```

```python
import jax
import jax.numpy as jnp
from jax import lax
from jax.experimental import pallas as pl
from jax.experimental.pallas import tpu as pltpu
from jax.sharding import Mesh
from jax.sharding import PartitionSpec as P

GX_GY = ("gx_0", "gx_1", "gx_2", "gy")
GX = ("gx_0", "gx_1", "gx_2")
MESH = pl.DeviceIdType.MESH


C = 256
R = 2048
SUB = 128
WIN = 256
NROW = 8384
FAR = 1.0e6


def dot(a, b, dims):
    return lax.dot_general(a, b, (dims, ((), ())), preferred_element_type=jnp.float32)


def one_hot(columns, start):
    lanes = lax.broadcasted_iota(jnp.int32, (SUB, WIN), 1).astype(jnp.float32)
    place = columns - start.astype(jnp.float32)
    return jnp.where(place == lanes, 1.0, 0.0).astype(jnp.bfloat16)

def conv_kernel(
    starts, idx, table, feat_t, turned, sums_in, in_grad, wgrad, gamma_grad, beta_grad,
    acc, picked,
):
    acc[...] = jnp.zeros_like(acc)
    beta_grad[...] = sums_in[0]
    gamma_grad[...] = sums_in[1]

    @pl.loop(0, 9)
    def _(step):
        conv_group(step, starts, idx, table, feat_t, turned, wgrad, acc, picked)

    in_grad[...] = acc[...].astype(jnp.bfloat16)


def conv_group(step, starts, idx, table, feat_t, turned, wgrad, acc, picked):
    lane0 = 24 - 3 * step

    def columns_at(row):
        return idx[step, pl.ds(row, SUB), :]

    def window(columns, start):
        hot = [
            one_hot(jnp.broadcast_to(columns[:, 2 - i : 3 - i], (SUB, WIN)), start)
            for i in range(3)
        ]
        return jnp.concatenate(hot, axis=0)

    def gather(j):
        row = j * SUB
        columns = columns_at(row)
        s = [pl.multiple_of(starts[j * 8 + w, lane0], 16) for w in range(2)]
        hots = [window(columns, a) for a in s]
        tabs = [table[pl.ds(a, WIN), :] for a in s]
        total = dot(jnp.concatenate(hots, axis=1), jnp.concatenate(tabs, axis=0), ((1,), (0,)))
        total = total.astype(jnp.bfloat16)
        for i in range(3):
            picked[pl.ds(row, SUB), i * C : (i + 1) * C] = total[i * SUB : (i + 1) * SUB]

    def gather_rest(j):
        row = j * SUB

        def more(start):
            columns = columns_at(row)
            start = pl.multiple_of(start, 16)
            part = dot(window(columns, start), table[pl.ds(start, WIN), :], ((1,), (0,)))
            part = part.astype(jnp.bfloat16)
            for i in range(3):
                picked[pl.ds(row, SUB), i * C : (i + 1) * C] += part[i * SUB : (i + 1) * SUB]
            lane = lax.broadcasted_iota(jnp.int32, (SUB, 128), 1)
            ahead = (lane < 3) & (columns >= (start + WIN).astype(jnp.float32))
            low = jnp.min(jnp.where(ahead, columns, FAR)).astype(jnp.int32)
            return jnp.where(low < NROW, low // 16 * 16, jnp.int32(FAR))

        lax.while_loop(lambda start: start < NROW, more, starts[j * 8 + 2, lane0])

    for j in range(R // SUB):
        gather(j)

    @pl.when(starts[3, lane0] < NROW)
    def _():
        for j in range(R // SUB):
            gather_rest(j)

    for i in range(3):
        wgrad[step * 3 + i] = dot(feat_t[...], picked[:, i * C : (i + 1) * C], ((1,), (0,)))
    acc[...] += dot(picked[...], turned[step], ((1,), (0,)))


def convolve(starts, idx, table, feat_t, turned, sums):
    whole = pl.BlockSpec(memory_space=pltpu.VMEM)
    in_grad, wgrad, gamma_grad, beta_grad = pl.pallas_call(
        conv_kernel,
        out_shape=(
            jax.ShapeDtypeStruct((R, C), jnp.bfloat16),
            jax.ShapeDtypeStruct((27, C, C), jnp.float32),
            jax.ShapeDtypeStruct((1, C), jnp.float32),
            jax.ShapeDtypeStruct((1, C), jnp.float32),
        ),
        in_specs=[
            pl.BlockSpec(memory_space=pltpu.SMEM),
            whole,
            whole,
            whole,
            whole,
            whole,
        ],
        out_specs=(whole,) * 4,
        scratch_shapes=[
            pltpu.VMEM((R, C), jnp.float32),
            pltpu.VMEM((R, 3 * C), jnp.bfloat16),
        ],
        compiler_params=pltpu.CompilerParams(vmem_limit_bytes=20 * 1024 * 1024),
        cost_estimate=pl.CostEstimate(
            flops=30_000_000_000, bytes_accessed=20_000_000, transcendentals=0
        ),
        name="conv_backward",
    )(starts, idx, table, feat_t, turned, sums)
    return in_grad, wgrad.reshape(27 * C, C), gamma_grad, beta_grad


AXES = ("gy", "gx_1", "gx_0")
TILE_AT = (0, 16, 32, 38)
HOLDS = (((0, 0), (0, 1), (3, 0)), ((1, 0), (1, 1), (3, 1)), ((2, 0), (2, 1)))


def scatter_kernel(part, out, s_a, r_a, *rest):
    s_b, r_b, s_c, r_c, s_d, r_d = (rest[3 * i : 3 * i + 3] for i in range(6))
    a_sem, b_sem, c_sem, d_sem = rest[18:]
    pos = [lax.axis_index(a) for a in AXES]
    core = lax.axis_index("gx_2")
    z = pos[2]

    def around(i):
        return lax.rem(z + 1 + i, 4)

    barrier = pltpu.get_barrier_semaphore()
    pl.semaphore_signal(barrier, 1, device_id={"gx_2": 1 - core}, device_id_type=MESH)
    for axis, at in zip(AXES, pos):
        for d in range(1, 4):
            peer = {axis: lax.rem(at + d, 4)}
            pl.semaphore_signal(barrier, 1, device_id=peer, device_id_type=MESH)

    def block(i, y, x, side, t):
        skip = (x * 54 + TILE_AT[t]) % 8
        base = around(i) * 1728 + (y * 2 + side) * 216 + x * 54 + TILE_AT[t] - skip
        rows = part[pl.ds(pl.multiple_of(base, 8), 24 if skip else 16), :]
        return rows[skip : skip + 16]

    sends = []

    def send(src, dst, sems, at, device):
        copy = pltpu.make_async_remote_copy(
            src_ref=src,
            dst_ref=dst,
            send_sem=sems.at[(0,) + at],
            recv_sem=sems.at[(1,) + at],
            device_id=device,
            device_id_type=MESH,
        )
        copy.start()
        sends.append(copy)
        return copy

    first = []
    for i in range(4):
        @pl.loop(0, 4)
        def _(y):
            for x in range(4):
                for t in range(4):
                    mine = block(i, y, x, 1 - core, t)
                    s_a[i, y * 4 + x, t] = mine.astype(jnp.bfloat16)

        if i == 0:
            pl.semaphore_wait(barrier, 10)
        first.append(send(s_a.at[i], r_a.at[i], a_sem, (i,), {"gx_2": 1 - core}))

    def spread(p, stage, sems, src, dst):
        axis = (p + stage) % 3
        return [
            send(
                src.at[lax.rem(pos[axis] + d, 4)],
                dst.at[d - 1],
                sems,
                (p, d - 1),
                {AXES[axis]: lax.rem(pos[axis] + d, 4)},
            )
            for d in range(1, 4)
        ]

    second = [[], [], []]
    for i in range(4):
        first[i].wait_recv()
        z_of = around(i)

        @pl.loop(0, 4)
        def _(y):
            for x in range(4):
                for t in range(4):
                    both = block(i, y, x, core, t) + r_a[i, y * 4 + x, t].astype(jnp.float32)
                    both = both.astype(jnp.bfloat16)
                    for p, holds in enumerate(HOLDS):
                        for n, (tile, side) in enumerate(holds):
                            if tile != t:
                                continue
                            piece = both[:, side * 128 : (side + 1) * 128]
                            if p == 0:
                                s_b[0][x, i * 4 + y, n] = piece
                            elif p == 1:
                                s_b[1][y, i * 4 + x, n] = piece
                            else:
                                s_b[2][z_of, x * 4 + y, n] = piece

        if i < 3:
            second[2].append(
                send(s_b[2].at[z_of], r_b[2].at[i], b_sem, (2, i), {"gx_0": z_of})
            )
        if i % 2:
            part_of = pl.ds((i - 1) * 4, 8)
            for p in range(2):
                for d in range(1, 4):
                    peer = lax.rem(pos[p] + d, 4)
                    second[p].append(
                        send(
                            s_b[p].at[peer, part_of],
                            r_b[p].at[d - 1, part_of],
                            b_sem,
                            (p, i // 2 * 3 + d - 1),
                            {AXES[p]: peer},
                        )
                    )

    def total(own, came, at):
        kind = jnp.float32
        return (own[at].astype(kind) + came[(0,) + at[1:]].astype(kind)) + (
            came[(1,) + at[1:]].astype(kind) + came[(2,) + at[1:]].astype(kind)
        )

    third = [None] * 3
    for p in (2, 0, 1):
        for copy in second[p]:
            copy.wait_recv()
        me = pos[p]

        @pl.loop(0, 16)
        def _(j):
            for t in range(len(HOLDS[p])):
                piece = total(s_b[p], r_b[p], (me, j, t)).astype(jnp.bfloat16)
                if p == 0:
                    s_c[p][j % 4, around(j // 4), t] = piece
                elif p == 1:
                    s_c[p][around(j // 4), j % 4, t] = piece
                else:
                    s_c[p][j // 4, j % 4, t] = piece

        third[p] = spread(p, 1, c_sem, s_c[p], r_c[p])

    fourth = [None] * 3
    for p in (2, 0, 1):
        for copy in third[p]:
            copy.wait_recv()
        me = pos[(p + 1) % 3]

        @pl.loop(0, 4)
        def _(j):
            for t in range(len(HOLDS[p])):
                s_d[p][j, t] = total(s_c[p], r_c[p], (me, j, t))

        fourth[p] = spread(p, 2, d_sem, s_d[p], r_d[p])

    for p in (2, 0, 1):
        for copy in fourth[p]:
            copy.wait_recv()
        me = pos[(p + 2) % 3]
        for n, (tile, side) in enumerate(HOLDS[p]):
            rows = pl.ds(TILE_AT[tile], 16)
            out[rows, side * 128 : (side + 1) * 128] = total(s_d[p], r_d[p], (me, n))

    for copy in sends:
        copy.wait_send()


def scatter_sum(part):
    def stage(lead, kind):
        return [pltpu.VMEM(lead + (len(h), 16, 128), kind) for h in HOLDS]

    half, full = jnp.bfloat16, jnp.float32
    return pl.pallas_call(
        scatter_kernel,
        out_shape=jax.ShapeDtypeStruct((54, C), jnp.float32),
        in_specs=[pl.BlockSpec(memory_space=pltpu.VMEM)],
        out_specs=pl.BlockSpec(memory_space=pltpu.VMEM),
        scratch_shapes=[
            pltpu.VMEM((4, 16, 4, 16, C), jnp.bfloat16),
            pltpu.VMEM((4, 16, 4, 16, C), jnp.bfloat16),
            *stage((4, 16), half),
            *stage((3, 16), half),
            *stage((4, 4), half),
            *stage((3, 4), half),
            *stage((4,), full),
            *stage((3,), full),
            pltpu.SemaphoreType.DMA((2, 4)),
            pltpu.SemaphoreType.DMA((2, 3, 6)),
            pltpu.SemaphoreType.DMA((2, 3, 3)),
            pltpu.SemaphoreType.DMA((2, 3, 3)),
        ],
        compiler_params=pltpu.CompilerParams(
            collective_id=1, has_side_effects=True, vmem_limit_bytes=24 * 1024 * 1024
        ),
        cost_estimate=pl.CostEstimate(flops=10_000_000, bytes_accessed=7_000_000, transcendentals=0),
        name="scatter_sum",
    )(part)


HB = 704
HIGH = 272
ROWS = NROW + WIN


def seg(b):
    return R + b * HB


def front_kernel(
    count, pre_in, cot_in, gamma_in, beta_in, links_in, border_in, feat_in, weight_in,
    table, columns, starts, sums, feat_t, turned,
    pre, cot, gamma, beta, links, border, feat, weight,
    grad, pick, near, far, list_left, list_own, list_right, high,
    note_own, note_left, note_right, note_out, note_in,
    load_sem, near_sem, far_sem, halo_sem, note_sem,
):
    f32 = jnp.float32
    z, y, core, x = (lax.axis_index(a) for a in GX_GY)
    slab = (z * 4 + y) * 2 + core
    me_near, me_far = x * 2 + core, z * 4 + y

    def near_id(p):
        return {"gy": p // 2, "gx_2": lax.rem(p, 2)}

    def far_id(p):
        return {"gx_0": p // 4, "gx_1": lax.rem(p, 4)}

    def slab_id(s):
        return {"gx_0": s // 8, "gx_1": lax.rem(s // 2, 4), "gx_2": lax.rem(s, 2)}

    loads = []
    for source, target in (
        (pre_in, pre),
        (border_in, border),
        (cot_in, cot),
        (gamma_in, gamma),
        (beta_in, beta),
        (links_in, links),
        (feat_in, feat),
        (weight_in, weight),
    ):
        loads.append(pltpu.make_async_copy(source, target, load_sem.at[len(loads)]))
        loads[-1].start()

    barrier = pltpu.get_barrier_semaphore()
    for d in range(1, 8):
        pl.semaphore_signal(
            barrier, 1, device_id=near_id(lax.rem(me_near + d, 8)), device_id_type=MESH
        )
    for d in range(1, 16):
        pl.semaphore_signal(
            barrier, 1, device_id=far_id(lax.rem(me_far + d, 16)), device_id_type=MESH
        )
    up, down = (core == 1) & (slab < 31), (core == 0) & (slab > 0)

    @pl.when(up)
    def _():
        pl.semaphore_signal(barrier, 1, device_id=slab_id(slab + 1), device_id_type=MESH)

    @pl.when(down)
    def _():
        pl.semaphore_signal(barrier, 1, device_id=slab_id(slab - 1), device_id_type=MESH)

    live_rows = count[0, 0]
    block = 128

    def live_at(t):
        row = lax.broadcasted_iota(jnp.int32, (block, C), 0) + t * block
        return row < live_rows

    def rows_at(t):
        return pl.ds(pl.multiple_of(t * block, block), block)

    def fold(a):
        return jnp.sum(a.reshape(block // 8, 8, C), axis=0)

    def first_sums(t, sums):
        zval = pre[rows_at(t), :].astype(f32)
        zlive = jnp.where(live_at(t), zval, 0.0)
        return sums[0] + fold(zlive), sums[1] + fold(zlive * zval)

    zero = jnp.zeros((8, C), f32)

    def stacked(a, b, *more):
        a, b = jnp.sum(a, axis=0, keepdims=True), jnp.sum(b, axis=0, keepdims=True)
        return jnp.concatenate([a, b] + [jnp.full((1, C), c, f32) for c in more], axis=1)

    def exchange(slots, me, size, sems, turn, ids):
        copies = []
        for d in range(1, size):
            copies.append(
                pltpu.make_async_remote_copy(
                    src_ref=slots.at[turn, me],
                    dst_ref=slots.at[turn, me],
                    send_sem=sems.at[turn, 0, d - 1],
                    recv_sem=sems.at[turn, 1, d - 1],
                    device_id=ids(lax.rem(me + d, size)),
                    device_id_type=MESH,
                )
            )
            copies[-1].start()
        return copies

    def add_up(slots, size, turn, copies):
        for copy in copies:
            copy.wait_recv()
        total = slots[turn, 0]
        for i in range(1, size):
            total = total + slots[turn, i]
        return total

    pending = []

    def all_sum(turn, value, meanwhile):
        near[turn, me_near] = value
        one = exchange(near, me_near, 8, near_sem, turn, near_id)
        meanwhile()
        far[turn, me_far] = add_up(near, 8, turn, one)
        two = exchange(far, me_far, 16, far_sem, turn, far_id)
        pending.extend(one + two)
        return add_up(far, 16, turn, two)

    def when(cond, act):
        @pl.when(cond)
        def _():
            act()

    has_right, has_left, has_next, has_last = x < 3, x > 0, slab < 31, slab > 0

    def note(source, target, n, device):
        return pltpu.make_async_remote_copy(
            src_ref=source,
            dst_ref=target,
            send_sem=note_sem.at[0, n],
            recv_sem=note_sem.at[1, n],
            device_id=device,
            device_id_type=MESH,
        )

    def note_to_right():
        return note(note_own, note_left, 0, {"gy": x + 1})

    def note_to_left():
        return note(note_own, note_right, 1, {"gy": x - 1})

    def note_ahead():
        return note(note_out, note_in, 2, slab_id(slab + 1))

    def blank(ref):
        ref[...] = jnp.zeros_like(ref)

    def notes_first():
        size = jnp.sum(jnp.where(border[...] < R, 1, 0), axis=1, keepdims=True)
        first = jnp.minimum(jnp.maximum(size - WIN, 0) // 16, (HB - HIGH) // 16)
        note_own[...] = jnp.broadcast_to(first, (8, 128))
        when(~has_left, lambda: blank(note_left))
        when(~has_right, lambda: blank(note_right))
        when(~has_last, lambda: blank(note_in))

    def notes_second():
        when(has_left, lambda: note_to_right().wait_recv())
        when(has_right, lambda: note_to_left().wait_recv())
        row = lax.broadcasted_iota(jnp.int32, (8, 128), 0)
        note_out[...] = jnp.where(
            row == 0, note_left[...], jnp.where(row == 1, note_own[...], note_right[...])
        )
        when(has_next, lambda: note_ahead().start())

    def plan(part, spare):
        moved = [note_in[b : b + 1, :] * 16 for b in range(3)]
        lane = lax.broadcasted_iota(jnp.int32, (1, 128), 1)
        third = lax.rem(lane, 3)

        def one(j, spare):
            at = pl.ds(pl.multiple_of(j * SUB, SUB), SUB)
            idx = links[:, 0, at]
            for b in range(3):
                inside = (idx >= seg(b)) & (idx < seg(b + 1))
                idx = jnp.where(inside, idx - moved[b], idx)
            idx = jnp.where(idx < NROW, idx, jnp.int32(FAR)).astype(f32)
            idx = jnp.concatenate([idx, jnp.full((101, SUB), FAR, f32)], axis=0).T
            for g in range(9):
                shift = (104 + 3 * g) % 128
                columns[g, at, :] = pltpu.roll(idx, shift, 1)
            begin = []
            for w in range(3):
                low = jnp.min(idx, axis=0, keepdims=True)
                low = jnp.minimum(low, jnp.minimum(pltpu.roll(low, 127, 1), pltpu.roll(low, 126, 1)))
                low = jnp.where(
                    third == 0,
                    low,
                    jnp.where(third == 1, pltpu.roll(low, 1, 1), pltpu.roll(low, 2, 1)),
                )
                start = jnp.where(low < NROW, jnp.floor(low * 0.0625) * 16.0, FAR)
                idx = jnp.where(idx >= start + WIN, idx, FAR)
                begin.append(jnp.minimum(start, float(NROW)) if w < 2 else start)
            spare = jnp.minimum(spare, begin[2])
            begin = [jnp.broadcast_to(b, (8, 128)) for b in begin]
            row = lax.broadcasted_iota(jnp.int32, (8, 128), 0)
            begin = jnp.where(row == 0, begin[0], jnp.where(row == 1, begin[1], begin[2]))
            starts[pl.ds(pl.multiple_of(j * 8, 8), 8), :] = begin.astype(jnp.int32)
            return spare

        def some(n, spare):
            for u in range(4):
                spare = one(part * 8 + n * 4 + u, spare)
            return spare

        return lax.fori_loop(0, 2, some, spare)

    def choose():
        lane = lax.broadcasted_iota(jnp.int32, (128, 128), 1)
        for t in range(6):
            width = min(128, HB - t * 128)
            names = border[:, t * 128 : t * 128 + width].astype(f32)
            if width < 128:
                names = jnp.concatenate([names, jnp.full((1, 128 - width), FAR, f32)], axis=1)
            names = jnp.broadcast_to(names, (128, 128)).T[:width]
            for c in range(R // 128):
                row = (lane[:width] + c * 128).astype(f32)
                pick[t * 128 : t * 128 + width, c * 128 : (c + 1) * 128] = jnp.where(
                    names == row, 1.0, 0.0
                ).astype(jnp.bfloat16)

        def clear(at, size):
            table[at : at + size, :] = jnp.zeros((size, C), jnp.bfloat16)

        clear(NROW, WIN)

        @pl.when(slab == 0)
        def _():
            for b in (0, 1, 2):
                clear(seg(b), HIGH)

        @pl.when(slab == 31)
        def _():
            for b in (6, 7, 8):
                clear(seg(b), WIN)

        for b in (0, 1, 2):
            clear(seg(b) + HIGH, HB - HIGH)

        for b in (6, 7, 8):
            clear(seg(b) + WIN, HB - WIN)

        for edge, db, missing in ((0, 0, list_left), (3, 2, list_right)):
            @pl.when(x == edge)
            def _():
                blank(missing)

                @pl.when(slab > 0)
                def _():
                    clear(seg(db), HIGH)

                @pl.when(slab < 31)
                def _():
                    clear(seg(6 + db), WIN)

    loads[0].wait()
    sum_z, sum_sq = lax.fori_loop(0, R // block, first_sums, (zero, zero))
    loads[1].wait()
    notes_first()
    extra = jnp.where(up | down, 1, 0)
    pl.semaphore_wait(barrier, 22 + extra)
    when(has_right, lambda: note_to_right().start())
    when(has_left, lambda: note_to_left().start())

    def during_first():
        choose()
        notes_second()

    whole = all_sum(0, stacked(sum_z, sum_sq, live_rows.astype(f32)), during_first)
    amount = whole[:, 2 * C :]
    mean = whole[:, :C] / amount
    var = whole[:, C : 2 * C] / amount - mean * mean
    rstd = lax.rsqrt(var + 1e-05)
    for load in loads[2:5]:
        load.wait()
    gain, shift = gamma[...], beta[...]

    def during_second():
        loads[6].wait()
        for t in range(8):
            feat_t[:, t * 256 : (t + 1) * 256] = feat[t * 256 : (t + 1) * 256, :].T
        loads[5].wait()
        when(has_last, lambda: note_ahead().wait_recv())

    def second_sums(t, sums):
        zhat = (pre[rows_at(t), :].astype(f32) - mean) * rstd
        act = gain * zhat + shift
        sig = jax.nn.sigmoid(act)
        g = cot[rows_at(t), :].astype(f32) * sig * (1.0 + act * (1.0 - sig))
        g = jnp.where(live_at(t), g, 0.0)
        grad[rows_at(t), :] = g
        return sums[0] + fold(g), sums[1] + fold(g * zhat)

    sum_g, sum_gz = lax.fori_loop(0, R // block, second_sums, (zero, zero))
    whole = all_sum(1, stacked(sum_g, sum_gz, 0.0), during_second)
    sums[0] = whole[:, :C]
    sums[1] = whole[:, C : 2 * C]
    scale = gain * rstd
    part_g, part_gz = whole[:, :C] / amount, whole[:, C : 2 * C] / amount

    @pl.loop(0, R // block)
    def _(t):
        zhat = (pre[rows_at(t), :].astype(f32) - mean) * rstd
        dz = scale * (grad[rows_at(t), :] - part_g - zhat * part_gz)
        table[rows_at(t), :] = jnp.where(live_at(t), dz, 0.0).astype(jnp.bfloat16)

    @pl.loop(0, 4)
    def _(t):
        at = pl.multiple_of(t * 176, 16)
        rows = dot(pick[pl.ds(at, 176), :], table[0:R, :], ((1,), (0,)))
        list_own[pl.ds(at, 176), :] = rows.astype(jnp.bfloat16)

    def hop(source, target, n, device):
        return pltpu.make_async_remote_copy(
            src_ref=source,
            dst_ref=target,
            send_sem=halo_sem.at[0, n],
            recv_sem=halo_sem.at[1, n],
            device_id=device,
            device_id_type=MESH,
        )

    lists = (list_left, list_own, list_right)

    def right():
        return hop(list_own, list_left, 3, {"gy": x + 1})

    def left():
        return hop(list_own, list_right, 5, {"gy": x - 1})

    def ahead(db):
        return hop(high.at[db], table.at[pl.ds(seg(db), HIGH), :], db, slab_id(slab + 1))

    def behind(db):
        target = table.at[pl.ds(seg(6 + db), WIN), :]
        return hop(lists[db].at[pl.ds(0, WIN), :], target, 6 + db, slab_id(slab - 1))

    def pass_on(db, mark):
        at = jnp.max(mark[...]) * 16
        high[db] = lists[db][pl.ds(at, HIGH), :]
        when(has_next, lambda: ahead(db).start())
        when(has_last, lambda: behind(db).start())

    when(has_right, lambda: right().start())
    when(has_left, lambda: left().start())
    pass_on(1, note_own)
    table[seg(4) : seg(5), :] = list_own[...]
    spare = plan(0, jnp.full((1, 128), FAR, f32))
    loads[7].wait()
    for db, there, came, mark in (
        (0, has_left, right, note_left),
        (2, has_right, left, note_right),
    ):
        when(there, lambda: came().wait_recv())
        when(there, lambda: pass_on(db, mark))
        table[seg(3 + db) : seg(4 + db), :] = lists[db][...]

    spare = plan(1, spare)
    row = lax.broadcasted_iota(jnp.int32, (8, 128), 0)
    starts[0:8, :] = jnp.where(row == 3, spare.astype(jnp.int32), starts[0:8, :])

    @pl.loop(0, 9)
    def _(g):
        for i in range(3):
            turned[g, i * C : (i + 1) * C, :] = weight[g * 3 + i].T

    for db, there in ((1, True), (0, has_left), (2, has_right)):
        when(has_last & there, lambda: ahead(db).wait_recv())
        when(has_next & there, lambda: behind(db).wait_recv())
    when(has_right, lambda: right().wait_send())
    when(has_left, lambda: left().wait_send())
    for db, there in ((1, True), (0, has_left), (2, has_right)):
        when(has_next & there, lambda: ahead(db).wait_send())
        when(has_last & there, lambda: behind(db).wait_send())
    when(has_right, lambda: note_to_right().wait_send())
    when(has_left, lambda: note_to_left().wait_send())
    when(has_next, lambda: note_ahead().wait_send())
    for copy in pending:
        copy.wait_send()


def front(counts, *arrays):
    vmem = pl.BlockSpec(memory_space=pltpu.VMEM)
    return pl.pallas_call(
        front_kernel,
        out_shape=(
            jax.ShapeDtypeStruct((ROWS, C), jnp.bfloat16),
            jax.ShapeDtypeStruct((9, R, 128), jnp.float32),
            jax.ShapeDtypeStruct((R // SUB * 8, 128), jnp.int32),
            jax.ShapeDtypeStruct((2, 1, C), jnp.float32),
            jax.ShapeDtypeStruct((C, R), jnp.bfloat16),
            jax.ShapeDtypeStruct((9, 3 * C, C), jnp.bfloat16),
        ),
        in_specs=[pl.BlockSpec(memory_space=pltpu.SMEM)]
        + [pl.BlockSpec(memory_space=pltpu.HBM)] * 8,
        out_specs=(vmem,) * 6,
        scratch_shapes=[pltpu.VMEM(a.shape, a.dtype) for a in arrays]
        + [
            pltpu.VMEM((R, C), jnp.float32),
            pltpu.VMEM((HB, R), jnp.bfloat16),
            pltpu.VMEM((2, 8, 1, 3 * C), jnp.float32),
            pltpu.VMEM((2, 16, 1, 3 * C), jnp.float32),
            pltpu.VMEM((HB, C), jnp.bfloat16),
            pltpu.VMEM((HB, C), jnp.bfloat16),
            pltpu.VMEM((HB, C), jnp.bfloat16),
            pltpu.VMEM((3, HIGH, C), jnp.bfloat16),
            *[pltpu.VMEM((8, 128), jnp.int32)] * 5,
            pltpu.SemaphoreType.DMA((8,)),
            pltpu.SemaphoreType.DMA((2, 2, 7)),
            pltpu.SemaphoreType.DMA((2, 2, 15)),
            pltpu.SemaphoreType.DMA((2, 9)),
            pltpu.SemaphoreType.DMA((2, 3)),
        ],
        compiler_params=pltpu.CompilerParams(
            collective_id=0, has_side_effects=True, vmem_limit_bytes=24 * 1024 * 1024
        ),
        cost_estimate=pl.CostEstimate(
            flops=1_000_000_000, bytes_accessed=10_000_000, transcendentals=1_000_000
        ),
        name="front",
    )(counts, *[pltpu.with_memory_space_constraint(a, pltpu.HBM) for a in arrays])


def body(features, pre_norm, out_grad, weight, gamma, beta, neighbors, boundary, counts):
    table, columns, starts, sums, feat_t, turned = front(
        counts,
        pre_norm[0, 0],
        out_grad[0, 0],
        gamma[None],
        beta[None],
        neighbors.reshape(27, 1, R),
        boundary.reshape(1, HB),
        features[0, 0],
        weight,
    )
    in_grad, local_wgrad, gamma_grad, beta_grad = convolve(
        starts, columns, table, feat_t, turned, sums
    )
    weight_grad = scatter_sum(local_wgrad)
    return (in_grad[None, None], weight_grad, gamma_grad[0], beta_grad[0])


def solution(mesh):
    torus = Mesh(mesh.devices.reshape(4, 4, 2, mesh.shape["gy"]), ("gx_0", "gx_1", "gx_2", "gy"))
    return jax.shard_map(
        body,
        mesh=torus,
        in_specs=(
            P(GX, "gy", None, None),
            P(GX, "gy", None, None),
            P(GX, "gy", None, None),
            P(),
            P(),
            P(),
            P(GX, "gy", None, None),
            P(GX, "gy", None),
            P(GX, "gy"),
        ),
        out_specs=(P(GX, "gy", None, None), P(GX_GY, None), P(), P()),
        check_vma=False,
    )
```
